32 devices in a mesh: row: 2 (over core), col: 16 (over z, y, x).
Axes of the slice: x: 2, y: 2, z: 4, core: 2. Of those that a mesh axis runs over, the one named last changes fastest.
Arguments:
- tokens: bfloat16 [2, 16384, 512], P(None, 'col', 'row'), may hold values from -8 to 8
- memory: bfloat16 [2, 16384, 512], P(None, 'col', 'row'), may hold values from -6 to 6
- cotangent: bfloat16 [2, 16384, 512], P(None, 'col', 'row'), may hold values from -6 to 6
- segments: int32 [2, 16384], P(None, 'col'), may hold values from 0 to 1023, as said below
- padding: int32 [2, 16384], P(None, 'col'), may hold values from 0 to 1, as said below
- self_query: bfloat16 [512, 512], P('row', 'col'), may hold values from -0.25 to 0.25
- self_key: bfloat16 [512, 512], P('row', 'col'), may hold values from -0.25 to 0.25
- self_value: bfloat16 [512, 512], P('row', 'col'), may hold values from -0.25 to 0.25
- self_output: bfloat16 [512, 512], P('row', 'col'), may hold values from -0.75 to 0.75
- cross_query: bfloat16 [512, 512], P('row', 'col'), may hold values from -0.25 to 0.25
- cross_key: bfloat16 [512, 512], P('row', 'col'), may hold values from -0.25 to 0.25
- cross_value: bfloat16 [512, 512], P('row', 'col'), may hold values from -0.25 to 0.25
- cross_output: bfloat16 [512, 512], P('row', 'col'), may hold values from -3 to 3
- feed_up: bfloat16 [512, 2048], P('row', 'col'), may hold values from -0.25 to 0.25
- feed_down: bfloat16 [2048, 512], P('row', 'col'), may hold values from -0.125 to 0.125
- norm_gain: float32 [3, 512], P(None, 'row'), may hold values from 0.5 to 1.5
- norm_bias: float32 [3, 512], P(None, 'row'), may hold values from -3 to 3
- omegas: float32 [3, 512], P(None, 'row'), may hold values from 0.5 to 1.5
Outputs:
- layer_out: bfloat16 [2, 16384, 512], P(None, 'col', 'row')
- tokens_grad: float32 [2, 16384, 512], P(None, 'col', 'row')
- memory_grad: float32 [2, 16384, 512], P(None, 'col', 'row')
- self_query_grad: float32 [512, 512], P('row', 'col')
- self_key_grad: float32 [512, 512], P('row', 'col')
- self_value_grad: float32 [512, 512], P('row', 'col')
- self_output_grad: float32 [512, 512], P('row', 'col')
- cross_query_grad: float32 [512, 512], P('row', 'col')
- cross_key_grad: float32 [512, 512], P('row', 'col')
- cross_value_grad: float32 [512, 512], P('row', 'col')
- cross_output_grad: float32 [512, 512], P('row', 'col')
- feed_up_grad: float32 [512, 2048], P('row', 'col')
- feed_down_grad: float32 [2048, 512], P('row', 'col')
- norm_gain_grad: float32 [3, 512], P(None, ('row', 'col'))
- norm_bias_grad: float32 [3, 512], P(None, ('row', 'col'))
- omegas_gradient: float32 [3, 512], P(None, ('row', 'col'))
The draws below stay inside these ranges and needn't reach their ends.
Inputs may be any that keep to these rules, and one draw needn't show every extreme that they name: `segments`: in each sequence of 1024 tokens, a token's number is the position within the sequence of the first token of its document; numbers never fall along a sequence, and the sequence's last token begins a document of its own. `padding`: in each sequence the ones come first and the zeros last; each sequence ends in 1 to 256 zeros.
All inputs are finite; a program needn't handle non-finite values.
Results may differ from the reference program's by a relative error of at most 0.04.
Values may be sent and summed in bfloat16 or wider, within the bound.
A program may use at most 192 MiB of HBM per device.

```python
import jax
import jax.numpy as jnp
from jax import lax

D = 512
HEADS = 8
HD = 64
FF = 2048
LEN = 1024
MEM = 1024
MICRO = 2
TOKENS = 16384
N_COL = 16


def draw_tokens(key, part):
    key = jax.random.fold_in(key, 37)
    noise_key, size_key, sign_key = jax.random.split(key, 3)
    offsets = jax.random.uniform(size_key, (MICRO, TOKENS, 1), jnp.float32, 0.5, 1.5)
    signs = jnp.where(jax.random.randint(sign_key, (MICRO, TOKENS, 1), 0, 2) == 1, 1.0, -1.0)
    place = jnp.arange(D, dtype=jnp.float32)[None, None, :] / (D - 1)
    noise = jnp.clip(jax.random.normal(noise_key, (MICRO, TOKENS, D), jnp.float32), -5.0, 5.0)
    profile = 0.5 + 1.5 * place
    return (noise + signs * offsets * profile).astype(jnp.bfloat16)


def draw_segments(key, part):
    sequences = MICRO * TOKENS // LEN
    base = jax.random.fold_in(key, 11)
    pick_key, mark_key = jax.random.split(base)
    levels = jax.random.randint(pick_key, (sequences, 1), 0, 4)
    spacing = jnp.left_shift(jnp.int32(8), 2 * levels)
    marks = jax.random.randint(mark_key, (sequences, LEN), 0, 1 << 30) % spacing
    positions = jnp.arange(LEN, dtype=jnp.int32)[None, :]
    starts = (marks == 0) | (positions == 0) | (positions == LEN - 1)
    firsts = lax.cummax(jnp.where(starts, positions, 0), axis=1)
    return firsts.reshape(MICRO, TOKENS).astype(jnp.int32)


def draw_padding(key, part):
    sequences = MICRO * TOKENS // LEN
    base = jax.random.fold_in(key, 23)
    tails = jax.random.randint(base, (sequences, 1), 1, LEN // 4 + 1)
    positions = jnp.arange(LEN, dtype=jnp.int32)[None, :]
    return (positions < LEN - tails).astype(jnp.int32).reshape(MICRO, TOKENS)


def strengthened(entries, rng, source, target, shards_of, factor):
    def block_of(axis_at):
        return (jnp.arange(entries.shape[axis_at]) // (entries.shape[axis_at] // shards_of)).reshape((-1,) + (1,) * (entries.ndim - 1 - axis_at))

    near = jax.random.permutation(rng, shards_of)[block_of(target)]
    second = (block_of(target) + shards_of // 2) % shards_of
    return jnp.where((block_of(source) == near) | (block_of(source) == second), factor * entries, entries)


def block_levels(own_key, dims, pieces, low, top_value):
    level = 1.0
    for position, parts in pieces:
        draws = jax.random.uniform(jax.random.fold_in(jax.random.fold_in(own_key, 6), position), (parts,), jnp.float32, low / len(pieces), top_value / len(pieces))
        level = level * jnp.repeat(jnp.exp(draws), dims[position] // parts).reshape((-1,) + (1,) * (len(dims) - 1 - position))
    return level


def gaussian(stream_key, shape, width, most, shards=(), kind=jnp.bfloat16):
    loudness = block_levels(stream_key, shape, shards, -0.22, 0.18) if shards else 1.0
    entries = jax.random.normal(stream_key, shape, jnp.float32) * width * loudness
    return jnp.minimum(jnp.maximum(entries, -most), most).astype(kind)


def gaussian_with(own_key, shape, spread, limit, cuts, heavy, kind=jnp.bfloat16):
    entries = spread * jax.random.normal(own_key, shape, jnp.float32)
    if cuts:
        entries = entries * block_levels(own_key, shape, cuts, -0.22, 0.18)
    return jnp.clip(strengthened(entries, jax.random.fold_in(own_key, 3), *heavy), -limit, limit).astype(kind)


def setup_inputs(seed: int = 0) -> dict:
    key_list = jax.random.split(jax.random.key(seed), 19)
    tokens = draw_tokens(jax.random.fold_in(key_list[18], 71), 0)
    memory = gaussian(key_list[1], (MICRO, MEM * N_COL, D), 1.0, 6.0, ((1, 16), (2, 2)))
    cotangent = gaussian_with(key_list[2], (MICRO, TOKENS, D), 1.0, 6.0, ((1, 16), (2, 2)), (1, 2, 16, 2.0))
    segments = draw_segments(jax.random.fold_in(key_list[18], 71), 0)
    padding = draw_padding(jax.random.fold_in(key_list[18], 71), 0)
    self_query = gaussian(key_list[5], (D, D), D ** -0.5, 0.25, ((0, 2), (1, 16)))
    self_key = gaussian(key_list[6], (D, D), D ** -0.5, 0.25, ((0, 2), (1, 16)))
    self_value = gaussian(key_list[7], (D, D), D ** -0.5, 0.25, ((0, 2), (1, 16)))
    self_output = gaussian(key_list[8], (D, D), (D // 8) ** -0.5, 0.75, ((0, 2), (1, 16)))
    cross_query = gaussian(key_list[9], (D, D), D ** -0.5, 0.25, ((0, 2), (1, 16)))
    cross_key = gaussian(key_list[10], (D, D), D ** -0.5, 0.25, ((0, 2), (1, 16)))
    cross_value = gaussian(key_list[11], (D, D), D ** -0.5, 0.25, ((0, 2), (1, 16)))
    cross_output = gaussian(key_list[12], (D, D), (D * 8 // MEM) ** -0.5, 3.0, ((0, 2), (1, 16)))
    feed_up = gaussian(key_list[13], (D, FF), D ** -0.5, 0.25, ((0, 2), (1, 16)))
    feed_down = gaussian(key_list[14], (FF, D), FF ** -0.5, 0.125, ((0, 2), (1, 16)))
    norm_gain = jnp.clip(1.0 + 0.1 * jax.random.normal(key_list[15], (3, D), jnp.float32), 0.5, 1.5)
    norm_bias = gaussian(key_list[16], (3, D), 0.3, 3.0, ((1, 2),), jnp.float32)
    omegas = jnp.clip(0.5 + 1.0 * jax.random.uniform(key_list[17], (3, D), jnp.float32) ** block_levels(key_list[17], (3, D), ((1, 2),), -0.2, 0.2), 0.5, 1.5)
    return {"tokens": tokens, "memory": memory, "cotangent": cotangent, "segments": segments, "padding": padding, "self_query": self_query, "self_key": self_key, "self_value": self_value, "self_output": self_output, "cross_query": cross_query, "cross_key": cross_key, "cross_value": cross_value, "cross_output": cross_output, "feed_up": feed_up, "feed_down": feed_down, "norm_gain": norm_gain, "norm_bias": norm_bias, "omegas": omegas}


EPSILON = 1e-05
MASKED = -1e+30
HIGHEST = lax.Precision.HIGHEST

@jax.custom_vjp
def low(v):
    return lax.optimization_barrier(v.astype(jnp.bfloat16)).astype(jnp.float32)

@jax.custom_vjp
def low_back(v):
    return v

def low_keep(v):
    return (low(v), None)

def low_pass(kept, grad):
    return (grad,)

def back_keep(v):
    return (v, None)

def back_low(kept, grad):
    return (low(grad),)
low.defvjp(low_keep, low_pass)
low_back.defvjp(back_keep, back_low)

def product(left_side, right_side):
    return jnp.matmul(left_side, right_side, precision=HIGHEST)

def layer_norm(resid, gain_row, bias_row):
    average = lax.optimization_barrier(jnp.mean(resid, axis=-1, keepdims=True))
    centred = resid - average
    variance = lax.optimization_barrier(jnp.mean(centred * centred, axis=-1, keepdims=True))
    return centred * lax.rsqrt(variance + EPSILON) * gain_row + bias_row

def attend(query_rows, keys_in, values_in, allowed):
    groups, length, _ = query_rows.shape
    key_rows = keys_in.shape[1]
    query_heads = query_rows.reshape(groups, length, HEADS, HD)
    key_heads = keys_in.reshape(groups, key_rows, HEADS, HD)
    value_heads = values_in.reshape(groups, key_rows, HEADS, HD)
    scores = jnp.einsum('gqhe,gkhe->ghqk', query_heads, key_heads, precision=HIGHEST) * HD ** (-0.5)
    scores = low_back(scores)
    if allowed is not None:
        scores = jnp.where(allowed[:, None], scores, MASKED)
    highest = lax.optimization_barrier(jnp.max(scores, axis=-1, keepdims=True))
    raised = jnp.exp(scores - highest)
    weighting = low(raised / lax.optimization_barrier(jnp.sum(raised, axis=-1, keepdims=True)))
    context = jnp.einsum('ghqk,gkhe->gqhe', weighting, value_heads, precision=HIGHEST)
    context = context.reshape(groups, length, HEADS * HD)
    return low(low_back(context))

def decoder(tokens_in, memory_in, allowed, params):
    self_query, self_key, self_value, self_output, cross_query, cross_key, cross_value, cross_output, feed_up, feed_down, norm_gain, norm_bias, omegas = params
    query_rows = low(low_back(product(tokens_in, self_query)))
    keys_self = low(low_back(product(tokens_in, self_key)))
    values_self = low(low_back(product(tokens_in, self_value)))
    context = attend(query_rows, keys_self, values_self, allowed)
    attn_out = low_back(product(context, self_output))
    first_norm = layer_norm(omegas[0] * tokens_in + attn_out, norm_gain[0], norm_bias[0])
    first_low = low(first_norm)
    probes = low(low_back(product(first_low, cross_query)))
    anchors = low(low_back(product(memory_in, cross_key)))
    payload = low(low_back(product(memory_in, cross_value)))
    cross_context = attend(probes, anchors, payload, None)
    cross_result = low_back(product(cross_context, cross_output))
    second_norm = layer_norm(omegas[1] * first_norm + cross_result, norm_gain[1], norm_bias[1])
    second_low = low(second_norm)
    hidden_pre = low_back(product(second_low, feed_up))
    hidden = low(jax.nn.gelu(hidden_pre, approximate=True))
    feed_result = low_back(product(hidden, feed_down))
    return layer_norm(omegas[2] * second_norm + feed_result, norm_gain[2], norm_bias[2])

def reference(tokens, memory, cotangent, segments, padding, self_query, self_key, self_value, self_output, cross_query, cross_key, cross_value, cross_output, feed_up, feed_down, norm_gain, norm_bias, omegas):
    sequences = MICRO * N_COL
    per_round = 2 if sequences % 2 == 0 else 1
    rounds = sequences // per_round
    token_groups = tokens.astype(jnp.float32).reshape(rounds, per_round, LEN, D)
    memory_groups = memory.astype(jnp.float32).reshape(rounds, per_round, MEM, D)
    cotangent_groups = cotangent.astype(jnp.float32).reshape(rounds, per_round, LEN, D)
    segment_groups = segments.reshape(rounds, per_round, LEN)
    padding_groups = padding.reshape(rounds, per_round, LEN)
    matrices = (self_query, self_key, self_value, self_output, cross_query, cross_key, cross_value, cross_output, feed_up, feed_down)
    params = tuple((matrix.astype(jnp.float32) for matrix in matrices)) + (norm_gain.astype(jnp.float32), norm_bias.astype(jnp.float32), omegas.astype(jnp.float32))
    positions = jnp.arange(LEN, dtype=jnp.int32)

    def one_round(summed, inputs):
        token_in, memory_in, cotangent_in, segment_in, padding_in = inputs
        same_doc = segment_in[:, :, None] == segment_in[:, None, :]
        causal = positions[None, :, None] >= positions[None, None, :]
        live_key = padding_in[:, None, :] == 1
        diagonal = positions[None, :, None] == positions[None, None, :]
        allowed = same_doc & causal & live_key | diagonal

        def forward(token_arg, memory_arg, param_arg):
            return decoder(token_arg, memory_arg, allowed, param_arg)
        result, pullback = jax.vjp(forward, token_in, memory_in, params)
        token_grad, memory_grad, param_grad = pullback(cotangent_in.astype(result.dtype))
        summed = jax.tree.map(lambda running, addend: running + addend.astype(running.dtype), summed, param_grad)
        return (summed, (result.astype(jnp.bfloat16), token_grad, memory_grad))
    zeros = jax.tree.map(lambda template: jnp.zeros_like(template), params)
    summed, (results, token_grads, memory_grads) = lax.scan(one_round, zeros, (token_groups, memory_groups, cotangent_groups, segment_groups, padding_groups))
    return (results.reshape(MICRO, TOKENS, D), token_grads.reshape(MICRO, TOKENS, D), memory_grads.reshape(MICRO, N_COL * MEM, D), summed[0], summed[1], summed[2], summed[3], summed[4], summed[5], summed[6], summed[7], summed[8], summed[9], summed[10], summed[11], summed[12])
```

```python
import jax
import jax.numpy as jnp
from jax import lax
from jax.experimental import pallas as pl
from jax.experimental.pallas import tpu as pltpu
from jax.sharding import PartitionSpec as P

F32 = jnp.float32
BF16 = jnp.bfloat16
EPSILON = 1e-05
MASKED = -1e30
T = 1024
D = 512
H = 8
HD = 64
TB = 256


def dot(left, right, left_dim, right_dim):
    return lax.dot_general(
        left, right, (((left_dim,), (right_dim,)), ((), ())), preferred_element_type=F32
    )


def gelu_both(v):
    root = 0.7978845608028654
    square = v * v
    t = jnp.tanh(root * v * (1.0 + 0.044715 * square))
    half = 0.5 * (1.0 + t)
    slope = half + (0.5 * root) * v * (1.0 - t * t) * (1.0 + (3.0 * 0.044715) * square)
    return v * half, slope


def compute(
    x_hbm, mem_hbm, cot_hbm, w_hbm, par, seg, pad,
    lo_hbm, tg_hbm, mg_hbm, g_hbm, e_hbm,
    xs, cs, xt, mt, w8, wup, wdn, qkv, pay, ctx, cctx, inv, xh0, xh1, rstd,
    flow, slow, tlow, ring, es, sg, gs, pcol, cols, gcol, acc, gsta, gstb,
    sem, esem, asem, bsem,
):
    def weight(r, m):
        return w8[r, :, m * 32:(m + 1) * 32, :].reshape(D, 256)

    def forward(m, source):
        return dot(weight(0, m), source[0:256], 1, 0) + dot(weight(1, m), source[256:512], 1, 0)

    def param(k):
        return pcol[:, k:k + 1]

    def add_col(k, value):
        cols[k] = cols[k] + (value[:, 0:128] + value[:, 128:256])

    loads = [
        pltpu.make_async_copy(x_hbm, xs.at[0], sem.at[0]),
        pltpu.make_async_copy(mem_hbm, xs.at[1], sem.at[1]),
        pltpu.make_async_copy(cot_hbm, cs, sem.at[2]),
        pltpu.make_async_copy(w_hbm.at[:, :, pl.ds(0, 256), :], w8, sem.at[3]),
        pltpu.make_async_copy(w_hbm.at[:, :, pl.ds(256, 128), :], wup, sem.at[4]),
        pltpu.make_async_copy(w_hbm.at[:, :, pl.ds(384, 128), :], wdn, sem.at[5]),
    ]
    for copy in loads:
        copy.start()
    pcol[...] = jnp.concatenate([par[...].T, jnp.zeros((D, 112), F32)], axis=1)
    cols[...] = jnp.zeros_like(cols)

    padlen = jnp.sum(pad[...], axis=1, keepdims=True)

    @pl.loop(0, 4)
    def _(j):
        at = pl.multiple_of(j * 256, 256)
        low = seg[:, pl.ds(at, 256)]
        here = at + lax.broadcasted_iota(jnp.int32, (1, 256), 1)
        high = jnp.minimum(here, padlen - 1)
        rows = lax.broadcasted_iota(jnp.int32, (T, 256), 0)
        fits = ((rows >= low) & (rows <= high)) | (rows == here)
        ring[0, :, pl.ds(at, 256)] = jnp.where(fits, 0.0, MASKED).astype(BF16)

    loads[0].wait()
    for r in range(2):
        xt[256 * r:256 * r + 256] = xs[0, r].T
    loads[1].wait()
    for r in range(2):
        mt[256 * r:256 * r + 256] = xs[1, r].T
    loads[3].wait()

    for m in range(3):
        out = forward(m, xt)
        if m == 0:
            out = out * 0.125
        qkv[m] = out.astype(BF16).reshape(H, HD, T)
    for m in (5, 6):
        pay[m - 4] = forward(m, mt).astype(BF16).reshape(H, HD, T)

    ones = jnp.ones((16, T), BF16)

    def attend(q, k, v, q_at, width, keys, masked):
        s = dot(k[:, 0:keys], q[:, q_at:q_at + width], 0, 0)
        if masked:
            s = s + ring[0, 0:keys, q_at:q_at + width].astype(F32)
        top = jnp.max(s, axis=0, keepdims=True)
        e = jnp.exp(s - top).astype(BF16)
        both = dot(v[:, 0:keys], e, 1, 0)
        inverse = 1.0 / both[HD:HD + 1]
        return e, both[0:HD] * inverse, inverse

    def self_tile(i, j):
        if j == 3:
            return 0, 256 * i
        if j == 1:
            return 512 * i, 1024
        return (0 if j == 0 else 256), 512 + 256 * i

    @pl.loop(0, 4)
    def _(pair):
        for i in range(2):
            h = pair * 2 + i
            v = jnp.concatenate([qkv[2, h], ones], axis=0)
            for j in range(4):
                keys = 256 * (j + 1)
                at = slice(256 * j, 256 * j + 256)
                e, out, inverse = attend(qkv[0, h], qkv[1, h], v, 256 * j, 256, keys, True)
                row, lane = self_tile(i, j)
                es[pair, row:row + keys, lane:lane + 256] = e
                ctx[h, :, at] = out.astype(BF16)
                inv[0, h, :, at] = inverse

    def norm(total):
        average = jnp.mean(total, axis=0, keepdims=True)
        centred = total - average
        factor = lax.rsqrt(jnp.mean(centred * centred, axis=0, keepdims=True) + EPSILON)
        return centred * factor, factor

    @pl.loop(0, 4)
    def _(tb):
        at = pl.ds(pl.multiple_of(tb * TB, TB), TB)
        out = forward(3, ctx[:, :, at].reshape(D, TB))
        normed, factor = norm(param(6) * xt[:, at].astype(F32) + out)
        xh0[:, at] = normed
        rstd[0, :, at] = factor
        flow[:, at] = (normed * param(0) + param(3)).astype(BF16)

    pay[0] = (forward(4, flow) * 0.125).astype(BF16).reshape(H, HD, T)

    def e_out(h, slot):
        return pltpu.make_async_copy(ring.at[slot], e_hbm.at[h], esem.at[slot])

    def e_in(h, slot):
        return pltpu.make_async_copy(e_hbm.at[h], ring.at[slot], esem.at[slot])

    @pl.loop(0, 2)
    def _(four):
        for slot in range(4):
            h = four * 4 + slot

            @pl.when(four > 0)
            def _():
                e_out(slot, slot).wait()

            v = jnp.concatenate([pay[2, h], ones], axis=0)
            for j in range(2):
                at = slice(512 * j, 512 * j + 512)
                e, out, inverse = attend(pay[0, h], pay[1, h], v, 512 * j, 512, T, False)
                ring[slot, :, at] = e
                cctx[h, :, at] = out.astype(BF16)
                inv[1, h, :, at] = inverse
            e_out(h, slot).start()

    @pl.loop(0, 4)
    def _(tb):
        at = pl.ds(pl.multiple_of(tb * TB, TB), TB)
        out = forward(7, cctx[:, :, at].reshape(D, TB))
        first = xh0[:, at] * param(0) + param(3)
        normed, factor = norm(param(7) * first + out)
        xh1[:, at] = normed
        rstd[1, :, at] = factor
        slow[:, at] = (normed * param(1) + param(4)).astype(BF16)

    for slot in range(4):
        e_out(4 + slot, slot).wait()
    loads[4].wait()
    loads[5].wait()
    loads[2].wait()

    def up(r, b):
        return wup[r, 4 * b:4 * b + 4].reshape(512, 256)

    def down(b):
        return wdn[b // 4, :, 32 * (b % 4):32 * (b % 4) + 32, :].reshape(D, 256)

    for b in range(4):
        place = slice(512 * (b % 2), 512 * (b % 2) + 512)
        for t in range(2):
            at = slice(512 * t, 512 * t + 512)
            v = dot(up(0, b), slow[0:256, at], 1, 0) + dot(up(1, b), slow[256:512, at], 1, 0)
            value, slope = gelu_both(v)
            ring[b // 2, place, at] = value.astype(BF16)
            ring[2 + b // 2, place, at] = slope.astype(BF16)

    def norm_back(upstream, normed, factor, k):
        scaled = upstream * param(k)
        one = jnp.mean(scaled, axis=0, keepdims=True)
        two = jnp.mean(scaled * normed, axis=0, keepdims=True)
        add_col(k, upstream * normed)
        add_col(3 + k, upstream)
        return factor * (scaled - one - normed * two)

    @pl.loop(0, 4)
    def _(tb):
        at = pl.ds(pl.multiple_of(tb * TB, TB), TB)
        out = None
        for b in range(8):
            part = dot(down(b), ring[b // 4, 256 * (b % 4):256 * (b % 4) + 256, at], 1, 0)
            out = part if out is None else out + part
        second = xh1[:, at] * param(1) + param(4)
        normed, factor = norm(param(8) * second + out)
        final = (normed * param(2) + param(5)).astype(BF16)
        upstream = jnp.concatenate([cs[0, at, :].T, cs[1, at, :].T], axis=0).astype(F32)
        for r in range(2):
            xs[0, r, at, :] = final[256 * r:256 * r + 256].T
        third = norm_back(upstream, normed, factor, 2)
        add_col(8, third * second)
        sg[:, at] = param(8) * third
        tlow[:, at] = third.astype(BF16)

    lo_out = pltpu.make_async_copy(xs.at[0], lo_hbm, sem.at[0])
    lo_out.start()

    pending = {}

    def send(key, source, target, which):
        pending[key] = pltpu.make_async_copy(source, target, which)
        pending[key].start()

    def settle(key):
        if key in pending:
            pending.pop(key).wait()

    turn = [0]

    def rows_out(r, row, value):
        slot = turn[0] % 4
        turn[0] += 1
        settle(("a", slot))
        gsta[slot] = value.astype(BF16).reshape(16, 32, 256)
        send(("a", slot), gsta.at[slot], g_hbm.at[r, :, pl.ds(row, 32), :], asem.at[slot])

    def square_grad(m, left, right):
        for r in range(2):
            rows_out(r, 32 * m, dot(left, right[256 * r:256 * r + 256], 1, 1))

    for f in range(8):
        rows = slice(256 * (f % 4), 256 * (f % 4) + 256)
        rows_out(f // 4, 384 + 32 * (f % 4), dot(tlow[...], ring[f // 4, rows, :], 1, 1))
        grad = dot(down(f), tlow[...], 0, 0) * ring[2 + f // 4, rows, :].astype(F32)
        ring[2 + f // 4, rows, :] = grad.astype(BF16)
    for b in range(4):
        grad = ring[2 + b // 2, 512 * (b % 2):512 * (b % 2) + 512, :]
        for r in range(2):
            settle(("b", r))
            part = dot(grad, slow[256 * r:256 * r + 256], 1, 1)
            gstb[r] = part.astype(BF16).reshape(4, 128, 256)
            send(
                ("b", r), gstb.at[r], g_hbm.at[r, pl.ds(4 * b, 4), pl.ds(256, 128), :], bsem.at[r]
            )
    for r in range(2):
        half = slice(256 * r, 256 * r + 256)
        for t in range(2):
            at = slice(512 * t, 512 * t + 512)
            part = None
            for b in range(4):
                place = slice(512 * (b % 2), 512 * (b % 2) + 512)
                one = dot(up(r, b), ring[2 + b // 2, place, at], 0, 0)
                part = one if part is None else part + one
            sg[half, at] = sg[half, at] + part

    for slot in range(4):
        e_in(slot, slot).start()

    @pl.loop(0, 4)
    def _(tb):
        at = pl.ds(pl.multiple_of(tb * TB, TB), TB)
        middle = norm_back(sg[:, at], xh1[:, at], rstd[1, :, at], 1)
        add_col(7, middle * (xh0[:, at] * param(0) + param(3)))
        sg[:, at] = param(7) * middle
        tlow[:, at] = middle.astype(BF16)

    square_grad(7, tlow[...], cctx[...].reshape(D, T))
    for r in range(2):
        slow[256 * r:256 * r + 256] = dot(weight(r, 7), tlow[...], 0, 0).astype(BF16)

    def scaled_grad(context, which, h):
        rows = pl.ds(pl.multiple_of(h * HD, HD), HD)
        g = (slow[rows, :].astype(F32) * inv[which, h]).astype(BF16)
        delta = jnp.sum(g.astype(F32) * context[h].astype(F32), axis=0, keepdims=True)
        return g, delta

    @pl.loop(0, 2)
    def _(four):
        for slot in range(4):
            h = four * 4 + slot
            e_in(h, slot).wait()
            g, delta = scaled_grad(cctx, 1, h)
            q, k, v = pay[0, h], pay[1, h], pay[2, h]
            dp = dot(v, g, 0, 0)
            e = ring[slot]
            ds = e * (dp - delta).astype(BF16)
            pay[0, h] = (dot(k, ds, 1, 0) * 0.125).astype(BF16)
            pay[1, h] = dot(q, ds, 1, 1).astype(BF16)
            pay[2, h] = dot(g, e, 1, 1).astype(BF16)

            @pl.when(four == 0)
            def _():
                e_in(h + 4, slot).start()

    grads = [pay[i].reshape(D, T) for i in range(3)]
    square_grad(4, grads[0], flow)
    square_grad(5, grads[1], mt)
    square_grad(6, grads[2], mt)
    for r in range(2):
        out = dot(weight(r, 5), grads[1], 0, 0) + dot(weight(r, 6), grads[2], 0, 0)
        gs[r] = out.T
    mg_out = pltpu.make_async_copy(gs, mg_hbm, sem.at[1])
    mg_out.start()
    for r in range(2):
        half = slice(256 * r, 256 * r + 256)
        sg[half] = sg[half] + dot(weight(r, 4), grads[0], 0, 0)

    @pl.loop(0, 4)
    def _(tb):
        at = pl.ds(pl.multiple_of(tb * TB, TB), TB)
        inner = norm_back(sg[:, at], xh0[:, at], rstd[0, :, at], 0)
        add_col(6, inner * xt[:, at].astype(F32))
        sg[:, at] = param(6) * inner
        tlow[:, at] = inner.astype(BF16)

    for k in range(9):
        gcol[:, k:k + 1] = jnp.sum(cols[k], axis=1, keepdims=True)

    square_grad(3, tlow[...], ctx[...].reshape(D, T))
    for r in range(2):
        slow[256 * r:256 * r + 256] = dot(weight(r, 3), tlow[...], 0, 0).astype(BF16)

    @pl.loop(0, 4)
    def _(pair):
        for i in range(2):
            h = pair * 2 + i
            g, delta = scaled_grad(ctx, 0, h)
            q, k, v = qkv[0, h], qkv[1, h], qkv[2, h]
            for j in (3, 2, 1, 0):
                keys = 256 * (j + 1)
                at = slice(256 * j, 256 * j + 256)
                row, lane = self_tile(i, j)
                e = es[pair, row:row + keys, lane:lane + 256]
                dp = dot(v[:, 0:keys], g[:, at], 0, 0)
                ds = e * (dp - delta[:, at]).astype(BF16)
                qkv[0, h, :, at] = (dot(k[:, 0:keys], ds, 1, 0) * 0.125).astype(BF16)
                new_k = dot(q[:, at], ds, 1, 1)
                new_v = dot(g[:, at], e, 1, 1)
                if j == 3:
                    acc[i, 0] = new_k
                    acc[i, 1] = new_v
                else:
                    acc[i, 0, :, 0:keys] = acc[i, 0, :, 0:keys] + new_k
                    acc[i, 1, :, 0:keys] = acc[i, 1, :, 0:keys] + new_v
            qkv[1, h] = acc[i, 0].astype(BF16)
            qkv[2, h] = acc[i, 1].astype(BF16)

    grads = [qkv[i].reshape(D, T) for i in range(3)]
    for m in range(3):
        square_grad(m, grads[m], xt)
    mg_out.wait()
    for r in range(2):
        out = sg[256 * r:256 * r + 256]
        for m in range(3):
            out = out + dot(weight(r, m), grads[m], 0, 0)
        gs[r] = out.T
    tg_out = pltpu.make_async_copy(gs, tg_hbm, sem.at[1])
    tg_out.start()
    tg_out.wait()
    lo_out.wait()
    for key in list(pending):
        settle(key)


def run_compute(x, mem, cot, w, par, seg, pad):
    anywhere = pl.BlockSpec(memory_space=pl.ANY)
    vmem = pl.BlockSpec(memory_space=pltpu.VMEM)
    V = pltpu.VMEM
    scratch = [
        V((2, 2, T, 256), BF16), V((2, T, 256), BF16),
        V((D, T), BF16), V((D, T), BF16),
        V((2, 16, 256, 256), BF16), V((2, 16, 128, 256), BF16), V((2, 16, 128, 256), BF16),
        V((3, H, HD, T), BF16), V((3, H, HD, T), BF16),
        V((H, HD, T), BF16), V((H, HD, T), BF16),
        V((2, H, 1, T), F32),
        V((D, T), F32), V((D, T), F32), V((2, 1, T), F32),
        V((D, T), BF16), V((D, T), BF16), V((D, T), BF16),
        V((4, T, T), BF16), V((4, T, 1280), BF16),
        V((D, T), F32), V((2, T, 256), F32),
        V((D, 128), F32), V((9, D, 128), F32),
        V((2, 2, HD, T), F32),
        V((4, 16, 32, 256), BF16), V((2, 4, 128, 256), BF16),
        pltpu.SemaphoreType.DMA((6,)), pltpu.SemaphoreType.DMA((4,)),
        pltpu.SemaphoreType.DMA((4,)), pltpu.SemaphoreType.DMA((2,)),
    ]
    shape = jax.ShapeDtypeStruct
    return pl.pallas_call(
        lambda *refs: compute(*refs[:12], *refs[13:37], refs[12], *refs[37:]),
        in_specs=[anywhere] * 4 + [vmem] * 3,
        out_specs=[anywhere] * 5 + [vmem],
        out_shape=[
            shape((2, T, 256), BF16), shape((2, T, 256), F32), shape((2, T, 256), F32),
            shape((2, 16, 512, 256), BF16), shape((H, T, T), BF16), shape((D, 128), F32),
        ],
        scratch_shapes=scratch,
        compiler_params=pltpu.CompilerParams(vmem_limit_bytes=63 * 2**20),
        name="layer",
    )(x, mem, cot, w, par, seg, pad)


CHIPS = 16


def to_sixteen(w):
    n = w.shape[1]
    if n == CHIPS:
        return w
    part = D // n

    def spread(block):
        block = block.reshape(2, n, -1, part, 256).swapaxes(1, 2).reshape(2, -1, CHIPS, 32, 256)
        return block.swapaxes(1, 2).reshape(2, CHIPS, -1, 256)

    return jnp.concatenate(
        [
            spread(w[:, :, :8 * part]),
            w[:, :, 8 * part:12 * part].reshape(2, CHIPS, 128, 256),
            spread(w[:, :, 12 * part:]),
        ],
        axis=2,
    )


def from_sixteen(g, n):
    if n == CHIPS:
        return g
    part = D // n

    def gather(block):
        block = block.reshape(2, CHIPS, -1, 32, 256).swapaxes(1, 2).reshape(2, -1, n, part, 256)
        return block.swapaxes(1, 2).reshape(2, n, -1, 256)

    return jnp.concatenate(
        [
            gather(g[:, :, :256]),
            g[:, :, 256:384].reshape(2, n, 4 * part, 256),
            gather(g[:, :, 384:]),
        ],
        axis=2,
    )


def body(
    tokens, memory, cotangent, segments, padding,
    self_query, self_key, self_value, self_output,
    cross_query, cross_key, cross_value, cross_output,
    feed_up, feed_down, norm_gain, norm_bias, omegas,
):
    row = lax.axis_index("row")
    n = lax.axis_size("col")
    part = D // n
    squares = (
        self_query, self_key, self_value, self_output,
        cross_query, cross_key, cross_value, cross_output,
    )
    blob = jnp.concatenate(
        [m.T for m in squares]
        + [feed_up.T]
        + [feed_down.T[:, 256 * s:256 * s + 256] for s in range(4)],
        axis=0,
    )
    w = lax.all_gather(blob, ("row", "col"), axis=0, tiled=False).reshape(2, n, 16 * part, 256)
    w = to_sixteen(w)
    par = jnp.concatenate([norm_gain, norm_bias, omegas], axis=0)
    par = lax.all_gather(par, "row", axis=1, tiled=True)
    par = jnp.concatenate([par, jnp.zeros((7, D), F32)], axis=0)

    def mine(array):
        return lax.all_to_all(array, "row", split_axis=0, concat_axis=0, tiled=True)

    seg = lax.dynamic_slice_in_dim(segments, row, 1, 0)
    pad = lax.dynamic_slice_in_dim(padding, row, 1, 0)
    lo, tg, mg, g, _, gcol = run_compute(mine(tokens), mine(memory), mine(cotangent), w, par, seg, pad)
    lo, tg, mg = mine(lo), mine(tg), mine(mg)
    g = from_sixteen(g, n).reshape(2 * n, 16 * part, 256)
    g = lax.psum_scatter(g, ("row", "col"), scatter_dimension=0, tiled=False)
    gcol = lax.psum_scatter(
        gcol.reshape(2 * n, part // 2, 128), ("row", "col"), scatter_dimension=0, tiled=False
    )
    g = g.astype(F32)
    small = gcol[:, 0:9].T
    last = 12 * part
    return (
        lo, tg, mg,
        *[g[part * m:part * m + part].T for m in range(8)],
        g[8 * part:last].T,
        jnp.concatenate([g[last + part * s:last + part * s + part].T for s in range(4)], axis=0),
        small[0:3], small[3:6], small[6:9],
    )


def solution(mesh):
    wide = P(None, "col", "row")
    square = P("row", "col")
    return jax.shard_map(
        body,
        mesh=mesh,
        in_specs=(wide,) * 3 + (P(None, "col"),) * 2 + (square,) * 10 + (P(None, "row"),) * 3,
        out_specs=(wide,) * 3 + (square,) * 10 + (P(None, ("row", "col")),) * 3,
        check_vma=False,
    )
```

```python
import jax
import jax.numpy as jnp
from jax import lax
from jax.experimental import pallas as pl
from jax.experimental.pallas import tpu as pltpu
from jax.sharding import PartitionSpec as P

F32 = jnp.float32
BF16 = jnp.bfloat16
EPSILON = 1e-05
MASKED = -1e30
T = 1024
D = 512
H = 8
HD = 64
TB = 256


def dot(left, right, left_dim, right_dim):
    return lax.dot_general(
        left, right, (((left_dim,), (right_dim,)), ((), ())), preferred_element_type=F32
    )


def gelu_both(v):
    root = 0.7978845608028654
    square = v * v
    t = jnp.tanh(root * v * (1.0 + 0.044715 * square))
    half = 0.5 * (1.0 + t)
    slope = half + (0.5 * root) * v * (1.0 - t * t) * (1.0 + (3.0 * 0.044715) * square)
    return v * half, slope


def layer(
    link, e_hbm, es_hbm, par, seg, pad,
    xs, cs, xt, mt, w8, wup, wdn, qkv, pay, ctx, cctx, inv, xh0, xh1, rstd,
    flow, slow, tlow, ring, sg, gs, pcol, cols, acc, gcol, esem,
):
    def weight(r, m):
        return w8[r, :, :, :, m * 32:(m + 1) * 32, :].reshape(D, 256)

    def forward(m, source):
        return dot(weight(0, m), source[0:256], 1, 0) + dot(weight(1, m), source[256:512], 1, 0)

    def param(k):
        return pcol[:, k:k + 1]

    def add_col(k, value):
        cols[k] = cols[k] + (value[:, 0:128] + value[:, 128:256])

    link.begin()
    cols[...] = jnp.zeros_like(cols)
    link.wait_input(0)
    for r in range(2):
        xt[256 * r:256 * r + 256] = xs[0, r].T
    link.wait_input(1)
    for r in range(2):
        mt[256 * r:256 * r + 256] = xs[1, r].T
    pcol[...] = jnp.zeros_like(pcol)
    for r in range(2):
        pcol[256 * r:256 * r + 256, 0:16] = par[r].T

    padlen = jnp.sum(link.line(pad), axis=1, keepdims=True)
    for j in range(4):
        low = link.line(seg)[:, 256 * j:256 * j + 256]
        here = 256 * j + lax.broadcasted_iota(jnp.int32, (1, 256), 1)
        high = jnp.minimum(here, padlen - 1)
        rows = lax.broadcasted_iota(jnp.int32, (T, 256), 0)
        fits = ((rows >= low) & (rows <= high)) | (rows == here)
        xs[j // 2, j % 2] = jnp.where(fits, 0.0, MASKED).astype(BF16)
    link.wait_weights(0)

    for m in range(3):
        out = forward(m, xt)
        if m == 0:
            out = out * 0.125
        qkv[m] = out.astype(BF16).reshape(H, HD, T)

    ones = jnp.ones((16, T), BF16)

    def attend(q, k, v, q_at, width, keys, masked):
        s = dot(k[:, 0:keys], q[:, q_at:q_at + width], 0, 0)
        if masked:
            j = q_at // 256
            s = s + xs[j // 2, j % 2, 0:keys, :].astype(F32)
        top = jnp.max(s, axis=0, keepdims=True)
        e = jnp.exp(s - top).astype(BF16)
        both = dot(v[:, 0:keys], e, 1, 0)
        inverse = 1.0 / both[HD:HD + 1]
        return e, both[0:HD] * inverse, inverse

    def self_tile(i, j):
        if j == 3:
            return 0, 256 * i
        if j == 1:
            return 512 * i, 1024
        return (0 if j == 0 else 256), 512 + 256 * i

    def own_out(pair):
        return pltpu.make_async_copy(ring.at[pair], es_hbm.at[pair], esem.at[pair])

    def own_in(pair):
        return pltpu.make_async_copy(es_hbm.at[pair], ring.at[pair], esem.at[pair])

    def e_out(h, slot):
        return pltpu.make_async_copy(ring.at[slot, :, pl.ds(0, T)], e_hbm.at[h], esem.at[slot])

    def e_in(h, slot):
        return pltpu.make_async_copy(e_hbm.at[h], ring.at[slot, :, pl.ds(0, T)], esem.at[slot])

    @pl.loop(0, 4)
    def _(pair):
        for i in range(2):
            h = pair * 2 + i
            v = jnp.concatenate([qkv[2, h], ones], axis=0)
            for j in range(4):
                keys = 256 * (j + 1)
                at = slice(256 * j, 256 * j + 256)
                e, out, inverse = attend(qkv[0, h], qkv[1, h], v, 256 * j, 256, keys, True)
                row, lane = self_tile(i, j)
                ring[pair, row:row + keys, lane:lane + 256] = e
                ctx[h, :, at] = out.astype(BF16)
                inv[0, h, :, at] = inverse
        own_out(pair).start()
        link.during_self(pair)

    link.wait_weights(1)
    for m in (5, 6):
        pay[m - 4] = forward(m, mt).astype(BF16).reshape(H, HD, T)

    def norm(total):
        average = jnp.mean(total, axis=0, keepdims=True)
        centred = total - average
        factor = lax.rsqrt(jnp.mean(centred * centred, axis=0, keepdims=True) + EPSILON)
        return centred * factor, factor

    @pl.loop(0, 4)
    def _(tb):
        at = pl.ds(pl.multiple_of(tb * TB, TB), TB)
        out = forward(3, ctx[:, :, at].reshape(D, TB))
        normed, factor = norm(param(6) * xt[:, at].astype(F32) + out)
        xh0[:, at] = normed
        rstd[0, :, at] = factor
        flow[:, at] = (normed * param(0) + param(3)).astype(BF16)

    pay[0] = (forward(4, flow) * 0.125).astype(BF16).reshape(H, HD, T)

    @pl.loop(0, 2)
    def _(four):
        for slot in range(4):
            h = four * 4 + slot

            @pl.when(four == 0)
            def _():
                own_out(slot).wait()

            @pl.when(four > 0)
            def _():
                e_out(slot, slot).wait()

            v = jnp.concatenate([pay[2, h], ones], axis=0)
            for j in range(2):
                at = slice(512 * j, 512 * j + 512)
                e, out, inverse = attend(pay[0, h], pay[1, h], v, 512 * j, 512, T, False)
                ring[slot, :, at.start:at.stop] = e
                cctx[h, :, at] = out.astype(BF16)
                inv[1, h, :, at] = inverse
            e_out(h, slot).start()
            link.during_cross(h)

    @pl.loop(0, 4)
    def _(tb):
        at = pl.ds(pl.multiple_of(tb * TB, TB), TB)
        out = forward(7, cctx[:, :, at].reshape(D, TB))
        first = xh0[:, at] * param(0) + param(3)
        normed, factor = norm(param(7) * first + out)
        xh1[:, at] = normed
        rstd[1, :, at] = factor
        slow[:, at] = (normed * param(1) + param(4)).astype(BF16)

    for slot in range(4):
        e_out(4 + slot, slot).wait()
    link.wait_weights(2)
    link.wait_weights(3)
    link.wait_input(2)

    def up(r, b):
        return wup[r, b].reshape(512, 256)

    def down(b):
        return wdn[b // 4, :, :, :, 32 * (b % 4):32 * (b % 4) + 32, :].reshape(D, 256)

    for b in range(4):
        place = slice(512 * (b % 2), 512 * (b % 2) + 512)
        for t in range(2):
            at = slice(512 * t, 512 * t + 512)
            v = dot(up(0, b), slow[0:256, at], 1, 0) + dot(up(1, b), slow[256:512, at], 1, 0)
            value, slope = gelu_both(v)
            ring[b // 2, place, at] = value.astype(BF16)
            ring[2 + b // 2, place, at] = slope.astype(BF16)

    def norm_back(upstream, normed, factor, k):
        scaled = upstream * param(k)
        one = jnp.mean(scaled, axis=0, keepdims=True)
        two = jnp.mean(scaled * normed, axis=0, keepdims=True)
        add_col(k, upstream * normed)
        add_col(3 + k, upstream)
        return factor * (scaled - one - normed * two)

    @pl.loop(0, 4)
    def _(tb):
        at = pl.ds(pl.multiple_of(tb * TB, TB), TB)
        out = None
        for b in range(8):
            part = dot(down(b), ring[b // 4, 256 * (b % 4):256 * (b % 4) + 256, at], 1, 0)
            out = part if out is None else out + part
        second = xh1[:, at] * param(1) + param(4)
        normed, factor = norm(param(8) * second + out)
        final = (normed * param(2) + param(5)).astype(BF16)
        upstream = jnp.concatenate([cs[0, at, :].T, cs[1, at, :].T], axis=0).astype(F32)
        for r in range(2):
            xs[0, r, at, :] = final[256 * r:256 * r + 256].T
        third = norm_back(upstream, normed, factor, 2)
        add_col(8, third * second)
        sg[:, at] = param(8) * third
        tlow[:, at] = third.astype(BF16)

    link.put_output(0)

    def square_grad(m, left, right):
        for r in range(2):
            part = dot(left, right[256 * r:256 * r + 256], 1, 1).astype(BF16)
            w8[r, :, :, :, 32 * m:32 * m + 32, :] = part.reshape(4, 2, 2, 32, 256)

    link.gathered()
    for f in range(8):
        rows = slice(256 * (f % 4), 256 * (f % 4) + 256)
        grad = dot(down(f), tlow[...], 0, 0) * ring[2 + f // 4, rows, 0:T].astype(F32)
        part = dot(tlow[...], ring[f // 4, rows, 0:T], 1, 1).astype(BF16)
        wdn[f // 4, :, :, :, 32 * (f % 4):32 * (f % 4) + 32, :] = part.reshape(4, 2, 2, 32, 256)
        ring[2 + f // 4, rows, 0:T] = grad.astype(BF16)
    link.reduce(0, 0)
    for r in range(2):
        half = slice(256 * r, 256 * r + 256)
        for t in range(2):
            at = slice(512 * t, 512 * t + 512)
            part = None
            for b in range(4):
                place = slice(512 * (b % 2), 512 * (b % 2) + 512)
                one = dot(up(r, b), ring[2 + b // 2, place, at], 0, 0)
                part = one if part is None else part + one
            sg[half, at] = sg[half, at] + part
    for b in range(4):
        grad = ring[2 + b // 2, 512 * (b % 2):512 * (b % 2) + 512, 0:T]
        for r in range(2):
            part = dot(grad, slow[256 * r:256 * r + 256], 1, 1).astype(BF16)
            wup[r, b] = part.reshape(2, 2, 128, 256)
    link.reduce(1, 0)
    link.reduce(0, 1)

    for slot in range(4):
        e_in(slot, slot).start()

    @pl.loop(0, 4)
    def _(tb):
        at = pl.ds(pl.multiple_of(tb * TB, TB), TB)
        middle = norm_back(sg[:, at], xh1[:, at], rstd[1, :, at], 1)
        add_col(7, middle * (xh0[:, at] * param(0) + param(3)))
        sg[:, at] = param(7) * middle
        tlow[:, at] = middle.astype(BF16)

    for r in range(2):
        slow[256 * r:256 * r + 256] = dot(weight(r, 7), tlow[...], 0, 0).astype(BF16)
    square_grad(7, tlow[...], cctx[...].reshape(D, T))
    link.reduce(1, 1)
    link.reduce(0, 2)

    def scaled_grad(context, which, h):
        rows = pl.ds(pl.multiple_of(h * HD, HD), HD)
        g = (slow[rows, :].astype(F32) * inv[which, h]).astype(BF16)
        delta = jnp.sum(g.astype(F32) * context[h].astype(F32), axis=0, keepdims=True)
        return g, delta

    @pl.loop(0, 2)
    def _(four):
        for slot in range(4):
            h = four * 4 + slot
            e_in(h, slot).wait()
            g, delta = scaled_grad(cctx, 1, h)
            q, k, v = pay[0, h], pay[1, h], pay[2, h]
            dp = dot(v, g, 0, 0)
            e = ring[slot, :, 0:T]
            ds = e * (dp - delta).astype(BF16)
            pay[0, h] = (dot(k, ds, 1, 0) * 0.125).astype(BF16)
            pay[1, h] = dot(q, ds, 1, 1).astype(BF16)
            pay[2, h] = dot(g, e, 1, 1).astype(BF16)

            @pl.when(four == 0)
            def _():
                e_in(h + 4, slot).start()

            @pl.when(four == 1)
            def _():
                own_in(slot).start()

            link.during_cross_back(h)

    grads = [pay[i].reshape(D, T) for i in range(3)]
    for r in range(2):
        out = dot(weight(r, 5), grads[1], 0, 0) + dot(weight(r, 6), grads[2], 0, 0)
        gs[r] = out.T.astype(BF16)
    link.put_output(1)
    for r in range(2):
        half = slice(256 * r, 256 * r + 256)
        sg[half] = sg[half] + dot(weight(r, 4), grads[0], 0, 0)
    square_grad(4, grads[0], flow)
    square_grad(5, grads[1], mt)
    square_grad(6, grads[2], mt)
    link.reduce(2, 0)

    @pl.loop(0, 4)
    def _(tb):
        at = pl.ds(pl.multiple_of(tb * TB, TB), TB)
        inner = norm_back(sg[:, at], xh0[:, at], rstd[0, :, at], 0)
        add_col(6, inner * xt[:, at].astype(F32))
        sg[:, at] = param(6) * inner
        tlow[:, at] = inner.astype(BF16)

    for k in range(9):
        part = jnp.sum(cols[k], axis=1, keepdims=True)
        gcol[:, :, :, :, :, k:k + 1] = part.reshape(2, 4, 2, 2, 16, 1)
    link.reduce(4, 0)
    link.reduce(2, 1)

    for r in range(2):
        slow[256 * r:256 * r + 256] = dot(weight(r, 3), tlow[...], 0, 0).astype(BF16)
    square_grad(3, tlow[...], ctx[...].reshape(D, T))
    link.reduce(4, 1)

    @pl.loop(0, 4)
    def _(pair):
        own_in(pair).wait()
        for i in range(2):
            h = pair * 2 + i
            g, delta = scaled_grad(ctx, 0, h)
            q, k, v = qkv[0, h], qkv[1, h], qkv[2, h]
            for j in (3, 2, 1, 0):
                keys = 256 * (j + 1)
                at = slice(256 * j, 256 * j + 256)
                row, lane = self_tile(i, j)
                e = ring[pair, row:row + keys, lane:lane + 256]
                dp = dot(v[:, 0:keys], g[:, at], 0, 0)
                ds = e * (dp - delta[:, at]).astype(BF16)
                qkv[0, h, :, at] = (dot(k[:, 0:keys], ds, 1, 0) * 0.125).astype(BF16)
                new_k = dot(q[:, at], ds, 1, 1)
                new_v = dot(g[:, at], e, 1, 1)
                if j == 3:
                    acc[i, 0] = new_k
                    acc[i, 1] = new_v
                else:
                    acc[i, 0, :, 0:keys] = acc[i, 0, :, 0:keys] + new_k
                    acc[i, 1, :, 0:keys] = acc[i, 1, :, 0:keys] + new_v
            qkv[1, h] = acc[i, 0].astype(BF16)
            qkv[2, h] = acc[i, 1].astype(BF16)
        link.during_self_back(pair)

    grads = [qkv[i].reshape(D, T) for i in range(3)]
    link.free_output(1)
    for r in range(2):
        out = sg[256 * r:256 * r + 256]
        for m in range(3):
            out = out + dot(weight(r, m), grads[m], 0, 0)
        gs[r] = out.T.astype(BF16)
    link.put_output(2)
    for m in range(3):
        square_grad(m, grads[m], xt)
    link.reduce(3, 0)
    link.finish()


class Alone:
    def __init__(self, inputs, outputs, weights, grads, buffers, sem):
        self.inputs, self.outputs, self.weights, self.grads = inputs, outputs, weights, grads
        self.xs, self.cs, self.gs, self.w8, self.wup, self.wdn = buffers
        self.sem = sem
        copy = pltpu.make_async_copy
        self.loads = [
            copy(inputs[0], self.xs.at[0], sem.at[0]),
            copy(inputs[1], self.xs.at[1], sem.at[1]),
            copy(inputs[2], self.cs, sem.at[2]),
            copy(self.squares(weights), self.w8, sem.at[3]),
            copy(weights.at[:, :, :, :, pl.ds(256, 128), :], self.wup, sem.at[4]),
            copy(weights.at[:, :, :, :, pl.ds(384, 128), :], self.wdn, sem.at[5]),
        ]
        self.stores = [
            copy(self.xs.at[0], outputs[0], sem.at[6]),
            copy(self.gs, outputs[1], sem.at[7]),
            copy(self.gs, outputs[2], sem.at[7]),
        ]

    def squares(self, ref):
        return ref.at[:, :, :, :, pl.ds(0, 256), :]

    def begin(self):
        for load in self.loads:
            load.start()

    def line(self, ref):
        return ref[0:1, :]

    def wait_input(self, i):
        self.loads[i].wait()

    def wait_weights(self, group):
        if group == 0:
            self.loads[3].wait()
        if group == 2:
            self.loads[4].wait()
            self.loads[5].wait()

    def gathered(self):
        pass

    def put_output(self, i):
        self.stores[i].start()

    def free_output(self, i):
        self.stores[i].wait()

    def during_self(self, pair):
        pass

    def during_cross(self, h):
        pass

    def during_cross_back(self, h):
        pass

    def during_self_back(self, pair):
        pass

    def reduce(self, group, step):
        pass

    def finish(self):
        copies = [
            pltpu.make_async_copy(self.w8, self.squares(self.grads), self.sem.at[0]),
            pltpu.make_async_copy(
                self.wup, self.grads.at[:, :, :, :, pl.ds(256, 128), :], self.sem.at[1]
            ),
            pltpu.make_async_copy(
                self.wdn, self.grads.at[:, :, :, :, pl.ds(384, 128), :], self.sem.at[2]
            ),
        ]
        for copy in copies:
            copy.start()
        for copy in copies:
            copy.wait()
        self.stores[0].wait()
        self.stores[2].wait()


ROW_PARTS = ((0, 96), (96, 256), (0, 128), (0, 128))


class Linked:
    def __init__(self, inputs, shards, params, outputs, gout, cout, buffers, landing, sems):
        self.inputs, self.shards, self.params = inputs, shards, params
        self.outputs, self.gout, self.cout = outputs, gout, cout
        self.xs, self.cs, self.gs, self.w8, self.wup, self.wdn, self.par, self.gcol = buffers
        self.land0, self.land1, self.land2, self.land3 = landing[:4]
        self.small = landing[4:]
        isem, lsem, gsend, grecv, osem, rsend, rrecv = sems
        r = lax.axis_index("row")
        col = lax.axis_index("col")
        z, y, x = col // 4, lax.rem(col // 2, 2), lax.rem(col, 2)
        self.r, self.z, self.y, self.x = r, z, y, x

        def chip(dz=0, dy=0, dx=0):
            to_z = lax.rem(z + dz, 4)
            to_y = 1 - y if dy else y
            to_x = 1 - x if dx else x
            return to_z * 4 + to_y * 2 + to_x

        self.zs = [lax.rem(z + d, 4) for d in range(4)]
        partner = (1 - r, col)
        across = {"x": (r, chip(dx=1)), "y": (r, chip(dy=1))}
        along = [(r, chip(dz=d)) for d in (1, 2, 3)]
        self.peers = [partner, across["x"], across["y"], *along]

        def remote(source, target, send, recv, device):
            return pltpu.make_async_remote_copy(
                src_ref=source, dst_ref=target, send_sem=send, recv_sem=recv,
                device_id=device, device_id_type=pl.DeviceIdType.MESH,
            )

        places = [self.xs.at[0], self.xs.at[1], self.cs]
        self.keep_in = [
            pltpu.make_async_copy(inputs[i].at[r], places[i].at[r], lsem.at[i]) for i in range(3)
        ]
        self.swap_in = [
            remote(inputs[i].at[1 - r], places[i].at[r], isem.at[0, i], isem.at[1, i], partner)
            for i in range(3)
        ]
        self.swap_par = remote(self.par.at[r], self.par.at[r], isem.at[0, 3], isem.at[1, 3], partner)

        sources = [self.xs.at[0], self.gs, self.gs]
        self.keep_out = [
            pltpu.make_async_copy(sources[i].at[r], outputs[i].at[r], lsem.at[3 + i]) for i in range(3)
        ]
        self.swap_out = [
            remote(sources[i].at[1 - r], outputs[i].at[r], osem.at[0, i], osem.at[1, i], partner)
            for i in range(3)
        ]

        holders = (self.w8, self.w8, self.wup, self.wdn)
        self.gathers = []
        for group in range(4):
            first, last = ROW_PARTS[group]
            middle = (first + last) // 2
            halves = []
            for half in range(2):
                rows = pl.ds((first, middle)[half], middle - first)
                ref = holders[group]
                send, recv = gsend.at[2 * group + half], grecv.at[2 * group + half]
                own = ref.at[r, z, y, x, rows]
                line = ref.at[r, :, y, x, rows]
                sheet = ref.at[r, :, :, x, rows] if half == 0 else ref.at[r, :, y, :, rows]
                whole = ref.at[r, :, :, :, rows]
                axes = ("y", "x") if half == 0 else ("x", "y")
                halves.append([
                    [remote(own, own, send.at[d], recv.at[d], along[d]) for d in range(3)],
                    [remote(line, line, send.at[3], recv.at[3], across[axes[0]])],
                    [remote(sheet, sheet, send.at[4], recv.at[4], across[axes[1]])],
                    [remote(whole, whole, send.at[5], recv.at[5], partner)],
                ])
            self.gathers.append(halves)

        grads = (self.wdn, self.wup, self.w8, self.w8)
        offsets = (0, 0, 128, 0)
        self.sums = []
        for group in range(4):
            ref, at = grads[group], offsets[group]
            rows = pl.ds(at, 128)
            send, recv = rsend.at[group], rrecv.at[group]
            steps = [[remote(ref.at[1 - r, :, :, :, rows], self.land0.at[group], send.at[0], recv.at[0], partner)]]
            one, two, three = [], [], []
            for half in range(2):
                part = pl.ds(at + 64 * half, 64)
                axes = ("x", "y") if half == 0 else ("y", "x")
                if half == 0:
                    source1 = ref.at[r, :, :, 1 - x, part]
                    source2 = ref.at[r, :, 1 - y, x, part]
                else:
                    source1 = ref.at[r, :, 1 - y, :, part]
                    source2 = ref.at[r, :, y, 1 - x, part]
                k = 1 + 5 * half
                one.append(remote(source1, self.land1.at[group, half], send.at[k], recv.at[k], across[axes[0]]))
                two.append(remote(source2, self.land2.at[group, half], send.at[k + 1], recv.at[k + 1], across[axes[1]]))
                for d in range(3):
                    three.append(remote(
                        ref.at[r, self.zs[d + 1], y, x, part], self.land3.at[group, half, d],
                        send.at[k + 2 + d], recv.at[k + 2 + d], along[d],
                    ))
            self.sums.append([*steps, one, two, three])
        send, recv = rsend.at[4], rrecv.at[4]
        ref = self.gcol
        self.sums.append([
            [remote(ref.at[1 - r], self.small[0], send.at[0], recv.at[0], partner)],
            [remote(ref.at[r, :, :, 1 - x], self.small[1], send.at[1], recv.at[1], across["x"])],
            [remote(ref.at[r, :, 1 - y, x], self.small[2], send.at[2], recv.at[2], across["y"])],
            [
                remote(ref.at[r, self.zs[d + 1], y, x], self.small[3].at[d], send.at[3 + d], recv.at[3 + d], along[d])
                for d in range(3)
            ],
        ])
        self.grads, self.offsets = grads, offsets
        self.done = set()

    def begin(self):
        r, z, y, x = self.r, self.z, self.y, self.x
        for copy in self.keep_in:
            copy.start()
        for m in range(8):
            self.w8[r, z, y, x, 32 * m:32 * m + 32, :] = self.shards[m][...].T
        self.wup[r, z, y, x] = self.shards[8][...].T
        for s in range(4):
            self.wdn[r, z, y, x, 32 * s:32 * s + 32, :] = self.shards[9][256 * s:256 * s + 256, :].T
        for k in range(3):
            self.par[r, 3 * k:3 * k + 3, :] = self.params[k][...]
        barrier = pltpu.get_barrier_semaphore()
        for peer in self.peers:
            pl.semaphore_signal(barrier, inc=1, device_id=peer, device_id_type=pl.DeviceIdType.MESH)
        pl.semaphore_wait(barrier, len(self.peers))
        self.gather(0, 0)
        self.swap_in[0].start()
        self.swap_par.start()
        self.swap_in[1].start()
        self.swap_in[2].start()

    def gather(self, group, step):
        for half in range(2):
            steps = self.gathers[group][half]
            if step > 0:
                for copy in steps[step - 1]:
                    copy.wait_recv()
            if step < 4:
                for copy in steps[step]:
                    copy.start()

    def line(self, ref):
        return ref[pl.ds(self.r, 1), :]

    def wait_input(self, i):
        self.keep_in[i].wait()
        self.swap_in[i].wait_recv()
        if i == 0:
            self.gather(0, 1)
        if i == 1:
            self.gather(0, 2)
            self.swap_par.wait_recv()

    def wait_weights(self, group):
        if group == 0:
            self.gather(0, 3)
            self.gather(1, 0)
            self.gather(0, 4)
        elif group == 1:
            self.gather(1, 4)
        elif group == 2:
            self.gather(2, 4)
            self.gather(3, 4)

    def gathered(self):
        for halves in self.gathers:
            for half in halves:
                for step in half:
                    for copy in step:
                        copy.wait_send()

    def at_turn(self, index, turns):
        for turn, actions in turns.items():

            @pl.when(index == turn)
            def _():
                for group, step, move in actions:
                    move(group, step)

    def during_self(self, pair):
        move = self.gather
        self.at_turn(pair, {
            0: [(1, 1, move)],
            1: [(1, 2, move)],
            2: [(1, 3, move), (2, 0, move)],
            3: [(3, 0, move)],
        })

    def during_cross(self, h):
        move = self.gather
        self.at_turn(h, {
            0: [(2, 1, move)],
            1: [(3, 1, move)],
            2: [(2, 2, move)],
            3: [(3, 2, move)],
            5: [(2, 3, move)],
            7: [(3, 3, move)],
        })

    def during_cross_back(self, h):
        move = self.reduce
        self.at_turn(h, {
            1: [(0, 3, move)],
            2: [(1, 2, move)],
            4: [(1, 3, move)],
            5: [(0, 4, move)],
            7: [(1, 4, move)],
        })

    def during_self_back(self, pair):
        move = self.reduce
        self.at_turn(pair, {
            0: [(2, 2, move), (4, 2, move)],
            1: [(2, 3, move), (4, 3, move)],
            2: [(2, 4, move), (4, 4, move)],
        })

    def put_output(self, i):
        self.keep_out[i].start()
        self.swap_out[i].start()

    def free_output(self, i):
        self.keep_out[i].wait()
        self.swap_out[i].wait_send()

    def reduce(self, group, step):
        r, z, y, x = self.r, self.z, self.y, self.x
        steps = self.sums[group]
        if step > 0:
            for copy in steps[step - 1]:
                copy.wait_recv()
        if group == 4:
            ref = self.gcol
            if step == 1:
                ref[r] = ref[r] + self.small[0][...]
            elif step == 2:
                ref[r, :, :, x] = ref[r, :, :, x] + self.small[1][...]
            elif step == 3:
                ref[r, :, y, x] = ref[r, :, y, x] + self.small[2][...]
            elif step == 4:
                total = ref[r, z, y, x]
                for d in range(3):
                    total = total + self.small[3][d]
                self.cout[...] = total
        elif step > 0:
            ref, at = self.grads[group], self.offsets[group]

            def add(place, value):
                total = ref[place].astype(F32) + value.astype(F32)
                ref[place] = total.astype(BF16)

            if step == 1:
                for k in range(4):
                    add((r, k, slice(None), slice(None), slice(at, at + 128)), self.land0[group, k])
            for half in range(2):
                part = slice(at + 64 * half, at + 64 * half + 64)
                if step == 2 and half == 0:
                    add((r, slice(None), slice(None), x, part), self.land1[group, half])
                elif step == 2:
                    add((r, slice(None), y, slice(None), part), self.land1[group, half])
                elif step == 3:
                    add((r, slice(None), y, x, part), self.land2[group, half])
                elif step == 4:
                    total = ref[r, z, y, x, part].astype(F32)
                    for d in range(3):
                        total = total + self.land3[group, half, d].astype(F32)
                    self.gout[group, 64 * half:64 * half + 64] = total
        if step < 4:
            for copy in steps[step]:
                copy.start()

    def finish(self):
        for step in range(1, 5):
            self.reduce(3, step)
        for steps in self.sums:
            for step in steps:
                for copy in step:
                    copy.wait_send()
        for copy in self.swap_in:
            copy.wait_send()
        self.swap_par.wait_send()
        for i in (0, 2):
            self.keep_out[i].wait()
            self.swap_out[i].wait_send()
        for copy in self.swap_out:
            copy.wait_recv()


CHIPS = 16


def to_sixteen(w):
    n = w.shape[1]
    if n == CHIPS:
        return w
    part = D // n

    def spread(block):
        block = block.reshape(2, n, -1, part, 256).swapaxes(1, 2).reshape(2, -1, CHIPS, 32, 256)
        return block.swapaxes(1, 2).reshape(2, CHIPS, -1, 256)

    return jnp.concatenate(
        [
            spread(w[:, :, :8 * part]),
            w[:, :, 8 * part:12 * part].reshape(2, CHIPS, 128, 256),
            spread(w[:, :, 12 * part:]),
        ],
        axis=2,
    )


def from_sixteen(g, n):
    if n == CHIPS:
        return g
    part = D // n

    def gather(block):
        block = block.reshape(2, CHIPS, -1, 32, 256).swapaxes(1, 2).reshape(2, -1, n, part, 256)
        return block.swapaxes(1, 2).reshape(2, n, -1, 256)

    return jnp.concatenate(
        [
            gather(g[:, :, :256]),
            g[:, :, 256:384].reshape(2, n, 4 * part, 256),
            gather(g[:, :, 384:]),
        ],
        axis=2,
    )


ANY = pl.BlockSpec(memory_space=pl.ANY)
VMEM = pl.BlockSpec(memory_space=pltpu.VMEM)
SHAPE = jax.ShapeDtypeStruct
STASH = [SHAPE((H, T, T), BF16), SHAPE((4, T, 1280), BF16)]


def layer_scratch():
    V = pltpu.VMEM
    return [
        V((2, 2, T, 256), BF16), V((2, T, 256), BF16),
        V((D, T), BF16), V((D, T), BF16),
        V((2, 4, 2, 2, 256, 256), BF16),
        V((2, 4, 2, 2, 128, 256), BF16), V((2, 4, 2, 2, 128, 256), BF16),
        V((3, H, HD, T), BF16), V((3, H, HD, T), BF16),
        V((H, HD, T), BF16), V((H, HD, T), BF16),
        V((2, H, 1, T), F32),
        V((D, T), F32), V((D, T), F32), V((2, 1, T), F32),
        V((D, T), BF16), V((D, T), BF16), V((D, T), BF16),
        V((4, T, 1280), BF16),
        V((D, T), F32), V((2, T, 256), BF16),
        V((D, 128), F32), V((9, D, 128), F32),
        V((2, 2, HD, T), F32),
        pltpu.SemaphoreType.DMA((4,)),
    ]


def run_alone(x, mem, cot, w, par, seg, pad):
    def kernel(x, mem, cot, w, par, seg, pad, lo, mg, tg, g, e, es, gcol, *rest):
        scratch, sem = rest[:-1], rest[-1]
        xs, cs, gs = scratch[0], scratch[1], scratch[20]
        link = Alone(
            (x, mem, cot), (lo, mg, tg), w, g, (xs, cs, gs, scratch[4], scratch[5], scratch[6]), sem
        )
        layer(link, e, es, par, seg, pad, *scratch[:-1], gcol, scratch[-1])

    wide = SHAPE((2, T, 256), BF16)
    return pl.pallas_call(
        kernel,
        in_specs=[ANY] * 4 + [VMEM] * 3,
        out_specs=[ANY] * 6 + [VMEM],
        out_shape=[wide] * 3
        + [SHAPE((2, 4, 2, 2, 512, 256), BF16), *STASH, SHAPE((2, 4, 2, 2, 16, 128), F32)],
        scratch_shapes=layer_scratch() + [pltpu.SemaphoreType.DMA((8,))],
        compiler_params=pltpu.CompilerParams(vmem_limit_bytes=63 * 2**20),
        name="layer",
    )(x, mem, cot, w, par, seg, pad)


def run_linked(inputs, shards, params, seg, pad):
    def kernel(*refs):
        inputs, shards, params, seg, pad = refs[0:3], refs[3:13], refs[13:16], refs[16], refs[17]
        outputs, e, es, gout, cout = refs[18:21], refs[21], refs[22], refs[23], refs[24]
        scratch = refs[25:25 + 25]
        par, gcol = refs[50], refs[51]
        landing, sems = refs[52:60], refs[60:]
        xs, cs, gs = scratch[0], scratch[1], scratch[20]
        link = Linked(
            inputs, shards, params, outputs, gout, cout,
            (xs, cs, gs, scratch[4], scratch[5], scratch[6], par, gcol), landing, sems,
        )
        layer(link, e, es, par, seg, pad, *scratch[:-1], gcol, scratch[-1])

    V = pltpu.VMEM
    DMA = pltpu.SemaphoreType.DMA
    wide = SHAPE((2, T, 256), BF16)
    return pl.pallas_call(
        kernel,
        in_specs=[ANY] * 3 + [VMEM] * 15,
        out_specs=[ANY] * 5 + [VMEM] * 2,
        out_shape=[wide] * 3 + STASH + [SHAPE((4, 128, 256), F32), SHAPE((16, 128), F32)],
        scratch_shapes=layer_scratch() + [
            V((2, 16, 256), F32), V((2, 4, 2, 2, 16, 128), F32),
            V((4, 4, 2, 2, 128, 256), BF16), V((4, 2, 4, 2, 64, 256), BF16),
            V((4, 2, 4, 64, 256), BF16), V((4, 2, 3, 64, 256), BF16),
            V((4, 2, 2, 16, 128), F32), V((4, 2, 16, 128), F32),
            V((4, 16, 128), F32), V((3, 16, 128), F32),
            DMA((2, 4)), DMA((6,)), DMA((8, 6)), DMA((8, 6)), DMA((2, 3)), DMA((5, 11)), DMA((5, 11)),
        ],
        compiler_params=pltpu.CompilerParams(
            vmem_limit_bytes=63 * 2**20, collective_id=0, has_side_effects=True
        ),
        name="layer",
    )(*inputs, *shards, *params, seg, pad)


def ending(lo, mg, tg, gout, cout):
    def kernel(lo, mg, tg, gout, cout, lo_out, tg_out, mg_out, *rest):
        lo_out[...] = lo[...]
        mg_out[...] = mg[...].astype(F32)
        tg_out[...] = tg[...].astype(F32)

        @pl.when(pl.program_id(0) == 0)
        def _():
            for m in range(8):
                at = 32 * (m % 4)
                rest[m][...] = gout[3 if m < 4 else 2, at:at + 32, :].T
            rest[8][...] = gout[1].T
            for s in range(4):
                rest[9][256 * s:256 * s + 256, :] = gout[0, 32 * s:32 * s + 32, :].T
            small = cout[...].T
            for k in range(3):
                rest[10 + k][...] = small[3 * k:3 * k + 3, :]

    part = pl.BlockSpec((1, 512, 256), lambda i: (i // 2, i % 2, 0))

    def whole(*shape):
        return pl.BlockSpec(shape, lambda i: (0,) * len(shape))

    shapes = [(256, 32)] * 8 + [(256, 128), (1024, 32)] + [(3, 16)] * 3
    return pl.pallas_call(
        kernel,
        grid=(4,),
        in_specs=[part] * 3 + [whole(4, 128, 256), whole(16, 128)],
        out_specs=[part] * 3 + [whole(*one) for one in shapes],
        out_shape=[SHAPE((2, T, 256), BF16), SHAPE((2, T, 256), F32), SHAPE((2, T, 256), F32)]
        + [SHAPE(one, F32) for one in shapes],
        name="ending",
    )(lo, mg, tg, gout, cout)


def body(
    tokens, memory, cotangent, segments, padding,
    self_query, self_key, self_value, self_output,
    cross_query, cross_key, cross_value, cross_output,
    feed_up, feed_down, norm_gain, norm_bias, omegas,
):
    n = lax.axis_size("col")
    squares = (
        self_query, self_key, self_value, self_output,
        cross_query, cross_key, cross_value, cross_output,
    )
    if n == CHIPS:
        lo, mg, tg, _, _, gout, cout = run_linked(
            (tokens, memory, cotangent), (*squares, feed_up, feed_down),
            (norm_gain, norm_bias, omegas), segments, padding,
        )
        return tuple(ending(lo, mg, tg, gout, cout))
    row = lax.axis_index("row")
    part = D // n
    blob = jnp.concatenate(
        [m.T for m in squares]
        + [feed_up.T]
        + [feed_down.T[:, 256 * s:256 * s + 256] for s in range(4)],
        axis=0,
    )
    w = lax.all_gather(blob, ("row", "col"), axis=0, tiled=False).reshape(2, n, 16 * part, 256)
    w = to_sixteen(w).reshape(2, 4, 2, 2, 512, 256)
    par = jnp.concatenate([norm_gain, norm_bias, omegas, jnp.zeros((7, 256), F32)], axis=0)
    par = lax.all_gather(par, "row", axis=0, tiled=False)

    def mine(array):
        return lax.all_to_all(array, "row", split_axis=0, concat_axis=0, tiled=True)

    seg = lax.dynamic_slice_in_dim(segments, row, 1, 0)
    pad = lax.dynamic_slice_in_dim(padding, row, 1, 0)
    lo, mg, tg, g, _, _, gcol = run_alone(
        mine(tokens), mine(memory), mine(cotangent), w, par, seg, pad
    )
    lo, tg, mg = mine(lo), mine(tg).astype(F32), mine(mg).astype(F32)
    g = from_sixteen(g.reshape(2, CHIPS, 512, 256), n).reshape(2 * n, 16 * part, 256)
    g = lax.psum_scatter(g.astype(F32), ("row", "col"), scatter_dimension=0, tiled=False)
    gcol = lax.psum_scatter(
        gcol.reshape(2 * n, part // 2, 128), ("row", "col"), scatter_dimension=0, tiled=False
    )
    small = gcol[:, 0:9].T
    last = 12 * part
    return (
        lo, tg, mg,
        *[g[part * m:part * m + part].T for m in range(8)],
        g[8 * part:last].T,
        jnp.concatenate([g[last + part * s:last + part * s + part].T for s in range(4)], axis=0),
        small[0:3], small[3:6], small[6:9],
    )


def solution(mesh):
    wide = P(None, "col", "row")
    square = P("row", "col")
    return jax.shard_map(
        body,
        mesh=mesh,
        in_specs=(wide,) * 3 + (P(None, "col"),) * 2 + (square,) * 10 + (P(None, "row"),) * 3,
        out_specs=(wide,) * 3 + (square,) * 10 + (P(None, ("row", "col")),) * 3,
        check_vma=False,
    )
```

```python
import jax
import jax.numpy as jnp
from jax import lax
from jax.experimental import pallas as pl
from jax.experimental.pallas import tpu as pltpu
from jax.sharding import PartitionSpec as P

F32 = jnp.float32
BF16 = jnp.bfloat16
EPSILON = 1e-05
MASKED = -1e30
T = 1024
D = 512
H = 8
HD = 64
TB = 256


def dot(left, right, left_dim, right_dim):
    return lax.dot_general(
        left, right, (((left_dim,), (right_dim,)), ((), ())), preferred_element_type=F32
    )


def gelu_both(v):
    root = 0.7978845608028654
    square = v * v
    t = jnp.tanh(root * v * (1.0 + 0.044715 * square))
    half = 0.5 * (1.0 + t)
    slope = half + (0.5 * root) * v * (1.0 - t * t) * (1.0 + (3.0 * 0.044715) * square)
    return v * half, slope


def layer(
    link, e_hbm, es_hbm, par, seg, pad,
    xs, cs, xt, mt, w8, wup, wdn, qkv, pay, ctx, cctx, inv, xh0, xh1, rstd,
    flow, slow, tlow, ring, sg, gs, pcol, cols, acc, gcol, esem,
):
    def weight(r, m):
        return w8[r, :, :, :, m * 32:(m + 1) * 32, :].reshape(D, 256)

    def forward(m, source):
        return dot(weight(0, m), source[0:256], 1, 0) + dot(weight(1, m), source[256:512], 1, 0)

    def param(k):
        return pcol[:, k:k + 1]

    def grad_of(ref, i):
        return ref[i].reshape(D, T)

    def add_col(k, value):
        cols[k] = cols[k] + (value[:, 0:128] + value[:, 128:256])

    link.begin()
    cols[...] = jnp.zeros_like(cols)
    link.wait_input(0)
    @part("turn_tokens")
    def _():
        for r in range(2):
            xt[256 * r:256 * r + 256] = xs[0, r].T

    link.moment("turn_tokens")
    link.wait_input(1)
    @part("turn_memory")
    def _():
        for r in range(2):
            mt[256 * r:256 * r + 256] = xs[1, r].T

    link.moment("turn_memory")
    pcol[...] = jnp.zeros_like(pcol)
    for r in range(2):
        pcol[256 * r:256 * r + 256, 0:16] = par[r].T

    @part("mask")
    def _():
        padlen = jnp.sum(link.line(pad), axis=1, keepdims=True)
        for j in range(4):
            low = link.line(seg)[:, 256 * j:256 * j + 256]
            here = 256 * j + lax.broadcasted_iota(jnp.int32, (1, 256), 1)
            high = jnp.minimum(here, padlen - 1)
            rows = lax.broadcasted_iota(jnp.int32, (T, 256), 0)
            fits = ((rows >= low) & (rows <= high)) | (rows == here)
            xs[j // 2, j % 2] = jnp.where(fits, 0.0, MASKED).astype(BF16)

    link.moment("mask")
    link.wait_weights(0)

    @part("self_projections")
    def _():
        for m in range(3):
            out = forward(m, xt)
            if m == 0:
                out = out * 0.125
            qkv[m] = out.astype(BF16).reshape(H, HD, T)

    link.moment("self_projections")
    ones = jnp.ones((16, T), BF16)

    def weighted(scores, v):
        top = jnp.max(scores, axis=0, keepdims=True)
        e = jnp.exp(scores - top).astype(BF16)
        both = dot(v, e, 1, 0)
        inverse = 1.0 / both[HD:HD + 1]
        return e, (both[0:HD] * inverse).astype(BF16), inverse

    def ahead(tiles, depth, product, rest):
        products = [product(*tile) for tile in tiles[:depth]]
        for n, tile in enumerate(tiles):
            if n + depth < len(tiles):
                products.append(product(*tiles[n + depth]))
            rest(*tile, products[n])

    def self_tile(i, j):
        if j == 3:
            return 0, 256 * i
        if j == 1:
            return 512 * i, 1024
        return (0 if j == 0 else 256), 512 + 256 * i

    def own_out(pair):
        return pltpu.make_async_copy(ring.at[pair], es_hbm.at[pair], esem.at[pair])

    def own_in(pair):
        return pltpu.make_async_copy(es_hbm.at[pair], ring.at[pair], esem.at[pair])

    def e_out(h, slot):
        return pltpu.make_async_copy(ring.at[slot, :, pl.ds(0, T)], e_hbm.at[h], esem.at[slot])

    def e_in(h, slot):
        return pltpu.make_async_copy(e_hbm.at[h], ring.at[slot, :, pl.ds(0, T)], esem.at[slot])

    @pl.loop(0, 4)
    def _(pair):
        @part("self_attention")
        def _():
            values = [jnp.concatenate([qkv[2, pair * 2 + i], ones], axis=0) for i in range(2)]

            def product(i, j):
                h, keys = pair * 2 + i, 256 * (j + 1)
                scores = dot(qkv[1, h, :, 0:keys], qkv[0, h, :, 256 * j:256 * j + 256], 0, 0)
                return scores + xs[j // 2, j % 2, 0:keys, :].astype(F32)

            def rest(i, j, scores):
                h, keys, at = pair * 2 + i, 256 * (j + 1), slice(256 * j, 256 * j + 256)
                e, out, inverse = weighted(scores, values[i][:, 0:keys])
                row, lane = self_tile(i, j)
                ring[pair, row:row + keys, lane:lane + 256] = e
                ctx[h, :, at] = out
                inv[0, h, :, at] = inverse

            ahead([(i, j) for j in range(4) for i in range(2)], 2, product, rest)

        own_out(pair).start()
        link.during_self(pair)

    link.wait_weights(1)
    @part("memory_projections")
    def _():
        for m in (5, 6):
            pay[m - 4] = forward(m, mt).astype(BF16).reshape(H, HD, T)

    def norm(total):
        average = jnp.mean(total, axis=0, keepdims=True)
        centred = total - average
        factor = lax.rsqrt(jnp.mean(centred * centred, axis=0, keepdims=True) + EPSILON)
        return centred * factor, factor

    @part("first_norm")
    def _():
        @pl.loop(0, 4)
        def _(tb):
            at = pl.ds(pl.multiple_of(tb * TB, TB), TB)
            out = forward(3, ctx[:, :, at].reshape(D, TB))
            normed, factor = norm(param(6) * xt[:, at].astype(F32) + out)
            xh0[:, at] = normed
            rstd[0, :, at] = factor
            flow[:, at] = (normed * param(0) + param(3)).astype(BF16)

    @part("probes")
    def _():
        pay[0] = (forward(4, flow) * 0.125).astype(BF16).reshape(H, HD, T)

    @pl.loop(0, 4)
    def _(two):
        slots = [lax.rem(two, 2) * 2 + i for i in range(2)]

        @pl.when(two < 2)
        def _():
            for slot in slots:
                own_out(slot).wait()

        @pl.when(two >= 2)
        def _():
            for slot in slots:
                e_out(slot, slot).wait()

        @part("cross_attention")
        def _():
            values = [jnp.concatenate([pay[2, two * 2 + i], ones], axis=0) for i in range(2)]

            def product(i, j):
                h = two * 2 + i
                return dot(pay[1, h], pay[0, h, :, 512 * j:512 * j + 512], 0, 0)

            def rest(i, j, scores):
                h, at = two * 2 + i, slice(512 * j, 512 * j + 512)
                e, out, inverse = weighted(scores, values[i])
                ring[slots[i], :, at] = e
                cctx[h, :, at] = out
                inv[1, h, :, at] = inverse

            ahead([(i, j) for i in range(2) for j in range(2)], 2, product, rest)

        for i in range(2):
            e_out(two * 2 + i, slots[i]).start()
        link.during_cross(two)

    link.wait_weights(2)

    @part("second_norm")
    def _():
        @pl.loop(0, 4)
        def _(tb):
            at = pl.ds(pl.multiple_of(tb * TB, TB), TB)
            out = forward(7, cctx[:, :, at].reshape(D, TB))
            first = xh0[:, at] * param(0) + param(3)
            normed, factor = norm(param(7) * first + out)
            xh1[:, at] = normed
            rstd[1, :, at] = factor
            slow[:, at] = (normed * param(1) + param(4)).astype(BF16)

    for slot in range(4):
        e_out(4 + slot, slot).wait()
    link.wait_weights(3)
    link.wait_input(2)

    def up(r, b):
        return wup[r, b].reshape(512, 256)

    def down(b):
        return wdn[b // 4, :, :, :, 32 * (b % 4):32 * (b % 4) + 32, :].reshape(D, 256)

    for part_of_two in range(2):

        @part("feed_up")
        def _():
            for b in (2 * part_of_two, 2 * part_of_two + 1):
                place = slice(512 * (b % 2), 512 * (b % 2) + 512)
                for t in range(2):
                    at = slice(512 * t, 512 * t + 512)
                    v = dot(up(0, b), slow[0:256, at], 1, 0) + dot(up(1, b), slow[256:512, at], 1, 0)
                    value, slope = gelu_both(v)
                    ring[b // 2, place, at] = value.astype(BF16)
                    ring[2 + b // 2, place, at] = slope.astype(BF16)

        if part_of_two == 0:
            link.moment("half_feed_up")

    link.wait_weights(4)

    def norm_back(upstream, normed, factor, k):
        scaled = upstream * param(k)
        one = jnp.mean(scaled, axis=0, keepdims=True)
        two = jnp.mean(scaled * normed, axis=0, keepdims=True)
        add_col(k, upstream * normed)
        add_col(3 + k, upstream)
        return factor * (scaled - one - normed * two)

    @part("feed_down")
    def _():
        @pl.loop(0, 4)
        def _(tb):
            at = pl.ds(pl.multiple_of(tb * TB, TB), TB)
            out = None
            for b in range(8):
                part = dot(down(b), ring[b // 4, 256 * (b % 4):256 * (b % 4) + 256, at], 1, 0)
                out = part if out is None else out + part
            second = xh1[:, at] * param(1) + param(4)
            normed, factor = norm(param(8) * second + out)
            final = (normed * param(2) + param(5)).astype(BF16)
            upstream = jnp.concatenate([cs[0, at, :].T, cs[1, at, :].T], axis=0).astype(F32)
            for r in range(2):
                xs[0, r, at, :] = final[256 * r:256 * r + 256].T
            third = norm_back(upstream, normed, factor, 2)
            add_col(8, third * second)
            sg[:, at] = param(8) * third
            tlow[:, at] = third.astype(BF16)

    link.put_output(0)

    def square_grad(m, left, right):
        for r in range(2):
            part = dot(left, right[256 * r:256 * r + 256], 1, 1).astype(BF16)
            w8[r, :, :, :, 32 * m:32 * m + 32, :] = part.reshape(4, 2, 2, 32, 256)

    link.gathered()
    @part("feed_down_back")
    def _():
        for f in range(8):
            rows = slice(256 * (f % 4), 256 * (f % 4) + 256)
            grad = dot(down(f), tlow[...], 0, 0) * ring[2 + f // 4, rows, 0:T].astype(F32)
            part = dot(tlow[...], ring[f // 4, rows, 0:T], 1, 1).astype(BF16)
            wdn[f // 4, :, :, :, 32 * (f % 4):32 * (f % 4) + 32, :] = part.reshape(4, 2, 2, 32, 256)
            ring[2 + f // 4, rows, 0:T] = grad.astype(BF16)

    link.moment("feed_down_back")
    @part("second_grad")
    def _():
        for r in range(2):
            half = slice(256 * r, 256 * r + 256)
            for t in range(2):
                at = slice(512 * t, 512 * t + 512)
                part = None
                for b in range(4):
                    place = slice(512 * (b % 2), 512 * (b % 2) + 512)
                    one = dot(up(r, b), ring[2 + b // 2, place, at], 0, 0)
                    part = one if part is None else part + one
                sg[half, at] = sg[half, at] + part

    @part("feed_up_grad")
    def _():
        for b in range(4):
            grad = ring[2 + b // 2, 512 * (b % 2):512 * (b % 2) + 512, 0:T]
            for r in range(2):
                part = dot(grad, slow[256 * r:256 * r + 256], 1, 1).astype(BF16)
                wup[r, b] = part.reshape(2, 2, 128, 256)

    link.moment("feed_up_grad")

    for slot in range(4):
        e_in(slot, slot).start()

    @part("middle_norm")
    def _():
        @pl.loop(0, 4)
        def _(tb):
            at = pl.ds(pl.multiple_of(tb * TB, TB), TB)
            middle = norm_back(sg[:, at], xh1[:, at], rstd[1, :, at], 1)
            add_col(7, middle * (xh0[:, at] * param(0) + param(3)))
            sg[:, at] = param(7) * middle
            tlow[:, at] = middle.astype(BF16)

    @part("cross_output_back")
    def _():
        for r in range(2):
            slow[256 * r:256 * r + 256] = dot(weight(r, 7), tlow[...], 0, 0).astype(BF16)
        square_grad(7, tlow[...], cctx[...].reshape(D, T))

    link.moment("cross_output_back")

    def scaled_grad(context, which, h):
        rows = pl.ds(pl.multiple_of(h * HD, HD), HD)
        g = (slow[rows, :].astype(F32) * inv[which, h]).astype(BF16)
        delta = jnp.sum(g.astype(F32) * context[h].astype(F32), axis=0, keepdims=True)
        return g, delta

    def grad_tile(ref, i, h, keys, at, g, e, dp, delta, first, last):
        q, k = ref[0, h, :, at], ref[1, h, :, 0:keys]
        ds = e * (dp - delta).astype(BF16)
        for n, part in ((0, dot(q, ds, 1, 1)), (1, dot(g, e, 1, 1))):
            acc[i, n, :, 0:keys] = part if first else acc[i, n, :, 0:keys] + part
        ref[0, h, :, at] = (dot(k, ds, 1, 0) * 0.125).astype(BF16)
        if last:
            ref[1, h] = acc[i, 0].astype(BF16)
            ref[2, h] = acc[i, 1].astype(BF16)

    @pl.loop(0, 4)
    def _(two):
        slots = [lax.rem(two, 2) * 2 + i for i in range(2)]
        for i in range(2):
            e_in(two * 2 + i, slots[i]).wait()

        @part("cross_back")
        def _():
            shared = [scaled_grad(cctx, 1, two * 2 + i) for i in range(2)]

            def product(i, j):
                return dot(pay[2, two * 2 + i], shared[i][0][:, 256 * j:256 * j + 256], 0, 0)

            def rest(i, j, dp):
                at = slice(256 * j, 256 * j + 256)
                g, delta = shared[i]
                grad_tile(
                    pay, i, two * 2 + i, T, at, g[:, at], ring[slots[i], :, at], dp, delta[:, at],
                    j == 0, j == 3,
                )

            ahead([(i, j) for i in range(2) for j in range(4)], 1, product, rest)

        @pl.when(two < 2)
        def _():
            for i in range(2):
                e_in(two * 2 + i + 4, slots[i]).start()

        @pl.when(two >= 2)
        def _():
            for slot in slots:
                own_in(slot).start()

        link.during_cross_back(two)

    @part("memory_grad")
    def _():
        for r in range(2):
            out = dot(weight(r, 5), grad_of(pay, 1), 0, 0) + dot(weight(r, 6), grad_of(pay, 2), 0, 0)
            gs[r] = out.T.astype(BF16)

    link.put_output(1)
    @part("cross_grads")
    def _():
        for r in range(2):
            half = slice(256 * r, 256 * r + 256)
            sg[half] = sg[half] + dot(weight(r, 4), grad_of(pay, 0), 0, 0)
        square_grad(4, grad_of(pay, 0), flow)
        square_grad(5, grad_of(pay, 1), mt)
        square_grad(6, grad_of(pay, 2), mt)

    link.moment("cross_grads")

    @part("inner_norm")
    def _():
        @pl.loop(0, 4)
        def _(tb):
            at = pl.ds(pl.multiple_of(tb * TB, TB), TB)
            inner = norm_back(sg[:, at], xh0[:, at], rstd[0, :, at], 0)
            add_col(6, inner * xt[:, at].astype(F32))
            sg[:, at] = param(6) * inner
            tlow[:, at] = inner.astype(BF16)

        for k in range(9):
            part = jnp.sum(cols[k], axis=1, keepdims=True)
            gcol[:, :, :, :, :, k:k + 1] = part.reshape(2, 4, 2, 2, 16, 1)

    link.moment("inner_norm")

    @part("self_output_back")
    def _():
        for r in range(2):
            slow[256 * r:256 * r + 256] = dot(weight(r, 3), tlow[...], 0, 0).astype(BF16)

    link.moment("self_output_back")

    @part("self_output_grad")
    def _():
        for r in range(2):
            right = ctx[...].reshape(D, T)[256 * r:256 * r + 256]
            part = dot(tlow[...], right, 1, 1).astype(BF16)
            wdn[r, :, :, :, 96:128, :] = part.reshape(4, 2, 2, 32, 256)

    @pl.loop(0, 4)
    def _(pair):
        own_in(pair).wait()
        @part("self_back")
        def _():
            shared = [scaled_grad(ctx, 0, pair * 2 + i) for i in range(2)]

            def product(i, j):
                at = slice(256 * j, 256 * j + 256)
                return dot(qkv[2, pair * 2 + i, :, 0:256 * (j + 1)], shared[i][0][:, at], 0, 0)

            def rest(i, j, dp):
                keys, at = 256 * (j + 1), slice(256 * j, 256 * j + 256)
                g, delta = shared[i]
                row, lane = self_tile(i, j)
                e = ring[pair, row:row + keys, lane:lane + 256]
                grad_tile(
                    qkv, i, pair * 2 + i, keys, at, g[:, at], e, dp, delta[:, at], j == 3, j == 0
                )

            ahead([(i, j) for i in range(2) for j in (3, 2, 1, 0)], 1, product, rest)

        @part("self_grads")
        def _():
            for m in range(3):
                grad = qkv[m, pl.ds(2 * pair, 2)].reshape(128, T)
                for r in range(2):
                    part = dot(grad, xt[256 * r:256 * r + 256], 1, 1).astype(BF16)
                    wdn[r, pair, :, :, 32 * m:32 * m + 32, :] = part.reshape(2, 2, 32, 256)

        link.during_self_back(pair)

    link.free_output(1)
    @part("tokens_grad")
    def _():
        for r in range(2):
            out = sg[256 * r:256 * r + 256]
            for m in range(3):
                out = out + dot(weight(r, m), grad_of(qkv, m), 0, 0)
            gs[r] = out.T.astype(BF16)

    link.put_output(2)
    link.finish()


def part(name):
    def run(section):
        with jax.named_scope(name):
            section()

    return run


class Alone:
    def __init__(self, inputs, outputs, weights, grads, buffers, sem):
        self.inputs, self.outputs, self.weights, self.grads = inputs, outputs, weights, grads
        self.xs, self.cs, self.gs, self.w8, self.wup, self.wdn = buffers
        self.sem = sem
        copy = pltpu.make_async_copy
        self.loads = [
            copy(inputs[0], self.xs.at[0], sem.at[0]),
            copy(inputs[1], self.xs.at[1], sem.at[1]),
            copy(inputs[2], self.cs, sem.at[2]),
            copy(self.squares(weights), self.w8, sem.at[3]),
            copy(weights.at[:, :, :, :, pl.ds(256, 128), :], self.wup, sem.at[4]),
            copy(weights.at[:, :, :, :, pl.ds(384, 128), :], self.wdn, sem.at[5]),
        ]
        self.stores = [
            copy(self.xs.at[0], outputs[0], sem.at[6]),
            copy(self.gs, outputs[1], sem.at[7]),
            copy(self.gs, outputs[2], sem.at[7]),
        ]

    def squares(self, ref):
        return ref.at[:, :, :, :, pl.ds(0, 256), :]

    def begin(self):
        for load in self.loads:
            load.start()

    def line(self, ref):
        return ref[0:1, :]

    def wait_input(self, i):
        self.loads[i].wait()

    def wait_weights(self, group):
        if group == 0:
            self.loads[3].wait()
        if group == 3:
            self.loads[4].wait()
        if group == 4:
            self.loads[5].wait()

    def gathered(self):
        pass

    def moment(self, name):
        down = pltpu.make_async_copy(
            self.wdn, self.grads.at[:, :, :, :, pl.ds(384, 128), :], self.sem.at[2]
        )
        if name == "feed_down_back":
            down.start()
        if name == "self_output_back":
            down.wait()

    def put_output(self, i):
        self.stores[i].start()

    def free_output(self, i):
        self.stores[i].wait()

    def during_self(self, pair):
        pass

    def during_cross(self, h):
        pass

    def during_cross_back(self, h):
        pass

    def during_self_back(self, pair):
        pass

    def finish(self):
        def grads(first, count):
            return self.grads.at[:, :, :, :, pl.ds(first, count), :]

        copies = [
            pltpu.make_async_copy(self.wdn, grads(0, 128), self.sem.at[0]),
            pltpu.make_async_copy(self.wup, grads(256, 128), self.sem.at[1]),
            pltpu.make_async_copy(
                self.w8.at[:, :, :, :, pl.ds(128, 128), :], grads(128, 128), self.sem.at[2]
            ),
        ]
        for copy in copies:
            copy.start()
        for copy in copies:
            copy.wait()
        self.stores[0].wait()
        self.stores[2].wait()


class Linked:
    def __init__(self, inputs, shards, params, outputs, gout, cout, buffers, landing, sems):
        self.inputs, self.shards, self.params = inputs, shards, params
        self.outputs, self.gout, self.cout = outputs, gout, cout
        self.xs, self.cs, self.gs, self.w8, self.wup, self.wdn, self.par, self.gcol = buffers
        self.land0, self.land1, self.land2, self.land3, self.plane_land, self.line_land = landing[:6]
        self.small = landing[6:]
        (self.isem, self.lsem, self.gsend, self.grecv, self.osem,
         self.rsend, self.rrecv, self.psend, self.precv) = sems
        r = lax.axis_index("row")
        col = lax.axis_index("col")
        z, y, x = col // 4, lax.rem(col // 2, 2), lax.rem(col, 2)
        self.r, self.z, self.y, self.x = r, z, y, x
        self.zs = [lax.rem(z + d, 4) for d in range(4)]
        self.partner = (1 - r, col)

        def chip(z, y, x):
            return (r, z * 4 + y * 2 + x)

        self.chip = chip
        self.across = {"x": chip(z, y, 1 - x), "y": chip(z, 1 - y, x)}
        self.along = [chip(self.zs[d], y, x) for d in (1, 2, 3)]
        self.others = [(y, 1 - x), (1 - y, x), (1 - y, 1 - x)]
        self.plane = [chip(z, *other) for other in self.others]
        self.peers = [self.partner, *self.plane, *self.along]
        self.holders = (
            (self.w8, 0, 96), (self.w8, 96, 128), (self.w8, 224, 32), (self.wup, 0, 128), (self.wdn, 0, 128)
        )

    def remote(self, source, target, send, recv, device):
        return pltpu.make_async_remote_copy(
            src_ref=source, dst_ref=target, send_sem=send, recv_sem=recv,
            device_id=device, device_id_type=pl.DeviceIdType.MESH,
        )


    def keep_in(self, i):
        place = (self.xs.at[0], self.xs.at[1], self.cs)[i]
        return pltpu.make_async_copy(self.inputs[i].at[self.r], place.at[self.r], self.lsem.at[i])

    def swap_in(self, i):
        place = (self.xs.at[0], self.xs.at[1], self.cs)[i]
        return self.remote(
            self.inputs[i].at[1 - self.r], place.at[self.r],
            self.isem.at[0, i], self.isem.at[1, i], self.partner,
        )

    def swap_par(self):
        place = self.par.at[self.r]
        return self.remote(place, place, self.isem.at[0, 3], self.isem.at[1, 3], self.partner)

    def keep_out(self, i):
        source = (self.xs.at[0], self.gs, self.gs)[i]
        return pltpu.make_async_copy(
            source.at[self.r], self.outputs[i].at[self.r], self.lsem.at[3 + i]
        )

    def swap_out(self, i):
        source = (self.xs.at[0], self.gs, self.gs)[i]
        return self.remote(
            source.at[1 - self.r], self.outputs[i].at[self.r],
            self.osem.at[0, i], self.osem.at[1, i], self.partner,
        )


    def gathers(self, group, step):
        ref, first, count = self.holders[group]
        r, z, y, x = self.r, self.z, self.y, self.x

        def move(place, at, half, device):
            piece = ref.at[place]
            return self.remote(
                piece, piece, self.gsend.at[group, half, at], self.grecv.at[group, half, at], device
            )

        if group < 2:
            rows = pl.ds(first, count)
            back = [z] + [self.zs[4 - d] for d in (1, 2, 3)]
            every = slice(None)
            if step == 0:
                order = (0, 2, 1)
                return [move((r, z, y, x, rows), d, 0, self.along[d]) for d in order] + [
                    move((r, z, y, x, rows), 3 + k, 0, self.plane[k]) for k in range(3)
                ]
            if step < 4:
                return [move((r, back[step], y, x, rows), 3 + 3 * step + k, 0, self.plane[k]) for k in range(3)]
            d = step - 4
            return [move((r, back[d], every, every, rows), 15 + d, 0, self.partner)]
        copies = []
        for half in range(2):
            rows = pl.ds(first + half * (count // 2), count // 2)
            every = slice(None)
            own = (r, z, y, x, rows)
            line = (r, every, y, x, rows)
            sheet = (r, every, every, x, rows) if half == 0 else (r, every, y, every, rows)
            axes = ("y", "x") if half == 0 else ("x", "y")
            if step == 0:
                copies += [move(own, d, half, self.along[d]) for d in range(3)]
            elif step == 3:
                copies.append(move((r, every, every, every, rows), 5, half, self.partner))
            else:
                place = line if step == 1 else sheet
                copies.append(move(place, 2 + step, half, self.across[axes[step - 1]]))
        return copies

    def start(self, group, step):
        for copy in self.gathers(group, step):
            copy.start()

    def wait(self, group, step):
        for copy in self.gathers(group, step):
            copy.wait_recv()

    def gather(self, group, step):
        self.wait(group, step - 1)
        self.start(group, step)

    def forward(self, group, d):
        self.gathers(group, 0)[(0, 2, 1).index(d - 1)].wait_recv()
        self.start(group, d)

    def share(self, group, d):
        if d == 0:
            for copy in self.gathers(group, 0)[3:]:
                copy.wait_recv()
        else:
            self.wait(group, d)
        self.start(group, 4 + d)

    def begin(self):
        r, z, y, x = self.r, self.z, self.y, self.x
        for i in range(3):
            self.keep_in(i).start()
        for m in range(8):
            self.w8[r, z, y, x, 32 * m:32 * m + 32, :] = self.shards[m][...]
        self.wup[r, z, y, x] = self.shards[8][...].T
        for s in range(4):
            self.wdn[r, z, y, x, 32 * s:32 * s + 32, :] = self.shards[9][:, 256 * s:256 * s + 256]
        for k in range(3):
            self.par[r, 3 * k:3 * k + 3, :] = self.params[k][...]
        barrier = pltpu.get_barrier_semaphore()
        for peer in self.peers:
            pl.semaphore_signal(barrier, inc=1, device_id=peer, device_id_type=pl.DeviceIdType.MESH)
        pl.semaphore_wait(barrier, len(self.peers))
        self.start(0, 0)
        self.swap_in(0).start()
        self.swap_par().start()
        self.swap_in(1).start()
        self.swap_in(2).start()

    def line(self, ref):
        return ref[pl.ds(self.r, 1), :]

    def wait_input(self, i):
        self.keep_in(i).wait()
        self.swap_in(i).wait_recv()
        if i == 1:
            self.swap_par().wait_recv()

    def wait_weights(self, group):
        if group < 2:
            for d in range(4):
                self.wait(group, 4 + d)
        else:
            self.wait(group, 3)

    def gathered(self):
        for group in range(5):
            for step in range(8 if group < 2 else 4):
                for copy in self.gathers(group, step):
                    copy.wait_send()


    def sums(self, group, step):
        r, z, y, x = self.r, self.z, self.y, self.x
        send, recv = self.rsend.at[group], self.rrecv.at[group]
        every = slice(None)
        if group == 3:
            ref = self.gcol
            if step == 0:
                return [self.remote(ref.at[1 - r], self.small[0], send.at[0], recv.at[0], self.partner)]
            if step == 1:
                source = ref.at[r, :, :, 1 - x]
                return [self.remote(source, self.small[1], send.at[1], recv.at[1], self.across["x"])]
            if step == 2:
                source = ref.at[r, :, 1 - y, x]
                return [self.remote(source, self.small[2], send.at[2], recv.at[2], self.across["y"])]
            return [
                self.remote(
                    ref.at[r, self.zs[d + 1], y, x], self.small[3].at[d],
                    send.at[3 + d], recv.at[3 + d], self.along[d],
                )
                for d in range(3)
            ]
        ref, at = self.summed(group)
        if step == 0:
            source = ref.at[1 - r, :, :, :, pl.ds(at, 128)]
            return [self.remote(source, self.land0.at[group], send.at[0], recv.at[0], self.partner)]
        copies = []
        for half in range(2):
            rows = pl.ds(at + 64 * half, 64)
            axes = ("x", "y") if half == 0 else ("y", "x")
            k = 1 + 5 * half
            if step == 1:
                place = (r, every, every, 1 - x, rows) if half == 0 else (r, every, 1 - y, every, rows)
                target, device = self.land1.at[group, half], self.across[axes[0]]
                copies.append(self.remote(ref.at[place], target, send.at[k], recv.at[k], device))
            elif step == 2:
                place = (r, every, 1 - y, x, rows) if half == 0 else (r, every, y, 1 - x, rows)
                target, device = self.land2.at[group, half], self.across[axes[1]]
                copies.append(self.remote(ref.at[place], target, send.at[k + 1], recv.at[k + 1], device))
            else:
                for d in range(3):
                    copies.append(self.remote(
                        ref.at[r, self.zs[d + 1], y, x, rows], self.land3.at[group, half, d],
                        send.at[k + 2 + d], recv.at[k + 2 + d], self.along[d],
                    ))
        return copies

    def summed(self, group):
        return ((self.wdn, 0), (self.wup, 0), (self.w8, 128))[group]

    def reduce(self, group, step):
        r, z, y, x = self.r, self.z, self.y, self.x
        every = slice(None)
        if step > 0:
            for copy in self.sums(group, step - 1):
                copy.wait_recv()
        if group == 3:
            ref = self.gcol
            if step == 1:
                ref[r] = ref[r] + self.small[0][...]
            elif step == 2:
                ref[r, :, :, x] = ref[r, :, :, x] + self.small[1][...]
            elif step == 3:
                ref[r, :, y, x] = ref[r, :, y, x] + self.small[2][...]
            elif step == 4:
                total = ref[r, z, y, x]
                for d in range(3):
                    total = total + self.small[3][d]
                self.cout[...] = total
        elif step > 0:
            ref, at = self.summed(group)

            def add(place, value):
                ref[place] = (ref[place].astype(F32) + value.astype(F32)).astype(BF16)

            if step == 1:
                for k in range(4):
                    add((r, k, every, every, slice(at, at + 128)), self.land0[group, k])
            for half in range(2):
                rows = slice(at + 64 * half, at + 64 * half + 64)
                if step == 2 and half == 0:
                    add((r, every, every, x, rows), self.land1[group, half])
                elif step == 2:
                    add((r, every, y, every, rows), self.land1[group, half])
                elif step == 3:
                    add((r, every, y, x, rows), self.land2[group, half])
                elif step == 4:
                    total = ref[r, z, y, x, rows].astype(F32)
                    for d in range(3):
                        total = total + self.land3[group, half, d].astype(F32)
                    self.gout[group, 64 * half:64 * half + 64] = total
        if step < 4:
            for copy in self.sums(group, step):
                copy.start()
        elif group == 0:
            for step in range(4):
                for copy in self.sums(group, step):
                    copy.wait_send()


    def plane_sums(self, p, step):
        r, z, y, x = self.r, self.z, self.y, self.x
        ref = self.wdn
        send, recv = self.psend.at[p], self.precv.at[p]
        if step == 0:
            return [self.remote(ref.at[1 - r, p], self.land0.at[3, p], send.at[0], recv.at[0], self.partner)]
        if step == 1:
            return [
                self.remote(
                    ref.at[r, p, to_y, to_x], self.plane_land.at[p, k],
                    send.at[1 + k], recv.at[1 + k], self.plane[k],
                )
                for k, (to_y, to_x) in enumerate(self.others)
            ]
        d = lax.rem(p - z + 4, 4)
        place = jnp.maximum(d - 1, 0)
        return [self.remote(
            ref.at[r, p, y, x], self.line_land.at[place],
            send.at[4], self.precv.at[4, place], self.chip(p, y, x),
        )]

    def reduce_plane(self, p, step):
        r, z, y, x = self.r, self.z, self.y, self.x
        ref = self.wdn
        if step > 0:
            for copy in self.plane_sums(p, step - 1):
                copy.wait_recv()
        if step == 1:
            for k in range(2):
                total = ref[r, p, k].astype(F32) + self.land0[3, p, k].astype(F32)
                ref[r, p, k] = total.astype(BF16)
        if step == 2:
            total = ref[r, p, y, x].astype(F32)
            for k in range(3):
                total = total + self.plane_land[p, k].astype(F32)
            ref[r, p, y, x] = total.astype(BF16)

            @pl.when(z != p)
            def _():
                self.plane_sums(p, 2)[0].start()
        else:
            for copy in self.plane_sums(p, step):
                copy.start()

    def end_planes(self):
        r, z, y, x = self.r, self.z, self.y, self.x
        total = self.wdn[r, z, y, x].astype(F32)
        for d in range(3):
            place = self.line_land.at[d]
            self.remote(
                place, place, self.psend.at[4, d], self.precv.at[4, d], self.along[d]
            ).wait_recv()
            total = total + self.line_land[d].astype(F32)
        self.gout[3] = total
        for p in range(4):
            for step in range(2):
                for copy in self.plane_sums(p, step):
                    copy.wait_send()

            @pl.when(z != p)
            def _():
                self.plane_sums(p, 2)[0].wait_send()


    def moment(self, name):
        if name == "turn_tokens":
            self.forward(0, 1)
            self.start(1, 0)
        elif name == "turn_memory":
            self.forward(0, 3)
            self.forward(0, 2)
        elif name == "mask":
            for d in (0, 1, 3, 2):
                self.share(0, d)
            for d in (1, 3, 2):
                self.forward(1, d)
        elif name == "half_feed_up":
            self.gather(4, 3)
        elif name == "feed_down_back":
            self.reduce(0, 0)
        elif name == "feed_up_grad":
            self.reduce(0, 1)
            self.reduce(1, 0)
        elif name == "cross_output_back":
            self.reduce(1, 1)
        elif name == "cross_grads":
            self.reduce(2, 0)
            self.reduce(1, 3)
        elif name == "inner_norm":
            self.reduce(3, 0)
            self.reduce(2, 1)
        elif name == "self_output_back":
            self.reduce(0, 4)

    def at_turn(self, index, turns):
        for turn, actions in turns.items():

            @pl.when(index == turn)
            def _():
                for move, *where in actions:
                    move(*where)

    def during_self(self, pair):
        self.at_turn(pair, {
            0: [(self.start, 2, 0), (self.start, 3, 0)],
            1: [(self.share, 1, 0), (self.start, 4, 0)],
            2: [(self.share, 1, 1), (self.share, 1, 3)],
            3: [(self.gather, 2, 1), (self.share, 1, 2), (self.gather, 3, 1), (self.gather, 2, 2)],
        })

    def during_cross(self, two):
        self.at_turn(two, {
            0: [(self.gather, 4, 1), (self.gather, 2, 3), (self.gather, 3, 2)],
            2: [(self.gather, 4, 2)],
            3: [(self.gather, 3, 3)],
        })

    def during_cross_back(self, two):
        self.at_turn(two, {
            1: [(self.reduce, 0, 2)],
            2: [(self.reduce, 1, 2)],
            3: [(self.reduce, 0, 3)],
        })

    def during_self_back(self, pair):
        @pl.when(pair >= 2)
        def _():
            self.reduce_plane(pair - 2, 2)

        @pl.when(pair >= 1)
        def _():
            self.reduce_plane(pair - 1, 1)

        self.reduce_plane(pair, 0)
        self.at_turn(pair, {
            0: [(self.reduce, 3, 1)],
            1: [(self.reduce, 1, 4)],
            2: [(self.reduce, 2, 2), (self.reduce, 3, 2)],
        })

    def put_output(self, i):
        self.keep_out(i).start()
        self.swap_out(i).start()

    def free_output(self, i):
        self.reduce_plane(2, 2)
        self.reduce_plane(3, 1)
        self.reduce(2, 3)
        self.reduce(3, 3)
        self.keep_out(i).wait()
        self.swap_out(i).wait_send()

    def finish(self):
        self.reduce_plane(3, 2)
        self.reduce(2, 4)
        self.reduce(3, 4)
        self.end_planes()
        for group in range(1, 4):
            for step in range(4):
                for copy in self.sums(group, step):
                    copy.wait_send()
        for i in range(3):
            self.swap_in(i).wait_send()
        self.swap_par().wait_send()
        for i in (0, 2):
            self.keep_out(i).wait()
            self.swap_out(i).wait_send()
        for i in range(3):
            self.swap_out(i).wait_recv()


CHIPS = 16


def to_sixteen(w):
    n = w.shape[1]
    if n == CHIPS:
        return w
    part = D // n

    def spread(block):
        block = block.reshape(2, n, -1, part, 256).swapaxes(1, 2).reshape(2, -1, CHIPS, 32, 256)
        return block.swapaxes(1, 2).reshape(2, CHIPS, -1, 256)

    return jnp.concatenate(
        [
            spread(w[:, :, :8 * part]),
            w[:, :, 8 * part:12 * part].reshape(2, CHIPS, 128, 256),
            spread(w[:, :, 12 * part:]),
        ],
        axis=2,
    )


def from_sixteen(g, n):
    if n == CHIPS:
        return g
    part = D // n

    def gather(block):
        block = block.reshape(2, CHIPS, -1, 32, 256).swapaxes(1, 2).reshape(2, -1, n, part, 256)
        return block.swapaxes(1, 2).reshape(2, n, -1, 256)

    return jnp.concatenate(
        [
            gather(g[:, :, :256]),
            g[:, :, 256:384].reshape(2, n, 4 * part, 256),
            gather(g[:, :, 384:]),
        ],
        axis=2,
    )


ANY = pl.BlockSpec(memory_space=pl.ANY)
VMEM = pl.BlockSpec(memory_space=pltpu.VMEM)
SHAPE = jax.ShapeDtypeStruct
STASH = [SHAPE((H, T, T), BF16), SHAPE((4, T, 1280), BF16)]


def layer_scratch():
    V = pltpu.VMEM
    return [
        V((2, 2, T, 256), BF16), V((2, T, 256), BF16),
        V((D, T), BF16), V((D, T), BF16),
        V((2, 4, 2, 2, 256, 256), BF16),
        V((2, 4, 2, 2, 128, 256), BF16), V((2, 4, 2, 2, 128, 256), BF16),
        V((3, H, HD, T), BF16), V((3, H, HD, T), BF16),
        V((H, HD, T), BF16), V((H, HD, T), BF16),
        V((2, H, 1, T), F32),
        V((D, T), F32), V((D, T), F32), V((2, 1, T), F32),
        V((D, T), BF16), V((D, T), BF16), V((D, T), BF16),
        V((4, T, 1280), BF16),
        V((D, T), F32), V((2, T, 256), BF16),
        V((D, 128), F32), V((9, D, 128), F32),
        V((2, 2, HD, T), F32),
        pltpu.SemaphoreType.DMA((4,)),
    ]


def run_alone(x, mem, cot, w, par, seg, pad):
    def kernel(x, mem, cot, w, par, seg, pad, lo, mg, tg, g, e, es, gcol, *rest):
        scratch, sem = rest[:-1], rest[-1]
        xs, cs, gs = scratch[0], scratch[1], scratch[20]
        link = Alone(
            (x, mem, cot), (lo, mg, tg), w, g, (xs, cs, gs, scratch[4], scratch[5], scratch[6]), sem
        )
        layer(link, e, es, par, seg, pad, *scratch[:-1], gcol, scratch[-1])

    wide = SHAPE((2, T, 256), BF16)
    return pl.pallas_call(
        kernel,
        in_specs=[ANY] * 4 + [VMEM] * 3,
        out_specs=[ANY] * 6 + [VMEM],
        out_shape=[wide] * 3
        + [SHAPE((2, 4, 2, 2, 512, 256), BF16), *STASH, SHAPE((2, 4, 2, 2, 16, 128), F32)],
        scratch_shapes=layer_scratch() + [pltpu.SemaphoreType.DMA((8,))],
        compiler_params=pltpu.CompilerParams(vmem_limit_bytes=63 * 2**20),
        name="layer",
    )(x, mem, cot, w, par, seg, pad)


def run_linked(inputs, shards, params, seg, pad):
    def kernel(*refs):
        inputs, shards, params, seg, pad = refs[0:3], refs[3:13], refs[13:16], refs[16], refs[17]
        outputs, e, es, gout, cout = refs[18:21], refs[21], refs[22], refs[23], refs[24]
        scratch = refs[25:25 + 25]
        par, gcol = refs[50], refs[51]
        landing, sems = refs[52:62], refs[62:]
        xs, cs, gs = scratch[0], scratch[1], scratch[20]
        link = Linked(
            inputs, shards, params, outputs, gout, cout,
            (xs, cs, gs, scratch[4], scratch[5], scratch[6], par, gcol), landing, sems,
        )
        layer(link, e, es, par, seg, pad, *scratch[:-1], gcol, scratch[-1])

    V = pltpu.VMEM
    DMA = pltpu.SemaphoreType.DMA
    wide = SHAPE((2, T, 256), BF16)
    return pl.pallas_call(
        kernel,
        in_specs=[ANY] * 3 + [VMEM] * 15,
        out_specs=[ANY] * 5 + [VMEM] * 2,
        out_shape=[wide] * 3 + STASH + [SHAPE((4, 128, 256), F32), SHAPE((16, 128), F32)],
        scratch_shapes=layer_scratch() + [
            V((2, 16, 256), F32), V((2, 4, 2, 2, 16, 128), F32),
            V((4, 4, 2, 2, 128, 256), BF16), V((3, 2, 4, 2, 64, 256), BF16),
            V((3, 2, 4, 64, 256), BF16), V((3, 2, 3, 64, 256), BF16),
            V((4, 3, 128, 256), BF16), V((3, 128, 256), BF16),
            V((4, 2, 2, 16, 128), F32), V((4, 2, 16, 128), F32),
            V((4, 16, 128), F32), V((3, 16, 128), F32),
            DMA((2, 4)), DMA((6,)), DMA((5, 2, 19)), DMA((5, 2, 19)), DMA((2, 3)),
            DMA((4, 11)), DMA((4, 11)), DMA((5, 5)), DMA((5, 5)),
        ],
        compiler_params=pltpu.CompilerParams(
            vmem_limit_bytes=63 * 2**20, collective_id=0, has_side_effects=True
        ),
        name="layer",
    )(*inputs, *shards, *params, seg, pad)


def ending(lo, mg, tg, gout, cout):
    def kernel(lo, mg, tg, gout, cout, lo_out, tg_out, mg_out, *rest):
        lo_out[...] = lo[...]
        mg_out[...] = mg[...].astype(F32)
        tg_out[...] = tg[...].astype(F32)

        @pl.when(pl.program_id(0) == 0)
        def _():
            for m in range(8):
                at = 32 * (m % 4)
                rest[m][...] = gout[3 if m < 4 else 2, at:at + 32, :]
            rest[8][...] = gout[1].T
            for s in range(4):
                rest[9][:, 256 * s:256 * s + 256] = gout[0, 32 * s:32 * s + 32, :]
            small = cout[...].T
            for k in range(3):
                rest[10 + k][...] = small[3 * k:3 * k + 3, :]

    part = pl.BlockSpec((1, 512, 256), lambda i: (i // 2, i % 2, 0))

    def whole(*shape):
        return pl.BlockSpec(shape, lambda i: (0,) * len(shape))

    shapes = [(32, 256)] * 8 + [(256, 128), (32, 1024)] + [(3, 16)] * 3
    return pl.pallas_call(
        kernel,
        grid=(4,),
        in_specs=[part] * 3 + [whole(4, 128, 256), whole(16, 128)],
        out_specs=[part] * 3 + [whole(*one) for one in shapes],
        out_shape=[SHAPE((2, T, 256), BF16), SHAPE((2, T, 256), F32), SHAPE((2, T, 256), F32)]
        + [SHAPE(one, F32) for one in shapes],
        name="ending",
    )(lo, mg, tg, gout, cout)


def body(
    tokens, memory, cotangent, segments, padding,
    self_query, self_key, self_value, self_output,
    cross_query, cross_key, cross_value, cross_output,
    feed_up, feed_down, norm_gain, norm_bias, omegas,
):
    n = lax.axis_size("col")
    squares = (
        self_query, self_key, self_value, self_output,
        cross_query, cross_key, cross_value, cross_output,
    )
    if n == CHIPS:
        lo, mg, tg, _, _, gout, cout = run_linked(
            (tokens, memory, cotangent), (*[m.T for m in squares], feed_up, feed_down.T),
            (norm_gain, norm_bias, omegas), segments, padding,
        )
        out = ending(lo, mg, tg, gout, cout)
        turned = [one.T for one in out[3:11]]
        return (*out[0:3], *turned, out[11], out[12].T, *out[13:16])
    row = lax.axis_index("row")
    part = D // n
    blob = jnp.concatenate(
        [m.T for m in squares]
        + [feed_up.T]
        + [feed_down.T[:, 256 * s:256 * s + 256] for s in range(4)],
        axis=0,
    )
    w = lax.all_gather(blob, ("row", "col"), axis=0, tiled=False).reshape(2, n, 16 * part, 256)
    w = to_sixteen(w).reshape(2, 4, 2, 2, 512, 256)
    par = jnp.concatenate([norm_gain, norm_bias, omegas, jnp.zeros((7, 256), F32)], axis=0)
    par = lax.all_gather(par, "row", axis=0, tiled=False)

    def mine(array):
        return lax.all_to_all(array, "row", split_axis=0, concat_axis=0, tiled=True)

    seg = lax.dynamic_slice_in_dim(segments, row, 1, 0)
    pad = lax.dynamic_slice_in_dim(padding, row, 1, 0)
    lo, mg, tg, g, _, _, gcol = run_alone(
        mine(tokens), mine(memory), mine(cotangent), w, par, seg, pad
    )
    lo, tg, mg = mine(lo), mine(tg).astype(F32), mine(mg).astype(F32)
    g = from_sixteen(g.reshape(2, CHIPS, 512, 256), n).reshape(2 * n, 16 * part, 256)
    g = lax.psum_scatter(g.astype(F32), ("row", "col"), scatter_dimension=0, tiled=False)
    gcol = lax.psum_scatter(
        gcol.reshape(2 * n, part // 2, 128), ("row", "col"), scatter_dimension=0, tiled=False
    )
    small = gcol[:, 0:9].T
    last = 12 * part
    return (
        lo, tg, mg,
        *[g[part * m:part * m + part].T for m in range(8)],
        g[8 * part:last].T,
        jnp.concatenate([g[last + part * s:last + part * s + part].T for s in range(4)], axis=0),
        small[0:3], small[3:6], small[6:9],
    )


def solution(mesh):
    wide = P(None, "col", "row")
    square = P("row", "col")
    return jax.shard_map(
        body,
        mesh=mesh,
        in_specs=(wide,) * 3 + (P(None, "col"),) * 2 + (square,) * 10 + (P(None, "row"),) * 3,
        out_specs=(wide,) * 3 + (square,) * 10 + (P(None, ("row", "col")),) * 3,
        check_vma=False,
    )
```

```python
import jax
import jax.numpy as jnp
from jax import lax
from jax.experimental import pallas as pl
from jax.experimental.pallas import tpu as pltpu
from jax.sharding import PartitionSpec as P

F32 = jnp.float32
BF16 = jnp.bfloat16
EPSILON = 1e-05
MASKED = -1e30
T = 1024
D = 512
H = 8
HD = 64
TB = 256


def dot(left, right, left_dim, right_dim):
    return lax.dot_general(
        left, right, (((left_dim,), (right_dim,)), ((), ())), preferred_element_type=F32
    )


SLOTS = (0, 1, 2, 3, 5, 6, 4, 7)


def gelu_both(v):
    root = 0.7978845608028654
    square = v * v
    t = jnp.tanh(root * v * (1.0 + 0.044715 * square))
    half = 0.5 * (1.0 + t)
    slope = half + (0.5 * root) * v * (1.0 - t * t) * (1.0 + (3.0 * 0.044715) * square)
    return v * half, slope


def layer(
    link, e_hbm, es_hbm, par, seg, pad,
    xs, cs, xt, mt, w8, wup, wdn, qkv, pay, ctx, cctx, inv, xh0, xh1, rstd,
    flow, slow, tlow, ring, sg, gs, pcol, cols, acc, gcol, esem,
):
    def weight(r, m):
        at = 32 * SLOTS.index(m)
        return w8[r, :, :, :, at:at + 32, :].reshape(D, 256)

    def forward(m, source):
        return dot(weight(0, m), source[0:256], 1, 0) + dot(weight(1, m), source[256:512], 1, 0)

    def param(k):
        return pcol[:, k:k + 1]

    def grad_of(ref, i):
        return ref[i].reshape(D, T)

    def add_col(k, value):
        cols[k] = cols[k] + (value[:, 0:128] + value[:, 128:256])

    link.begin()
    cols[...] = jnp.zeros_like(cols)
    link.wait_input(0)
    @part("turn_tokens")
    def _():
        for r in range(2):
            xt[256 * r:256 * r + 256] = xs[0, r].T

    link.moment("turn_tokens")
    link.wait_input(1)
    @part("turn_memory")
    def _():
        for r in range(2):
            mt[256 * r:256 * r + 256] = xs[1, r].T

    link.moment("turn_memory")
    pcol[...] = jnp.zeros_like(pcol)
    for r in range(2):
        pcol[256 * r:256 * r + 256, 0:16] = par[r].T

    @part("mask")
    def _():
        padlen = jnp.sum(link.line(pad), axis=1, keepdims=True)
        for j in range(4):
            low = link.line(seg)[:, 256 * j:256 * j + 256]
            here = 256 * j + lax.broadcasted_iota(jnp.int32, (1, 256), 1)
            high = jnp.minimum(here, padlen - 1)
            rows = lax.broadcasted_iota(jnp.int32, (T, 256), 0)
            fits = ((rows >= low) & (rows <= high)) | (rows == here)
            xs[j // 2, j % 2] = jnp.where(fits, 0.0, MASKED).astype(BF16)

    link.moment("mask")
    ones = jnp.ones((16, T), BF16)

    def weighted(scores, v):
        top = jnp.max(scores, axis=0, keepdims=True)
        e = jnp.exp(scores - top).astype(BF16)
        both = dot(v, e, 1, 0)
        inverse = 1.0 / both[HD:HD + 1]
        return e, (both[0:HD] * inverse).astype(BF16), inverse

    def ahead(tiles, depth, product, rest):
        products = [product(*tile) for tile in tiles[:depth]]
        for n, tile in enumerate(tiles):
            if n + depth < len(tiles):
                products.append(product(*tiles[n + depth]))
            rest(*tile, products[n])

    def self_tile(i, j):
        if j == 3:
            return 0, 256 * i
        if j == 1:
            return 512 * i, 1024
        return (0 if j == 0 else 256), 512 + 256 * i

    def own_out(pair):
        return pltpu.make_async_copy(ring.at[pair], es_hbm.at[pair], esem.at[pair])

    def own_in(pair):
        return pltpu.make_async_copy(es_hbm.at[pair], ring.at[pair], esem.at[pair])

    def e_out(h, slot):
        return pltpu.make_async_copy(ring.at[slot, :, pl.ds(0, T)], e_hbm.at[h], esem.at[slot])

    def e_in(h, slot):
        return pltpu.make_async_copy(e_hbm.at[h], ring.at[slot, :, pl.ds(0, T)], esem.at[slot])

    @pl.loop(0, 4)
    def _(turn):
        pair = link.pair_of(turn)
        link.before_self(turn)

        @part("self_projections")
        def _():
            left = [w8[r, pair, :, :, 0:96, :].reshape(384, 256) for r in range(2)]
            out = dot(left[0], xt[0:256], 1, 0) + dot(left[1], xt[256:512], 1, 0)
            for n in range(12):
                block = out[32 * n:32 * n + 32]
                if n % 3 == 0:
                    block = block * 0.125
                half = n // 3 % 2
                qkv[n % 3, pair * 2 + n // 6, 32 * half:32 * half + 32, :] = block.astype(BF16)

        link.amid_self(turn)

        @part("self_attention")
        def _():
            values = [jnp.concatenate([qkv[2, pair * 2 + i], ones], axis=0) for i in range(2)]

            def product(i, j):
                h, keys = pair * 2 + i, 256 * (j + 1)
                scores = dot(qkv[1, h, :, 0:keys], qkv[0, h, :, 256 * j:256 * j + 256], 0, 0)
                return scores + xs[j // 2, j % 2, 0:keys, :].astype(F32)

            def rest(i, j, scores):
                h, keys, at = pair * 2 + i, 256 * (j + 1), slice(256 * j, 256 * j + 256)
                e, out, inverse = weighted(scores, values[i][:, 0:keys])
                row, lane = self_tile(i, j)
                ring[pair, row:row + keys, lane:lane + 256] = e
                ctx[h, :, at] = out
                inv[0, h, :, at] = inverse

            ahead([(i, j) for j in range(4) for i in range(2)], 2, product, rest)

        own_out(pair).start()
        link.during_self(turn)

    link.wait_weights(1)
    @part("memory_projections")
    def _():
        for m in (5, 6):
            pay[m - 4] = forward(m, mt).astype(BF16).reshape(H, HD, T)

    link.moment("memory_projections")

    def norm(total):
        average = jnp.mean(total, axis=0, keepdims=True)
        centred = total - average
        factor = lax.rsqrt(jnp.mean(centred * centred, axis=0, keepdims=True) + EPSILON)
        return centred * factor, factor

    @part("first_norm")
    def _():
        @pl.loop(0, 4)
        def _(tb):
            at = pl.ds(pl.multiple_of(tb * TB, TB), TB)
            out = forward(3, ctx[:, :, at].reshape(D, TB))
            normed, factor = norm(param(6) * xt[:, at].astype(F32) + out)
            xh0[:, at] = normed
            rstd[0, :, at] = factor
            flow[:, at] = (normed * param(0) + param(3)).astype(BF16)

    link.moment("first_norm")
    link.wait_weights(2)

    @part("probes")
    def _():
        pay[0] = (forward(4, flow) * 0.125).astype(BF16).reshape(H, HD, T)

    link.moment("probes")

    @pl.loop(0, 4)
    def _(two):
        slots = [lax.rem(two, 2) * 2 + i for i in range(2)]

        @pl.when(two < 2)
        def _():
            for slot in slots:
                own_out(slot).wait()

        @pl.when(two >= 2)
        def _():
            for slot in slots:
                e_out(slot, slot).wait()

        @part("cross_attention")
        def _():
            values = [jnp.concatenate([pay[2, two * 2 + i], ones], axis=0) for i in range(2)]

            def product(i, j):
                h = two * 2 + i
                return dot(pay[1, h], pay[0, h, :, 512 * j:512 * j + 512], 0, 0)

            def rest(i, j, scores):
                h, at = two * 2 + i, slice(512 * j, 512 * j + 512)
                e, out, inverse = weighted(scores, values[i])
                ring[slots[i], :, at] = e
                cctx[h, :, at] = out
                inv[1, h, :, at] = inverse

            ahead([(i, j) for i in range(2) for j in range(2)], 2, product, rest)

        for i in range(2):
            e_out(two * 2 + i, slots[i]).start()
        link.during_cross(two)

    link.wait_weights(3)

    @part("second_norm")
    def _():
        @pl.loop(0, 4)
        def _(tb):
            at = pl.ds(pl.multiple_of(tb * TB, TB), TB)
            out = forward(7, cctx[:, :, at].reshape(D, TB))
            first = xh0[:, at] * param(0) + param(3)
            normed, factor = norm(param(7) * first + out)
            xh1[:, at] = normed
            rstd[1, :, at] = factor
            slow[:, at] = (normed * param(1) + param(4)).astype(BF16)

    for slot in range(4):
        e_out(4 + slot, slot).wait()
    link.wait_weights(4)
    link.wait_input(2)

    def up(r, b):
        return wup[r, b].reshape(512, 256)

    def down(b):
        return wdn[b // 4, :, :, :, 32 * (b % 4):32 * (b % 4) + 32, :].reshape(D, 256)

    for part_of_two in range(2):

        @part("feed_up")
        def _():
            for b in (2 * part_of_two, 2 * part_of_two + 1):
                place = slice(512 * (b % 2), 512 * (b % 2) + 512)
                for t in range(2):
                    at = slice(512 * t, 512 * t + 512)
                    v = dot(up(0, b), slow[0:256, at], 1, 0) + dot(up(1, b), slow[256:512, at], 1, 0)
                    value, slope = gelu_both(v)
                    ring[b // 2, place, at] = value.astype(BF16)
                    ring[2 + b // 2, place, at] = slope.astype(BF16)

        if part_of_two == 0:
            link.moment("half_feed_up")

    link.wait_weights(5)

    def norm_back(upstream, normed, factor, k):
        scaled = upstream * param(k)
        one = jnp.mean(scaled, axis=0, keepdims=True)
        two = jnp.mean(scaled * normed, axis=0, keepdims=True)
        add_col(k, upstream * normed)
        add_col(3 + k, upstream)
        return factor * (scaled - one - normed * two)

    @part("feed_down")
    def _():
        @pl.loop(0, 4)
        def _(tb):
            at = pl.ds(pl.multiple_of(tb * TB, TB), TB)
            out = None
            for b in range(8):
                part = dot(down(b), ring[b // 4, 256 * (b % 4):256 * (b % 4) + 256, at], 1, 0)
                out = part if out is None else out + part
            second = xh1[:, at] * param(1) + param(4)
            normed, factor = norm(param(8) * second + out)
            final = (normed * param(2) + param(5)).astype(BF16)
            upstream = jnp.concatenate([cs[0, at, :].T, cs[1, at, :].T], axis=0).astype(F32)
            for r in range(2):
                xs[0, r, at, :] = final[256 * r:256 * r + 256].T
            third = norm_back(upstream, normed, factor, 2)
            add_col(8, third * second)
            sg[:, at] = param(8) * third
            tlow[:, at] = third.astype(BF16)

    link.put_output(0)

    def square_grad(m, left, right):
        for r in range(2):
            part = dot(left, right[256 * r:256 * r + 256], 1, 1).astype(BF16)
            at = 32 * SLOTS.index(m)
            w8[r, :, :, :, at:at + 32, :] = part.reshape(4, 2, 2, 32, 256)

    link.gathered()
    @part("feed_down_back")
    def _():
        for f in range(8):
            rows = slice(256 * (f % 4), 256 * (f % 4) + 256)
            grad = dot(down(f), tlow[...], 0, 0) * ring[2 + f // 4, rows, 0:T].astype(F32)
            part = dot(tlow[...], ring[f // 4, rows, 0:T], 1, 1).astype(BF16)
            wdn[f // 4, :, :, :, 32 * (f % 4):32 * (f % 4) + 32, :] = part.reshape(4, 2, 2, 32, 256)
            ring[2 + f // 4, rows, 0:T] = grad.astype(BF16)

    link.moment("feed_down_back")
    @part("second_grad")
    def _():
        for r in range(2):
            half = slice(256 * r, 256 * r + 256)
            for t in range(2):
                at = slice(512 * t, 512 * t + 512)
                part = None
                for b in range(4):
                    place = slice(512 * (b % 2), 512 * (b % 2) + 512)
                    one = dot(up(r, b), ring[2 + b // 2, place, at], 0, 0)
                    part = one if part is None else part + one
                sg[half, at] = sg[half, at] + part

    @part("feed_up_grad")
    def _():
        for b in range(4):
            grad = ring[2 + b // 2, 512 * (b % 2):512 * (b % 2) + 512, 0:T]
            for r in range(2):
                part = dot(grad, slow[256 * r:256 * r + 256], 1, 1).astype(BF16)
                wup[r, b] = part.reshape(2, 2, 128, 256)

    link.moment("feed_up_grad")

    for slot in range(4):
        e_in(slot, slot).start()

    @part("middle_norm")
    def _():
        @pl.loop(0, 4)
        def _(tb):
            at = pl.ds(pl.multiple_of(tb * TB, TB), TB)
            middle = norm_back(sg[:, at], xh1[:, at], rstd[1, :, at], 1)
            add_col(7, middle * (xh0[:, at] * param(0) + param(3)))
            sg[:, at] = param(7) * middle
            tlow[:, at] = middle.astype(BF16)

    @part("cross_output_back")
    def _():
        for r in range(2):
            slow[256 * r:256 * r + 256] = dot(weight(r, 7), tlow[...], 0, 0).astype(BF16)
        square_grad(7, tlow[...], cctx[...].reshape(D, T))

    link.moment("cross_output_back")

    def scaled_grad(context, which, h):
        rows = pl.ds(pl.multiple_of(h * HD, HD), HD)
        g = (slow[rows, :].astype(F32) * inv[which, h]).astype(BF16)
        delta = jnp.sum(g.astype(F32) * context[h].astype(F32), axis=0, keepdims=True)
        return g, delta

    def grad_tile(ref, i, h, keys, at, g, e, dp, delta, first, last):
        q, k = ref[0, h, :, at], ref[1, h, :, 0:keys]
        ds = e * (dp - delta).astype(BF16)
        for n, part in ((0, dot(q, ds, 1, 1)), (1, dot(g, e, 1, 1))):
            acc[i, n, :, 0:keys] = part if first else acc[i, n, :, 0:keys] + part
        ref[0, h, :, at] = (dot(k, ds, 1, 0) * 0.125).astype(BF16)
        if last:
            ref[1, h] = acc[i, 0].astype(BF16)
            ref[2, h] = acc[i, 1].astype(BF16)

    @pl.loop(0, 4)
    def _(two):
        slots = [lax.rem(two, 2) * 2 + i for i in range(2)]
        for i in range(2):
            e_in(two * 2 + i, slots[i]).wait()

        @part("cross_back")
        def _():
            shared = [scaled_grad(cctx, 1, two * 2 + i) for i in range(2)]

            def product(i, j):
                return dot(pay[2, two * 2 + i], shared[i][0][:, 256 * j:256 * j + 256], 0, 0)

            def rest(i, j, dp):
                at = slice(256 * j, 256 * j + 256)
                g, delta = shared[i]
                grad_tile(
                    pay, i, two * 2 + i, T, at, g[:, at], ring[slots[i], :, at], dp, delta[:, at],
                    j == 0, j == 3,
                )

            ahead([(i, j) for i in range(2) for j in range(4)], 1, product, rest)

        @pl.when(two < 2)
        def _():
            for i in range(2):
                e_in(two * 2 + i + 4, slots[i]).start()

        @pl.when(two >= 2)
        def _():
            for slot in slots:
                own_in(slot).start()

        link.during_cross_back(two)

    @part("memory_grad")
    def _():
        for r in range(2):
            out = dot(weight(r, 5), grad_of(pay, 1), 0, 0) + dot(weight(r, 6), grad_of(pay, 2), 0, 0)
            gs[r] = out.T.astype(BF16)

    link.put_output(1)
    link.moment("memory_grad")
    @part("cross_grads")
    def _():
        for r in range(2):
            half = slice(256 * r, 256 * r + 256)
            sg[half] = sg[half] + dot(weight(r, 4), grad_of(pay, 0), 0, 0)
        square_grad(4, grad_of(pay, 0), flow)
        square_grad(5, grad_of(pay, 1), mt)
        square_grad(6, grad_of(pay, 2), mt)

    link.moment("cross_grads")

    @part("inner_norm")
    def _():
        @pl.loop(0, 4)
        def _(tb):
            at = pl.ds(pl.multiple_of(tb * TB, TB), TB)
            inner = norm_back(sg[:, at], xh0[:, at], rstd[0, :, at], 0)
            add_col(6, inner * xt[:, at].astype(F32))
            sg[:, at] = param(6) * inner
            tlow[:, at] = inner.astype(BF16)

        for k in range(9):
            part = jnp.sum(cols[k], axis=1, keepdims=True)
            gcol[:, :, :, :, :, k:k + 1] = part.reshape(2, 4, 2, 2, 16, 1)

    link.moment("inner_norm")

    @part("self_output_back")
    def _():
        for r in range(2):
            slow[256 * r:256 * r + 256] = dot(weight(r, 3), tlow[...], 0, 0).astype(BF16)

    link.moment("self_output_back")

    @pl.loop(0, 4)
    def _(turn):
        pair = link.pair_back(turn)
        own_in(pair).wait()
        @part("self_back")
        def _():
            shared = [scaled_grad(ctx, 0, pair * 2 + i) for i in range(2)]

            def product(i, j):
                at = slice(256 * j, 256 * j + 256)
                return dot(qkv[2, pair * 2 + i, :, 0:256 * (j + 1)], shared[i][0][:, at], 0, 0)

            def rest(i, j, dp):
                keys, at = 256 * (j + 1), slice(256 * j, 256 * j + 256)
                g, delta = shared[i]
                row, lane = self_tile(i, j)
                e = ring[pair, row:row + keys, lane:lane + 256]
                grad_tile(
                    qkv, i, pair * 2 + i, keys, at, g[:, at], e, dp, delta[:, at], j == 3, j == 0
                )

            ahead([(i, j) for i in range(2) for j in (3, 2, 1, 0)], 1, product, rest)

        link.amid_self_back(turn)

        @pl.when(turn == 0)
        def _():
            @part("self_output_grad")
            def _():
                for r in range(2):
                    right = ctx[...].reshape(D, T)[256 * r:256 * r + 256]
                    part = dot(tlow[...], right, 1, 1).astype(BF16)
                    wdn[r, :, :, :, 96:128, :] = part.reshape(4, 2, 2, 32, 256)

        @part("self_grads")
        def _():
            left = jnp.concatenate([qkv[m, pl.ds(2 * pair, 2)].reshape(128, T) for m in range(3)], axis=0)
            for r in range(2):
                part = dot(left, xt[256 * r:256 * r + 256], 1, 1).astype(BF16)
                for m in range(3):
                    wdn[r, pair, :, :, 32 * m:32 * m + 32, :] = part[128 * m:128 * m + 128].reshape(2, 2, 32, 256)

        link.during_self_back(turn)

    link.free_output(1)
    @part("tokens_grad")
    def _():
        for r in range(2):
            out = sg[256 * r:256 * r + 256]
            for m in range(3):
                out = out + dot(weight(r, m), grad_of(qkv, m), 0, 0)
            gs[r] = out.T.astype(BF16)

    link.moment("tokens_grad")
    link.put_output(2)
    link.finish()


def part(name):
    def run(section):
        with jax.named_scope(name):
            section()

    return run


class Alone:
    def __init__(self, inputs, outputs, weights, grads, buffers, sem):
        self.inputs, self.outputs, self.weights, self.grads = inputs, outputs, weights, grads
        self.xs, self.cs, self.gs, self.w8, self.wup, self.wdn = buffers
        self.sem = sem
        copy = pltpu.make_async_copy
        self.loads = [
            copy(inputs[0], self.xs.at[0], sem.at[0]),
            copy(inputs[1], self.xs.at[1], sem.at[1]),
            copy(inputs[2], self.cs, sem.at[2]),
            copy(self.squares(weights), self.w8, sem.at[3]),
            copy(weights.at[:, :, :, :, pl.ds(256, 128), :], self.wup, sem.at[4]),
            copy(weights.at[:, :, :, :, pl.ds(384, 128), :], self.wdn, sem.at[5]),
        ]
        self.stores = [
            copy(self.xs.at[0], outputs[0], sem.at[6]),
            copy(self.gs, outputs[1], sem.at[7]),
            copy(self.gs, outputs[2], sem.at[7]),
        ]

    def squares(self, ref):
        return ref.at[:, :, :, :, pl.ds(0, 256), :]

    def begin(self):
        for load in self.loads:
            load.start()

    def line(self, ref):
        return ref[0:1, :]

    def wait_input(self, i):
        self.loads[i].wait()

    def wait_weights(self, group):
        if group == 4:
            self.loads[4].wait()
        if group == 5:
            self.loads[5].wait()

    def gathered(self):
        pass

    def moment(self, name):
        down = pltpu.make_async_copy(
            self.wdn, self.grads.at[:, :, :, :, pl.ds(384, 128), :], self.sem.at[2]
        )
        if name == "mask":
            self.loads[3].wait()
        if name == "feed_down_back":
            down.start()
        if name == "self_output_back":
            down.wait()

    def put_output(self, i):
        self.stores[i].start()

    def free_output(self, i):
        self.stores[i].wait()

    def pair_of(self, turn):
        return turn

    def before_self(self, turn):
        pass

    def amid_self(self, turn):
        pass

    def during_self(self, turn):
        pass

    def during_cross(self, h):
        pass

    def during_cross_back(self, h):
        pass

    def pair_back(self, turn):
        return turn

    def amid_self_back(self, turn):
        pass

    def during_self_back(self, turn):
        pass

    def finish(self):
        def grads(first, count):
            return self.grads.at[:, :, :, :, pl.ds(first, count), :]

        copies = [
            pltpu.make_async_copy(self.wdn, grads(0, 128), self.sem.at[0]),
            pltpu.make_async_copy(self.wup, grads(256, 128), self.sem.at[1]),
            pltpu.make_async_copy(
                self.w8.at[:, :, :, :, pl.ds(128, 128), :], grads(128, 128), self.sem.at[2]
            ),
        ]
        for copy in copies:
            copy.start()
        for copy in copies:
            copy.wait()
        self.stores[0].wait()
        self.stores[2].wait()


class Linked:
    def __init__(self, inputs, shards, params, outputs, gout, cout, buffers, landing, sems):
        self.inputs, self.shards, self.params = inputs, shards, params
        self.outputs, self.gout, self.cout = outputs, gout, cout
        self.xs, self.cs, self.gs, self.w8, self.wup, self.wdn, self.par, self.gcol = buffers
        self.land0, self.land1, self.land2, self.land3, self.plane_land, self.line_land = landing[:6]
        self.small = landing[6:]
        (self.isem, self.lsem, self.gsend, self.grecv, self.osem,
         self.rsend, self.rrecv, self.psend, self.precv) = sems
        r = lax.axis_index("row")
        col = lax.axis_index("col")
        z, y, x = col // 4, lax.rem(col // 2, 2), lax.rem(col, 2)
        self.r, self.z, self.y, self.x = r, z, y, x
        self.zs = [lax.rem(z + d, 4) for d in range(4)]
        self.partner = (1 - r, col)

        def chip(z, y, x):
            return (r, z * 4 + y * 2 + x)

        self.chip = chip
        self.across = {"x": chip(z, y, 1 - x), "y": chip(z, 1 - y, x)}
        self.along = [chip(self.zs[d], y, x) for d in (1, 2, 3)]
        self.others = [(y, 1 - x), (1 - y, x), (1 - y, 1 - x)]
        self.plane = [chip(z, *other) for other in self.others]
        self.peers = [self.partner, *self.plane, *self.along]
        self.holders = (
            (self.w8, 0, 96), (self.w8, 96, 96), (self.w8, 192, 32), (self.w8, 224, 32),
            (self.wup, 0, 128), (self.wdn, 0, 128),
        )

    def remote(self, source, target, send, recv, device):
        return pltpu.make_async_remote_copy(
            src_ref=source, dst_ref=target, send_sem=send, recv_sem=recv,
            device_id=device, device_id_type=pl.DeviceIdType.MESH,
        )


    def keep_in(self, i):
        place = (self.xs.at[0], self.xs.at[1], self.cs)[i]
        return pltpu.make_async_copy(self.inputs[i].at[self.r], place.at[self.r], self.lsem.at[i])

    def swap_in(self, i):
        place = (self.xs.at[0], self.xs.at[1], self.cs)[i]
        return self.remote(
            self.inputs[i].at[1 - self.r], place.at[self.r],
            self.isem.at[0, i], self.isem.at[1, i], self.partner,
        )

    def swap_par(self):
        place = self.par.at[self.r]
        return self.remote(place, place, self.isem.at[0, 3], self.isem.at[1, 3], self.partner)

    def keep_out(self, i):
        source = (self.xs.at[0], self.gs, self.gs)[i]
        return pltpu.make_async_copy(
            source.at[self.r], self.outputs[i].at[self.r], self.lsem.at[3 + i]
        )

    def swap_out(self, i):
        source = (self.xs.at[0], self.gs, self.gs)[i]
        return self.remote(
            source.at[1 - self.r], self.outputs[i].at[self.r],
            self.osem.at[0, i], self.osem.at[1, i], self.partner,
        )


    def gathers(self, group, step):
        ref, first, count = self.holders[group]
        r, z, y, x = self.r, self.z, self.y, self.x

        def move(place, at, half, device):
            piece = ref.at[place]
            return self.remote(
                piece, piece, self.gsend.at[group, half, at], self.grecv.at[group, half, at], device
            )

        if group < 3:
            rows = pl.ds(first, count)
            back = [z] + [self.zs[4 - d] for d in (1, 2, 3)]
            every = slice(None)
            if step == 0:
                order = (0, 2, 1)
                return [move((r, z, y, x, rows), d, 0, self.along[d]) for d in order] + [
                    move((r, z, y, x, rows), 3 + k, 0, self.plane[k]) for k in range(3)
                ]
            if step < 4:
                return [move((r, back[step], y, x, rows), 3 + 3 * step + k, 0, self.plane[k]) for k in range(3)]
            d = step - 4
            return [move((r, back[d], every, every, rows), 15 + d, 0, self.partner)]
        copies = []
        for half in range(2):
            rows = pl.ds(first + half * (count // 2), count // 2)
            every = slice(None)
            own = (r, z, y, x, rows)
            line = (r, every, y, x, rows)
            sheet = (r, every, every, x, rows) if half == 0 else (r, every, y, every, rows)
            axes = ("y", "x") if half == 0 else ("x", "y")
            if step == 0:
                copies += [move(own, d, half, self.along[d]) for d in range(3)]
            elif step == 3:
                copies.append(move((r, every, every, every, rows), 5, half, self.partner))
            else:
                place = line if step == 1 else sheet
                copies.append(move(place, 2 + step, half, self.across[axes[step - 1]]))
        return copies

    def start(self, group, step):
        for copy in self.gathers(group, step):
            copy.start()

    def start_along(self, group):
        for copy in self.gathers(group, 0)[:3]:
            copy.start()

    def start_plane(self, group):
        for copy in self.gathers(group, 0)[3:]:
            copy.start()

    def wait(self, group, step):
        for copy in self.gathers(group, step):
            copy.wait_recv()

    def gather(self, group, step):
        self.wait(group, step - 1)
        self.start(group, step)

    def forward(self, group, d):
        self.gathers(group, 0)[(0, 2, 1).index(d - 1)].wait_recv()
        self.start(group, d)

    def share(self, group, d):
        if d == 0:
            for copy in self.gathers(group, 0)[3:]:
                copy.wait_recv()
        else:
            self.wait(group, d)
        self.start(group, 4 + d)

    def begin(self):
        r, z, y, x = self.r, self.z, self.y, self.x
        for i in range(3):
            self.keep_in(i).start()
        for m in range(8):
            self.w8[r, z, y, x, 32 * m:32 * m + 32, :] = self.shards[SLOTS[m]][...]
        self.wup[r, z, y, x] = self.shards[8][...].T
        for s in range(4):
            self.wdn[r, z, y, x, 32 * s:32 * s + 32, :] = self.shards[9][:, 256 * s:256 * s + 256]
        for k in range(3):
            self.par[r, 3 * k:3 * k + 3, :] = self.params[k][...]
        barrier = pltpu.get_barrier_semaphore()
        for peer in self.peers:
            pl.semaphore_signal(barrier, inc=1, device_id=peer, device_id_type=pl.DeviceIdType.MESH)
        pl.semaphore_wait(barrier, len(self.peers))
        self.start(0, 0)
        self.swap_in(0).start()
        self.swap_par().start()
        self.swap_in(1).start()
        self.swap_in(2).start()

    def line(self, ref):
        return ref[pl.ds(self.r, 1), :]

    def wait_input(self, i):
        self.keep_in(i).wait()
        self.swap_in(i).wait_recv()
        if i == 1:
            self.swap_par().wait_recv()

    def wait_weights(self, group):
        if group < 3:
            for d in range(4):
                self.wait(group, 4 + d)
        else:
            self.wait(group, 3)

    def gathered(self):
        for group in range(6):
            for step in range(8 if group < 3 else 4):
                for copy in self.gathers(group, step):
                    copy.wait_send()


    def sums(self, group, step):
        r, z, y, x = self.r, self.z, self.y, self.x
        send, recv = self.rsend.at[group], self.rrecv.at[group]
        every = slice(None)
        if group == 3:
            ref = self.gcol
            if step == 0:
                return [self.remote(ref.at[1 - r], self.small[0], send.at[0], recv.at[0], self.partner)]
            if step == 1:
                source = ref.at[r, :, :, 1 - x]
                return [self.remote(source, self.small[1], send.at[1], recv.at[1], self.across["x"])]
            if step == 2:
                source = ref.at[r, :, 1 - y, x]
                return [self.remote(source, self.small[2], send.at[2], recv.at[2], self.across["y"])]
            return [
                self.remote(
                    ref.at[r, self.zs[d + 1], y, x], self.small[3].at[d],
                    send.at[3 + d], recv.at[3 + d], self.along[d],
                )
                for d in range(3)
            ]
        ref, at, count = self.summed(group)
        land0, land1, land2, land3 = self.landing(group)
        if step == 0:
            source = ref.at[1 - r, :, :, :, pl.ds(at, count)]
            return [self.remote(source, land0, send.at[0], recv.at[0], self.partner)]
        copies = []
        for half in range(2):
            rows = pl.ds(at + count // 2 * half, count // 2)
            axes = ("x", "y") if half == 0 else ("y", "x")
            k = 1 + 5 * half
            if step == 1:
                place = (r, every, every, 1 - x, rows) if half == 0 else (r, every, 1 - y, every, rows)
                target, device = land1.at[half], self.across[axes[0]]
                copies.append(self.remote(ref.at[place], target, send.at[k], recv.at[k], device))
            elif step == 2:
                place = (r, every, 1 - y, x, rows) if half == 0 else (r, every, y, 1 - x, rows)
                target, device = land2.at[half], self.across[axes[1]]
                copies.append(self.remote(ref.at[place], target, send.at[k + 1], recv.at[k + 1], device))
            else:
                for d in range(3):
                    copies.append(self.remote(
                        ref.at[r, self.zs[d + 1], y, x, rows], land3.at[half, d],
                        send.at[k + 2 + d], recv.at[k + 2 + d], self.along[d],
                    ))
        return copies

    def summed(self, group):
        return ((self.wdn, 0, 128), (self.wup, 0, 128), (self.w8, 128, 96), None, (self.w8, 224, 32))[group]

    def landing(self, group):
        first, count = {2: (0, 96), 4: (96, 32)}.get(group, (0, 128))
        which = 2 if group == 4 else group
        rows, half = pl.ds(first, count), pl.ds(first // 2, count // 2)
        return (
            self.land0.at[which, :, :, :, rows], self.land1.at[which, :, :, :, half],
            self.land2.at[which, :, :, half], self.land3.at[which, :, :, half],
        )

    def reduce(self, group, step):
        r, z, y, x = self.r, self.z, self.y, self.x
        every = slice(None)
        if step > 0:
            for copy in self.sums(group, step - 1):
                copy.wait_recv()
        if group == 3:
            ref = self.gcol
            if step == 1:
                ref[r] = ref[r] + self.small[0][...]
            elif step == 2:
                ref[r, :, :, x] = ref[r, :, :, x] + self.small[1][...]
            elif step == 3:
                ref[r, :, y, x] = ref[r, :, y, x] + self.small[2][...]
            elif step == 4:
                total = ref[r, z, y, x]
                for d in range(3):
                    total = total + self.small[3][d]
                self.cout[...] = total
        elif step > 0:
            ref, at, count = self.summed(group)
            land0, land1, land2, land3 = self.landing(group)
            middle = count // 2

            def add(place, value):
                ref[place] = (ref[place].astype(F32) + value.astype(F32)).astype(BF16)

            if step == 1:
                for k in range(4):
                    add((r, k, every, every, slice(at, at + count)), land0[k])
            for half in range(2):
                rows = slice(at + middle * half, at + middle * half + middle)
                if step == 2 and half == 0:
                    add((r, every, every, x, rows), land1[half])
                elif step == 2:
                    add((r, every, y, every, rows), land1[half])
                elif step == 3:
                    add((r, every, y, x, rows), land2[half])
                elif step == 4:
                    total = ref[r, z, y, x, rows].astype(F32)
                    for d in range(3):
                        total = total + land3[half, d].astype(F32)
                    first = (96 if group == 4 else 0) + middle * half
                    self.gout[2 if group == 4 else group, first:first + middle] = total
        if step < 4:
            for copy in self.sums(group, step):
                copy.start()
        elif group == 0:
            for step in range(4):
                for copy in self.sums(group, step):
                    copy.wait_send()


    def pair_back(self, turn):
        return lax.rem(self.z + 1 + turn, 4)

    def plane_sums(self, turn, step):
        r, z, y, x = self.r, self.z, self.y, self.x
        ref, p = self.wdn, self.pair_back(turn)
        send, recv = self.psend.at[turn], self.precv.at[turn]
        if step == 0:
            return [self.remote(ref.at[1 - r, p], self.land0.at[3, turn], send.at[0], recv.at[0], self.partner)]
        if step == 1:
            return [
                self.remote(
                    ref.at[r, p, to_y, to_x], self.plane_land.at[turn, k],
                    send.at[1 + k], recv.at[1 + k], self.plane[k],
                )
                for k, (to_y, to_x) in enumerate(self.others)
            ]
        return [self.remote(
            ref.at[r, p, y, x], self.line_land.at[turn], send.at[4], recv.at[4], self.chip(p, y, x)
        )]

    def reduce_plane(self, turn, step):
        r, z, y, x = self.r, self.z, self.y, self.x
        ref, p = self.wdn, self.pair_back(turn)
        if step > 0:
            for copy in self.plane_sums(turn, step - 1):
                copy.wait_recv()
        if step == 1:
            for k in range(2):
                total = ref[r, p, k].astype(F32) + self.land0[3, turn, k].astype(F32)
                ref[r, p, k] = total.astype(BF16)
        if step == 2:
            total = ref[r, p, y, x].astype(F32)
            for k in range(3):
                total = total + self.plane_land[turn, k].astype(F32)
            ref[r, p, y, x] = total.astype(BF16)
        for copy in self.plane_sums(turn, step):
            copy.start()

    def end_planes(self):
        for copy in self.plane_sums(3, 1):
            copy.wait_recv()
        total = self.wdn[self.r, self.z, self.y, self.x].astype(F32)
        for k in range(3):
            total = total + self.plane_land[3, k].astype(F32)
        for turn in range(3):
            for copy in self.plane_sums(turn, 2):
                copy.wait_recv()
            total = total + self.line_land[turn].astype(F32)
        self.gout[3] = total
        for turn in range(4):
            for step in range(3 if turn < 3 else 2):
                for copy in self.plane_sums(turn, step):
                    copy.wait_send()


    def moment(self, name):
        if name == "turn_tokens":
            self.forward(0, 1)
            self.share(0, 0)
        elif name == "turn_memory":
            self.forward(0, 3)
            self.start_along(1)
            self.forward(0, 2)
            self.start_plane(1)
        elif name == "memory_projections":
            self.gather(3, 1)
        elif name == "first_norm":
            for d in (0, 1, 3, 2):
                self.share(2, d)
            self.gather(5, 1)
        elif name == "probes":
            self.gather(3, 2)
        elif name == "half_feed_up":
            self.gather(5, 3)
        elif name == "feed_down_back":
            self.reduce(0, 0)
        elif name == "feed_up_grad":
            self.reduce(0, 1)
            self.reduce(1, 0)
        elif name == "cross_output_back":
            self.reduce(1, 1)
            self.reduce(4, 0)
        elif name == "memory_grad":
            self.reduce(0, 3)
        elif name == "cross_grads":
            self.reduce(2, 0)
            self.reduce(4, 2)
        elif name == "inner_norm":
            self.reduce(3, 0)
            self.reduce(2, 1)
            self.reduce(1, 3)
        elif name == "tokens_grad":
            self.reduce_plane(2, 2)

    def at_turn(self, index, turns):
        for turn, actions in turns.items():

            @pl.when(index == turn)
            def _():
                for move, *where in actions:
                    move(*where)

    def pair_of(self, turn):
        back = turn + turn // 2 * (1 - 2 * lax.rem(turn, 2))
        return lax.rem(self.z - back + 4, 4)

    def before_self(self, turn):
        self.at_turn(turn, {n: [(self.wait, 0, 4 + d)] for n, d in enumerate((0, 1, 3, 2))})

    def amid_self(self, turn):
        self.at_turn(turn, {
            0: [(self.share, 0, 1)],
            1: [(self.share, 0, 3)],
            2: [(self.share, 0, 2)],
            3: [(self.forward, 2, 1), (self.forward, 2, 3), (self.forward, 2, 2)],
        })

    def during_self(self, turn):
        self.at_turn(turn, {
            0: [(self.start_along, 2), (self.start, 3, 0), (self.start, 4, 0)],
            1: [
                (self.forward, 1, 1), (self.forward, 1, 3), (self.forward, 1, 2),
                (self.start_plane, 2), (self.start, 5, 0),
            ],
            2: [(self.share, 1, 0)],
            3: [(self.share, 1, 1), (self.share, 1, 3), (self.share, 1, 2), (self.gather, 4, 1)],
        })

    def during_cross(self, two):
        self.at_turn(two, {
            0: [(self.gather, 4, 2)],
            1: [(self.gather, 5, 2), (self.gather, 3, 3)],
            3: [(self.gather, 4, 3)],
        })

    def during_cross_back(self, two):
        self.at_turn(two, {
            0: [(self.reduce, 4, 1)],
            1: [(self.reduce, 0, 2)],
            3: [(self.reduce, 1, 2)],
        })

    def amid_self_back(self, turn):
        @pl.when(turn == 0)
        def _():
            self.reduce(0, 4)

        @pl.when(turn >= 1)
        def _():
            self.reduce_plane(turn - 1, 1)

    def during_self_back(self, turn):
        self.reduce_plane(turn, 0)
        self.at_turn(turn, {
            0: [(self.reduce, 3, 1), (self.reduce, 4, 3)],
            1: [(self.reduce, 2, 2)],
            2: [(self.reduce, 1, 4), (self.reduce, 3, 2), (self.reduce, 4, 4)],
            3: [(self.reduce, 2, 3), (self.reduce_plane, 0, 2), (self.reduce_plane, 1, 2)],
        })

    def put_output(self, i):
        self.keep_out(i).start()
        self.swap_out(i).start()

    def free_output(self, i):
        self.reduce_plane(3, 1)
        self.reduce(3, 3)
        self.keep_out(i).wait()
        self.swap_out(i).wait_send()

    def finish(self):
        self.reduce(3, 4)
        self.reduce(2, 4)
        self.end_planes()
        for group in range(1, 5):
            for step in range(4):
                for copy in self.sums(group, step):
                    copy.wait_send()
        for i in range(3):
            self.swap_in(i).wait_send()
        self.swap_par().wait_send()
        for i in (0, 2):
            self.keep_out(i).wait()
            self.swap_out(i).wait_send()
        for i in range(3):
            self.swap_out(i).wait_recv()


CHIPS = 16


def to_sixteen(w):
    n = w.shape[1]
    if n == CHIPS:
        return w
    part = D // n

    def spread(block):
        block = block.reshape(2, n, -1, part, 256).swapaxes(1, 2).reshape(2, -1, CHIPS, 32, 256)
        return block.swapaxes(1, 2).reshape(2, CHIPS, -1, 256)

    return jnp.concatenate(
        [
            spread(w[:, :, :8 * part]),
            w[:, :, 8 * part:12 * part].reshape(2, CHIPS, 128, 256),
            spread(w[:, :, 12 * part:]),
        ],
        axis=2,
    )


def from_sixteen(g, n):
    if n == CHIPS:
        return g
    part = D // n

    def gather(block):
        block = block.reshape(2, CHIPS, -1, 32, 256).swapaxes(1, 2).reshape(2, -1, n, part, 256)
        return block.swapaxes(1, 2).reshape(2, n, -1, 256)

    return jnp.concatenate(
        [
            gather(g[:, :, :256]),
            g[:, :, 256:384].reshape(2, n, 4 * part, 256),
            gather(g[:, :, 384:]),
        ],
        axis=2,
    )


ANY = pl.BlockSpec(memory_space=pl.ANY)
VMEM = pl.BlockSpec(memory_space=pltpu.VMEM)
SHAPE = jax.ShapeDtypeStruct
STASH = [SHAPE((H, T, T), BF16), SHAPE((4, T, 1280), BF16)]


def layer_scratch():
    V = pltpu.VMEM
    return [
        V((2, 2, T, 256), BF16), V((2, T, 256), BF16),
        V((D, T), BF16), V((D, T), BF16),
        V((2, 4, 2, 2, 256, 256), BF16),
        V((2, 4, 2, 2, 128, 256), BF16), V((2, 4, 2, 2, 128, 256), BF16),
        V((3, H, HD, T), BF16), V((3, H, HD, T), BF16),
        V((H, HD, T), BF16), V((H, HD, T), BF16),
        V((2, H, 1, T), F32),
        V((D, T), F32), V((D, T), F32), V((2, 1, T), F32),
        V((D, T), BF16), V((D, T), BF16), V((D, T), BF16),
        V((4, T, 1280), BF16),
        V((D, T), F32), V((2, T, 256), BF16),
        V((D, 128), F32), V((9, D, 128), F32),
        V((2, 2, HD, T), F32),
        pltpu.SemaphoreType.DMA((4,)),
    ]


def run_alone(x, mem, cot, w, par, seg, pad):
    def kernel(x, mem, cot, w, par, seg, pad, lo, mg, tg, g, e, es, gcol, *rest):
        scratch, sem = rest[:-1], rest[-1]
        xs, cs, gs = scratch[0], scratch[1], scratch[20]
        link = Alone(
            (x, mem, cot), (lo, mg, tg), w, g, (xs, cs, gs, scratch[4], scratch[5], scratch[6]), sem
        )
        layer(link, e, es, par, seg, pad, *scratch[:-1], gcol, scratch[-1])

    wide = SHAPE((2, T, 256), BF16)
    return pl.pallas_call(
        kernel,
        in_specs=[ANY] * 4 + [VMEM] * 3,
        out_specs=[ANY] * 6 + [VMEM],
        out_shape=[wide] * 3
        + [SHAPE((2, 4, 2, 2, 512, 256), BF16), *STASH, SHAPE((2, 4, 2, 2, 16, 128), F32)],
        scratch_shapes=layer_scratch() + [pltpu.SemaphoreType.DMA((8,))],
        compiler_params=pltpu.CompilerParams(vmem_limit_bytes=63 * 2**20),
        name="layer",
    )(x, mem, cot, w, par, seg, pad)


def run_linked(inputs, shards, params, seg, pad):
    def kernel(*refs):
        inputs, shards, params, seg, pad = refs[0:3], refs[3:13], refs[13:16], refs[16], refs[17]
        outputs, e, es, gout, cout = refs[18:21], refs[21], refs[22], refs[23], refs[24]
        scratch = refs[25:25 + 25]
        par, gcol = refs[50], refs[51]
        landing, sems = refs[52:62], refs[62:]
        xs, cs, gs = scratch[0], scratch[1], scratch[20]
        link = Linked(
            inputs, shards, params, outputs, gout, cout,
            (xs, cs, gs, scratch[4], scratch[5], scratch[6], par, gcol), landing, sems,
        )
        layer(link, e, es, par, seg, pad, *scratch[:-1], gcol, scratch[-1])

    V = pltpu.VMEM
    DMA = pltpu.SemaphoreType.DMA
    wide = SHAPE((2, T, 256), BF16)
    return pl.pallas_call(
        kernel,
        in_specs=[ANY] * 3 + [VMEM] * 15,
        out_specs=[ANY] * 5 + [VMEM] * 2,
        out_shape=[wide] * 3 + STASH + [SHAPE((4, 128, 256), F32), SHAPE((16, 128), F32)],
        scratch_shapes=layer_scratch() + [
            V((2, 16, 256), F32), V((2, 4, 2, 2, 16, 128), F32),
            V((4, 4, 2, 2, 128, 256), BF16), V((3, 2, 4, 2, 64, 256), BF16),
            V((3, 2, 4, 64, 256), BF16), V((3, 2, 3, 64, 256), BF16),
            V((4, 3, 128, 256), BF16), V((3, 128, 256), BF16),
            V((4, 2, 2, 16, 128), F32), V((4, 2, 16, 128), F32),
            V((4, 16, 128), F32), V((3, 16, 128), F32),
            DMA((2, 4)), DMA((6,)), DMA((6, 2, 19)), DMA((6, 2, 19)), DMA((2, 3)),
            DMA((5, 11)), DMA((5, 11)), DMA((5, 5)), DMA((5, 5)),
        ],
        compiler_params=pltpu.CompilerParams(
            vmem_limit_bytes=63 * 2**20, collective_id=0, has_side_effects=True
        ),
        name="layer",
    )(*inputs, *shards, *params, seg, pad)


def ending(lo, mg, tg, gout, cout):
    def kernel(lo, mg, tg, gout, cout, lo_out, tg_out, mg_out, *rest):
        lo_out[...] = lo[...]
        mg_out[...] = mg[...].astype(F32)
        tg_out[...] = tg[...].astype(F32)

        @pl.when(pl.program_id(0) == 0)
        def _():
            for m in range(8):
                at = 32 * (SLOTS.index(m) % 4)
                rest[m][...] = gout[3 if m < 4 else 2, at:at + 32, :]
            rest[8][...] = gout[1].T
            for s in range(4):
                rest[9][:, 256 * s:256 * s + 256] = gout[0, 32 * s:32 * s + 32, :]
            small = cout[...].T
            for k in range(3):
                rest[10 + k][...] = small[3 * k:3 * k + 3, :]

    part = pl.BlockSpec((1, 512, 256), lambda i: (i // 2, i % 2, 0))

    def whole(*shape):
        return pl.BlockSpec(shape, lambda i: (0,) * len(shape))

    shapes = [(32, 256)] * 8 + [(256, 128), (32, 1024)] + [(3, 16)] * 3
    return pl.pallas_call(
        kernel,
        grid=(4,),
        in_specs=[part] * 3 + [whole(4, 128, 256), whole(16, 128)],
        out_specs=[part] * 3 + [whole(*one) for one in shapes],
        out_shape=[SHAPE((2, T, 256), BF16), SHAPE((2, T, 256), F32), SHAPE((2, T, 256), F32)]
        + [SHAPE(one, F32) for one in shapes],
        name="ending",
    )(lo, mg, tg, gout, cout)


def body(
    tokens, memory, cotangent, segments, padding,
    self_query, self_key, self_value, self_output,
    cross_query, cross_key, cross_value, cross_output,
    feed_up, feed_down, norm_gain, norm_bias, omegas,
):
    n = lax.axis_size("col")
    squares = (
        self_query, self_key, self_value, self_output,
        cross_query, cross_key, cross_value, cross_output,
    )
    if n == CHIPS:
        lo, mg, tg, _, _, gout, cout = run_linked(
            (tokens, memory, cotangent), (*[m.T for m in squares], feed_up, feed_down.T),
            (norm_gain, norm_bias, omegas), segments, padding,
        )
        out = ending(lo, mg, tg, gout, cout)
        turned = [one.T for one in out[3:11]]
        return (*out[0:3], *turned, out[11], out[12].T, *out[13:16])
    row = lax.axis_index("row")
    part = D // n
    blob = jnp.concatenate(
        [squares[m].T for m in SLOTS]
        + [feed_up.T]
        + [feed_down.T[:, 256 * s:256 * s + 256] for s in range(4)],
        axis=0,
    )
    w = lax.all_gather(blob, ("row", "col"), axis=0, tiled=False).reshape(2, n, 16 * part, 256)
    w = to_sixteen(w).reshape(2, 4, 2, 2, 512, 256)
    par = jnp.concatenate([norm_gain, norm_bias, omegas, jnp.zeros((7, 256), F32)], axis=0)
    par = lax.all_gather(par, "row", axis=0, tiled=False)

    def mine(array):
        return lax.all_to_all(array, "row", split_axis=0, concat_axis=0, tiled=True)

    seg = lax.dynamic_slice_in_dim(segments, row, 1, 0)
    pad = lax.dynamic_slice_in_dim(padding, row, 1, 0)
    lo, mg, tg, g, _, _, gcol = run_alone(
        mine(tokens), mine(memory), mine(cotangent), w, par, seg, pad
    )
    lo, tg, mg = mine(lo), mine(tg).astype(F32), mine(mg).astype(F32)
    g = from_sixteen(g.reshape(2, CHIPS, 512, 256), n).reshape(2 * n, 16 * part, 256)
    g = lax.psum_scatter(g.astype(F32), ("row", "col"), scatter_dimension=0, tiled=False)
    gcol = lax.psum_scatter(
        gcol.reshape(2 * n, part // 2, 128), ("row", "col"), scatter_dimension=0, tiled=False
    )
    small = gcol[:, 0:9].T
    last = 12 * part
    return (
        lo, tg, mg,
        *[g[part * i:part * i + part].T for i in (SLOTS.index(m) for m in range(8))],
        g[8 * part:last].T,
        jnp.concatenate([g[last + part * s:last + part * s + part].T for s in range(4)], axis=0),
        small[0:3], small[3:6], small[6:9],
    )


def solution(mesh):
    wide = P(None, "col", "row")
    square = P("row", "col")
    return jax.shard_map(
        body,
        mesh=mesh,
        in_specs=(wide,) * 3 + (P(None, "col"),) * 2 + (square,) * 10 + (P(None, "row"),) * 3,
        out_specs=(wide,) * 3 + (square,) * 10 + (P(None, ("row", "col")),) * 3,
        check_vma=False,
    )
```

```python
import jax
import jax.numpy as jnp
from jax import lax
from jax.experimental import pallas as pl
from jax.experimental.pallas import tpu as pltpu
from jax.sharding import PartitionSpec as P

F32 = jnp.float32
BF16 = jnp.bfloat16
EPSILON = 1e-05
MASKED = -1e30
T = 1024
D = 512
H = 8
HD = 64
TB = 256


def dot(left, right, left_dim, right_dim):
    return lax.dot_general(
        left, right, (((left_dim,), (right_dim,)), ((), ())), preferred_element_type=F32
    )


SLOTS = (0, 1, 2, 3, 5, 6, 4, 7)


def gelu_both(v):
    root = 0.7978845608028654
    square = v * v
    t = jnp.tanh(root * v * (1.0 + 0.044715 * square))
    half = 0.5 * (1.0 + t)
    slope = half + (0.5 * root) * v * (1.0 - t * t) * (1.0 + (3.0 * 0.044715) * square)
    return v * half, slope


def layer(
    link, e_hbm, es_hbm, par, seg, pad,
    xs, cs, xt, mt, w8, wup, wdn, qkv, pay, ctx, cctx, inv, xh0, xh1, rstd,
    flow, slow, tlow, ring, sg, gs, pcol, cols, acc, gcol, esem,
):
    def weight(r, m):
        at = 32 * SLOTS.index(m)
        return w8[r, :, :, :, at:at + 32, :].reshape(D, 256)

    def forward(m, source):
        return dot(weight(0, m), source[0:256], 1, 0) + dot(weight(1, m), source[256:512], 1, 0)

    def param(k):
        return pcol[:, k:k + 1]

    def grad_of(ref, i):
        return ref[i].reshape(D, T)

    def add_col(k, value):
        cols[k] = cols[k] + (value[:, 0:128] + value[:, 128:256])

    link.begin()
    cols[...] = jnp.zeros_like(cols)
    link.wait_input(0)
    @part("turn_tokens")
    def _():
        for r in range(2):
            xt[256 * r:256 * r + 256] = xs[0, r].T

    link.moment("turn_tokens")
    link.wait_input(1)
    @part("turn_memory")
    def _():
        for r in range(2):
            mt[256 * r:256 * r + 256] = xs[1, r].T

    link.moment("turn_memory")
    pcol[...] = jnp.zeros_like(pcol)
    for r in range(2):
        pcol[256 * r:256 * r + 256, 0:16] = par[r].T

    @part("mask")
    def _():
        padlen = jnp.sum(link.line(pad), axis=1, keepdims=True)
        for j in range(4):
            low = link.line(seg)[:, 256 * j:256 * j + 256]
            here = 256 * j + lax.broadcasted_iota(jnp.int32, (1, 256), 1)
            high = jnp.minimum(here, padlen - 1)
            rows = lax.broadcasted_iota(jnp.int32, (T, 256), 0)
            fits = ((rows >= low) & (rows <= high)) | (rows == here)
            xs[j // 2, j % 2] = jnp.where(fits, 0.0, MASKED).astype(BF16)

    link.moment("mask")
    ones = jnp.ones((16, T), BF16)

    def weighted(scores, v):
        top = jnp.max(scores, axis=0, keepdims=True)
        e = jnp.exp(scores - top).astype(BF16)
        both = dot(v, e, 1, 0)
        inverse = 1.0 / both[HD:HD + 1]
        return e, (both[0:HD] * inverse).astype(BF16), inverse

    def ahead(tiles, depth, product, rest):
        products = [product(*tile) for tile in tiles[:depth]]
        for n, tile in enumerate(tiles):
            if n + depth < len(tiles):
                products.append(product(*tiles[n + depth]))
            rest(*tile, products[n])

    def self_tile(i, j):
        if j == 3:
            return 0, 256 * i
        if j == 1:
            return 512 * i, 1024
        return (0 if j == 0 else 256), 512 + 256 * i

    def own_out(pair):
        return pltpu.make_async_copy(ring.at[pair], es_hbm.at[pair], esem.at[pair])

    def own_in(pair):
        return pltpu.make_async_copy(es_hbm.at[pair], ring.at[pair], esem.at[pair])

    def e_out(h, slot):
        return pltpu.make_async_copy(ring.at[slot, :, pl.ds(0, T)], e_hbm.at[h], esem.at[slot])

    def e_in(h, slot):
        return pltpu.make_async_copy(e_hbm.at[h], ring.at[slot, :, pl.ds(0, T)], esem.at[slot])

    @pl.loop(0, 4)
    def _(turn):
        pair = link.pair_of(turn)
        link.before_self(turn)

        @part("self_projections")
        def _():
            left = [w8[r, pair, :, :, 0:96, :].reshape(384, 256) for r in range(2)]
            out = dot(left[0], xt[0:256], 1, 0) + dot(left[1], xt[256:512], 1, 0)
            for n in range(12):
                block = out[32 * n:32 * n + 32]
                if n % 3 == 0:
                    block = block * 0.125
                half = n // 3 % 2
                qkv[n % 3, pair * 2 + n // 6, 32 * half:32 * half + 32, :] = block.astype(BF16)

        link.amid_self(turn)

        @part("self_attention")
        def _():
            values = [jnp.concatenate([qkv[2, pair * 2 + i], ones], axis=0) for i in range(2)]

            def product(i, j):
                h, keys = pair * 2 + i, 256 * (j + 1)
                scores = dot(qkv[1, h, :, 0:keys], qkv[0, h, :, 256 * j:256 * j + 256], 0, 0)
                return scores + xs[j // 2, j % 2, 0:keys, :].astype(F32)

            def rest(i, j, scores):
                h, keys, at = pair * 2 + i, 256 * (j + 1), slice(256 * j, 256 * j + 256)
                e, out, inverse = weighted(scores, values[i][:, 0:keys])
                row, lane = self_tile(i, j)
                ring[pair, row:row + keys, lane:lane + 256] = e
                ctx[h, :, at] = out
                inv[0, h, :, at] = inverse

            ahead([(i, j) for j in range(4) for i in range(2)], 2, product, rest)

        own_out(pair).start()
        link.during_self(turn)

    link.wait_weights(1)
    @part("memory_projections")
    def _():
        for m in (5, 6):
            pay[m - 4] = forward(m, mt).astype(BF16).reshape(H, HD, T)

    link.moment("memory_projections")

    def norm(total):
        average = jnp.mean(total, axis=0, keepdims=True)
        centred = total - average
        factor = lax.rsqrt(jnp.mean(centred * centred, axis=0, keepdims=True) + EPSILON)
        return centred * factor, factor

    @part("first_norm")
    def _():
        def product(tb):
            return forward(3, ctx[:, :, TB * tb:TB * tb + TB].reshape(D, TB))

        def rest(tb, out):
            at = slice(TB * tb, TB * tb + TB)
            normed, factor = norm(param(6) * xt[:, at].astype(F32) + out)
            xh0[:, at] = normed
            rstd[0, :, at] = factor
            flow[:, at] = (normed * param(0) + param(3)).astype(BF16)

        ahead([(tb,) for tb in range(4)], 1, product, rest)

    link.moment("first_norm")
    link.wait_weights(2)

    @part("probes")
    def _():
        pay[0] = (forward(4, flow) * 0.125).astype(BF16).reshape(H, HD, T)

    link.moment("probes")

    @pl.loop(0, 4)
    def _(two):
        slots = [lax.rem(two, 2) * 2 + i for i in range(2)]

        @pl.when(two < 2)
        def _():
            for slot in slots:
                own_out(slot).wait()

        @pl.when(two >= 2)
        def _():
            for slot in slots:
                e_out(slot, slot).wait()

        @part("cross_attention")
        def _():
            values = [jnp.concatenate([pay[2, two * 2 + i], ones], axis=0) for i in range(2)]

            def product(i, j):
                h = two * 2 + i
                return dot(pay[1, h], pay[0, h, :, 512 * j:512 * j + 512], 0, 0)

            def rest(i, j, scores):
                h, at = two * 2 + i, slice(512 * j, 512 * j + 512)
                e, out, inverse = weighted(scores, values[i])
                ring[slots[i], :, at] = e
                cctx[h, :, at] = out
                inv[1, h, :, at] = inverse

            ahead([(i, j) for i in range(2) for j in range(2)], 2, product, rest)

        for i in range(2):
            e_out(two * 2 + i, slots[i]).start()
        link.during_cross(two)

    link.wait_weights(3)

    @part("second_norm")
    def _():
        def product(tb):
            return forward(7, cctx[:, :, TB * tb:TB * tb + TB].reshape(D, TB))

        def rest(tb, out):
            at = slice(TB * tb, TB * tb + TB)
            first = xh0[:, at] * param(0) + param(3)
            normed, factor = norm(param(7) * first + out)
            xh1[:, at] = normed
            rstd[1, :, at] = factor
            slow[:, at] = (normed * param(1) + param(4)).astype(BF16)

        ahead([(tb,) for tb in range(4)], 1, product, rest)

    for slot in range(4):
        e_out(4 + slot, slot).wait()
    link.wait_weights(4)
    link.wait_input(2)

    def up(r, b):
        return wup[r, b].reshape(512, 256)

    def down(b):
        return wdn[b // 4, :, :, :, 32 * (b % 4):32 * (b % 4) + 32, :].reshape(D, 256)

    for part_of_two in range(2):

        @part("feed_up")
        def _():
            for b in (2 * part_of_two, 2 * part_of_two + 1):
                place = slice(512 * (b % 2), 512 * (b % 2) + 512)
                for t in range(2):
                    at = slice(512 * t, 512 * t + 512)
                    v = dot(up(0, b), slow[0:256, at], 1, 0) + dot(up(1, b), slow[256:512, at], 1, 0)
                    value, slope = gelu_both(v)
                    ring[b // 2, place, at] = value.astype(BF16)
                    ring[2 + b // 2, place, at] = slope.astype(BF16)

        if part_of_two == 0:
            link.moment("half_feed_up")

    link.wait_weights(5)

    def norm_back(upstream, normed, factor, k):
        scaled = upstream * param(k)
        one = jnp.mean(scaled, axis=0, keepdims=True)
        two = jnp.mean(scaled * normed, axis=0, keepdims=True)
        add_col(k, upstream * normed)
        add_col(3 + k, upstream)
        return factor * (scaled - one - normed * two)

    @part("feed_down")
    def _():
        @pl.loop(0, 2)
        def _(two):
            def place(n):
                return pl.ds(pl.multiple_of((two * 2 + n) * TB, TB), TB)

            def product(n):
                at, out = place(n), None
                for b in range(8):
                    piece = dot(down(b), ring[b // 4, 256 * (b % 4):256 * (b % 4) + 256, at], 1, 0)
                    out = piece if out is None else out + piece
                return out

            def rest(n, out):
                at = place(n)
                second = xh1[:, at] * param(1) + param(4)
                normed, factor = norm(param(8) * second + out)
                final = (normed * param(2) + param(5)).astype(BF16)
                upstream = jnp.concatenate([cs[0, at, :].T, cs[1, at, :].T], axis=0).astype(F32)
                for r in range(2):
                    xs[0, r, at, :] = final[256 * r:256 * r + 256].T
                third = norm_back(upstream, normed, factor, 2)
                add_col(8, third * second)
                sg[:, at] = param(8) * third
                tlow[:, at] = third.astype(BF16)

            ahead([(n,) for n in range(2)], 1, product, rest)

    link.put_output(0)

    def square_grad(m, left, right):
        for r in range(2):
            part = dot(left, right[256 * r:256 * r + 256], 1, 1).astype(BF16)
            at = 32 * SLOTS.index(m)
            w8[r, :, :, :, at:at + 32, :] = part.reshape(4, 2, 2, 32, 256)

    link.gathered()
    @part("feed_down_back")
    def _():
        for f in range(8):
            rows = slice(256 * (f % 4), 256 * (f % 4) + 256)
            grad = dot(down(f), tlow[...], 0, 0) * ring[2 + f // 4, rows, 0:T].astype(F32)
            part = dot(tlow[...], ring[f // 4, rows, 0:T], 1, 1).astype(BF16)
            wdn[f // 4, :, :, :, 32 * (f % 4):32 * (f % 4) + 32, :] = part.reshape(4, 2, 2, 32, 256)
            ring[2 + f // 4, rows, 0:T] = grad.astype(BF16)

    link.moment("feed_down_back")
    @part("second_grad")
    def _():
        for r in range(2):
            half = slice(256 * r, 256 * r + 256)
            for t in range(2):
                at = slice(512 * t, 512 * t + 512)
                part = None
                for b in range(4):
                    place = slice(512 * (b % 2), 512 * (b % 2) + 512)
                    one = dot(up(r, b), ring[2 + b // 2, place, at], 0, 0)
                    part = one if part is None else part + one
                sg[half, at] = sg[half, at] + part

    @part("feed_up_grad")
    def _():
        for b in range(4):
            grad = ring[2 + b // 2, 512 * (b % 2):512 * (b % 2) + 512, 0:T]
            for r in range(2):
                part = dot(grad, slow[256 * r:256 * r + 256], 1, 1).astype(BF16)
                wup[r, b] = part.reshape(2, 2, 128, 256)

    link.moment("feed_up_grad")

    for slot in range(4):
        e_in(slot, slot).start()

    @part("middle_norm")
    def _():
        @pl.loop(0, 4)
        def _(tb):
            at = pl.ds(pl.multiple_of(tb * TB, TB), TB)
            middle = norm_back(sg[:, at], xh1[:, at], rstd[1, :, at], 1)
            add_col(7, middle * (xh0[:, at] * param(0) + param(3)))
            sg[:, at] = param(7) * middle
            tlow[:, at] = middle.astype(BF16)

    @part("cross_output_back")
    def _():
        for r in range(2):
            slow[256 * r:256 * r + 256] = dot(weight(r, 7), tlow[...], 0, 0).astype(BF16)
        square_grad(7, tlow[...], cctx[...].reshape(D, T))

    link.moment("cross_output_back")

    def scaled_grad(context, which, h):
        rows = pl.ds(pl.multiple_of(h * HD, HD), HD)
        g = (slow[rows, :].astype(F32) * inv[which, h]).astype(BF16)
        delta = jnp.sum(g.astype(F32) * context[h].astype(F32), axis=0, keepdims=True)
        return g, delta

    def grad_tile(ref, i, h, keys, at, g, e, dp, delta, first, last):
        q, k = ref[0, h, :, at], ref[1, h, :, 0:keys]
        ds = e * (dp - delta).astype(BF16)
        for n, part in ((0, dot(q, ds, 1, 1)), (1, dot(g, e, 1, 1))):
            acc[i, n, :, 0:keys] = part if first else acc[i, n, :, 0:keys] + part
        ref[0, h, :, at] = (dot(k, ds, 1, 0) * 0.125).astype(BF16)
        if last:
            ref[1, h] = acc[i, 0].astype(BF16)
            ref[2, h] = acc[i, 1].astype(BF16)

    @pl.loop(0, 4)
    def _(two):
        slots = [lax.rem(two, 2) * 2 + i for i in range(2)]
        for i in range(2):
            e_in(two * 2 + i, slots[i]).wait()

        @part("cross_back")
        def _():
            shared = [scaled_grad(cctx, 1, two * 2 + i) for i in range(2)]

            def product(i, j):
                return dot(pay[2, two * 2 + i], shared[i][0][:, 256 * j:256 * j + 256], 0, 0)

            def rest(i, j, dp):
                at = slice(256 * j, 256 * j + 256)
                g, delta = shared[i]
                grad_tile(
                    pay, i, two * 2 + i, T, at, g[:, at], ring[slots[i], :, at], dp, delta[:, at],
                    j == 0, j == 3,
                )

            ahead([(i, j) for i in range(2) for j in range(4)], 1, product, rest)

        @pl.when(two < 2)
        def _():
            for i in range(2):
                e_in(two * 2 + i + 4, slots[i]).start()

        @pl.when(two >= 2)
        def _():
            for slot in slots:
                own_in(slot).start()

        link.during_cross_back(two)

    @part("memory_grad")
    def _():
        for r in range(2):
            out = dot(weight(r, 5), grad_of(pay, 1), 0, 0) + dot(weight(r, 6), grad_of(pay, 2), 0, 0)
            gs[r] = out.T.astype(BF16)

    link.put_output(1)
    link.moment("memory_grad")
    @part("cross_grads")
    def _():
        for r in range(2):
            half = slice(256 * r, 256 * r + 256)
            sg[half] = sg[half] + dot(weight(r, 4), grad_of(pay, 0), 0, 0)
        square_grad(4, grad_of(pay, 0), flow)
        square_grad(5, grad_of(pay, 1), mt)
        square_grad(6, grad_of(pay, 2), mt)

    link.moment("cross_grads")

    @part("inner_norm")
    def _():
        @pl.loop(0, 4)
        def _(tb):
            at = pl.ds(pl.multiple_of(tb * TB, TB), TB)
            inner = norm_back(sg[:, at], xh0[:, at], rstd[0, :, at], 0)
            add_col(6, inner * xt[:, at].astype(F32))
            sg[:, at] = param(6) * inner
            tlow[:, at] = inner.astype(BF16)

        for k in range(9):
            part = jnp.sum(cols[k], axis=1, keepdims=True)
            gcol[:, :, :, :, :, k:k + 1] = part.reshape(2, 4, 2, 2, 16, 1)

    link.moment("inner_norm")

    @part("self_output_back")
    def _():
        for r in range(2):
            slow[256 * r:256 * r + 256] = dot(weight(r, 3), tlow[...], 0, 0).astype(BF16)

    link.moment("self_output_back")

    @pl.loop(0, 4)
    def _(turn):
        pair = link.pair_back(turn)
        own_in(pair).wait()
        @part("self_back")
        def _():
            shared = [scaled_grad(ctx, 0, pair * 2 + i) for i in range(2)]

            def product(i, j):
                at = slice(256 * j, 256 * j + 256)
                return dot(qkv[2, pair * 2 + i, :, 0:256 * (j + 1)], shared[i][0][:, at], 0, 0)

            def rest(i, j, dp):
                keys, at = 256 * (j + 1), slice(256 * j, 256 * j + 256)
                g, delta = shared[i]
                row, lane = self_tile(i, j)
                e = ring[pair, row:row + keys, lane:lane + 256]
                grad_tile(
                    qkv, i, pair * 2 + i, keys, at, g[:, at], e, dp, delta[:, at], j == 3, j == 0
                )

            ahead([(i, j) for i in range(2) for j in (3, 2, 1, 0)], 1, product, rest)

        link.amid_self_back(turn)

        @pl.when(turn == 0)
        def _():
            @part("self_output_grad")
            def _():
                for r in range(2):
                    right = ctx[...].reshape(D, T)[256 * r:256 * r + 256]
                    part = dot(tlow[...], right, 1, 1).astype(BF16)
                    wdn[r, :, :, :, 96:128, :] = part.reshape(4, 2, 2, 32, 256)

        @part("self_grads")
        def _():
            left = jnp.concatenate([qkv[m, pl.ds(2 * pair, 2)].reshape(128, T) for m in range(3)], axis=0)
            for r in range(2):
                part = dot(left, xt[256 * r:256 * r + 256], 1, 1).astype(BF16)
                for m in range(3):
                    wdn[r, pair, :, :, 32 * m:32 * m + 32, :] = part[128 * m:128 * m + 128].reshape(2, 2, 32, 256)

        link.during_self_back(turn)

    link.free_output(1)
    @part("tokens_grad")
    def _():
        for r in range(2):
            out = sg[256 * r:256 * r + 256]
            for m in range(3):
                out = out + dot(weight(r, m), grad_of(qkv, m), 0, 0)
            gs[r] = out.T.astype(BF16)

    link.moment("tokens_grad")
    link.put_output(2)
    link.finish()


def part(name):
    def run(section):
        with jax.named_scope(name):
            section()

    return run


class Alone:
    def __init__(self, inputs, outputs, weights, grads, buffers, sem):
        self.inputs, self.outputs, self.weights, self.grads = inputs, outputs, weights, grads
        self.xs, self.cs, self.gs, self.w8, self.wup, self.wdn = buffers
        self.sem = sem
        copy = pltpu.make_async_copy
        self.loads = [
            copy(inputs[0], self.xs.at[0], sem.at[0]),
            copy(inputs[1], self.xs.at[1], sem.at[1]),
            copy(inputs[2], self.cs, sem.at[2]),
            copy(self.squares(weights), self.w8, sem.at[3]),
            copy(weights.at[:, :, :, :, pl.ds(256, 128), :], self.wup, sem.at[4]),
            copy(weights.at[:, :, :, :, pl.ds(384, 128), :], self.wdn, sem.at[5]),
        ]
        self.stores = [
            copy(self.xs.at[0], outputs[0], sem.at[6]),
            copy(self.gs, outputs[1], sem.at[7]),
            copy(self.gs, outputs[2], sem.at[7]),
        ]

    def squares(self, ref):
        return ref.at[:, :, :, :, pl.ds(0, 256), :]

    def begin(self):
        for load in self.loads:
            load.start()

    def line(self, ref):
        return ref[0:1, :]

    def wait_input(self, i):
        self.loads[i].wait()

    def wait_weights(self, group):
        if group == 4:
            self.loads[4].wait()
        if group == 5:
            self.loads[5].wait()

    def gathered(self):
        pass

    def moment(self, name):
        down = pltpu.make_async_copy(
            self.wdn, self.grads.at[:, :, :, :, pl.ds(384, 128), :], self.sem.at[2]
        )
        if name == "mask":
            self.loads[3].wait()
        if name == "feed_down_back":
            down.start()
        if name == "self_output_back":
            down.wait()

    def put_output(self, i):
        self.stores[i].start()

    def free_output(self, i):
        self.stores[i].wait()

    def pair_of(self, turn):
        return turn

    def before_self(self, turn):
        pass

    def amid_self(self, turn):
        pass

    def during_self(self, turn):
        pass

    def during_cross(self, h):
        pass

    def during_cross_back(self, h):
        pass

    def pair_back(self, turn):
        return turn

    def amid_self_back(self, turn):
        pass

    def during_self_back(self, turn):
        pass

    def finish(self):
        def grads(first, count):
            return self.grads.at[:, :, :, :, pl.ds(first, count), :]

        copies = [
            pltpu.make_async_copy(self.wdn, grads(0, 128), self.sem.at[0]),
            pltpu.make_async_copy(self.wup, grads(256, 128), self.sem.at[1]),
            pltpu.make_async_copy(
                self.w8.at[:, :, :, :, pl.ds(128, 128), :], grads(128, 128), self.sem.at[2]
            ),
        ]
        for copy in copies:
            copy.start()
        for copy in copies:
            copy.wait()
        self.stores[0].wait()
        self.stores[2].wait()


class Linked:
    def __init__(self, inputs, shards, params, outputs, gout, cout, buffers, landing, sems):
        self.inputs, self.shards, self.params = inputs, shards, params
        self.outputs, self.gout, self.cout = outputs, gout, cout
        self.xs, self.cs, self.gs, self.w8, self.wup, self.wdn, self.par, self.gcol = buffers
        self.land0, self.land1, self.land2, self.land3, self.plane_land, self.line_land = landing[:6]
        self.small = landing[6:]
        (self.isem, self.lsem, self.gsend, self.grecv, self.osem,
         self.rsend, self.rrecv, self.psend, self.precv) = sems
        r = lax.axis_index("row")
        col = lax.axis_index("col")
        z, y, x = col // 4, lax.rem(col // 2, 2), lax.rem(col, 2)
        self.r, self.z, self.y, self.x = r, z, y, x
        self.zs = [lax.rem(z + d, 4) for d in range(4)]
        self.partner = (1 - r, col)

        def chip(z, y, x):
            return (r, z * 4 + y * 2 + x)

        self.chip = chip
        self.across = {"x": chip(z, y, 1 - x), "y": chip(z, 1 - y, x)}
        self.along = [chip(self.zs[d], y, x) for d in (1, 2, 3)]
        self.others = [(y, 1 - x), (1 - y, x), (1 - y, 1 - x)]
        self.plane = [chip(z, *other) for other in self.others]
        self.peers = [self.partner, *self.plane, *self.along]
        self.holders = (
            (self.w8, 0, 96), (self.w8, 96, 96), (self.w8, 192, 32), (self.w8, 224, 32),
            (self.wup, 0, 128), (self.wdn, 0, 128),
        )

    def remote(self, source, target, send, recv, device):
        return pltpu.make_async_remote_copy(
            src_ref=source, dst_ref=target, send_sem=send, recv_sem=recv,
            device_id=device, device_id_type=pl.DeviceIdType.MESH,
        )


    def keep_in(self, i):
        place = (self.xs.at[0], self.xs.at[1], self.cs)[i]
        return pltpu.make_async_copy(self.inputs[i].at[self.r], place.at[self.r], self.lsem.at[i])

    def swap_in(self, i):
        place = (self.xs.at[0], self.xs.at[1], self.cs)[i]
        return self.remote(
            self.inputs[i].at[1 - self.r], place.at[self.r],
            self.isem.at[0, i], self.isem.at[1, i], self.partner,
        )

    def swap_par(self):
        place = self.par.at[self.r]
        return self.remote(place, place, self.isem.at[0, 3], self.isem.at[1, 3], self.partner)

    def keep_out(self, i):
        source = (self.xs.at[0], self.gs, self.gs)[i]
        return pltpu.make_async_copy(
            source.at[self.r], self.outputs[i].at[self.r], self.lsem.at[3 + i]
        )

    def swap_out(self, i):
        source = (self.xs.at[0], self.gs, self.gs)[i]
        return self.remote(
            source.at[1 - self.r], self.outputs[i].at[self.r],
            self.osem.at[0, i], self.osem.at[1, i], self.partner,
        )


    def gathers(self, group, step):
        ref, first, count = self.holders[group]
        r, z, y, x = self.r, self.z, self.y, self.x

        def move(place, at, half, device):
            piece = ref.at[place]
            return self.remote(
                piece, piece, self.gsend.at[group, half, at], self.grecv.at[group, half, at], device
            )

        if group < 3:
            rows = pl.ds(first, count)
            back = [z] + [self.zs[4 - d] for d in (1, 2, 3)]
            every = slice(None)
            if step == 0:
                order = (0, 2, 1)
                return [move((r, z, y, x, rows), d, 0, self.along[d]) for d in order] + [
                    move((r, z, y, x, rows), 3 + k, 0, self.plane[k]) for k in range(3)
                ]
            if step < 4:
                return [move((r, back[step], y, x, rows), 3 + 3 * step + k, 0, self.plane[k]) for k in range(3)]
            d = step - 4
            return [move((r, back[d], every, every, rows), 15 + d, 0, self.partner)]
        copies = []
        for half in range(2):
            rows = pl.ds(first + half * (count // 2), count // 2)
            every = slice(None)
            own = (r, z, y, x, rows)
            line = (r, every, y, x, rows)
            sheet = (r, every, every, x, rows) if half == 0 else (r, every, y, every, rows)
            axes = ("y", "x") if half == 0 else ("x", "y")
            if step == 0:
                copies += [move(own, d, half, self.along[d]) for d in range(3)]
            elif step == 3:
                copies.append(move((r, every, every, every, rows), 5, half, self.partner))
            else:
                place = line if step == 1 else sheet
                copies.append(move(place, 2 + step, half, self.across[axes[step - 1]]))
        return copies

    def start(self, group, step):
        for copy in self.gathers(group, step):
            copy.start()

    def start_along(self, group):
        for copy in self.gathers(group, 0)[:3]:
            copy.start()

    def start_plane(self, group):
        for copy in self.gathers(group, 0)[3:]:
            copy.start()

    def wait(self, group, step):
        for copy in self.gathers(group, step):
            copy.wait_recv()

    def gather(self, group, step):
        self.wait(group, step - 1)
        self.start(group, step)

    def forward(self, group, d):
        self.gathers(group, 0)[(0, 2, 1).index(d - 1)].wait_recv()
        self.start(group, d)

    def share(self, group, d):
        if d == 0:
            for copy in self.gathers(group, 0)[3:]:
                copy.wait_recv()
        else:
            self.wait(group, d)
        self.start(group, 4 + d)

    def begin(self):
        r, z, y, x = self.r, self.z, self.y, self.x
        barrier = pltpu.get_barrier_semaphore()
        for peer in self.peers:
            pl.semaphore_signal(barrier, inc=1, device_id=peer, device_id_type=pl.DeviceIdType.MESH)
        for i in range(3):
            self.keep_in(i).start()
        for m in range(8):
            self.w8[r, z, y, x, 32 * m:32 * m + 32, :] = self.shards[SLOTS[m]][...]
        self.wup[r, z, y, x] = self.shards[8][...].T
        for s in range(4):
            self.wdn[r, z, y, x, 32 * s:32 * s + 32, :] = self.shards[9][:, 256 * s:256 * s + 256]
        for k in range(3):
            self.par[r, 3 * k:3 * k + 3, :] = self.params[k][...]
        pl.semaphore_wait(barrier, len(self.peers))
        self.start(0, 0)
        self.swap_in(0).start()
        self.swap_par().start()
        self.swap_in(1).start()
        self.swap_in(2).start()

    def line(self, ref):
        return ref[pl.ds(self.r, 1), :]

    def wait_input(self, i):
        self.keep_in(i).wait()
        self.swap_in(i).wait_recv()
        if i == 1:
            self.swap_par().wait_recv()

    def wait_weights(self, group):
        if group < 3:
            for d in range(4):
                self.wait(group, 4 + d)
        else:
            self.wait(group, 3)

    def gathered(self):
        for group in range(6):
            for step in range(8 if group < 3 else 4):
                for copy in self.gathers(group, step):
                    copy.wait_send()


    def sums(self, group, step):
        r, z, y, x = self.r, self.z, self.y, self.x
        send, recv = self.rsend.at[group], self.rrecv.at[group]
        every = slice(None)
        if group == 3:
            ref = self.gcol
            if step == 0:
                return [self.remote(ref.at[1 - r], self.small[0], send.at[0], recv.at[0], self.partner)]
            if step == 1:
                source = ref.at[r, :, :, 1 - x]
                return [self.remote(source, self.small[1], send.at[1], recv.at[1], self.across["x"])]
            if step == 2:
                source = ref.at[r, :, 1 - y, x]
                return [self.remote(source, self.small[2], send.at[2], recv.at[2], self.across["y"])]
            return [
                self.remote(
                    ref.at[r, self.zs[d + 1], y, x], self.small[3].at[d],
                    send.at[3 + d], recv.at[3 + d], self.along[d],
                )
                for d in range(3)
            ]
        ref, at, count = self.summed(group)
        land0, land1, land2, land3 = self.landing(group)
        if step == 0:
            source = ref.at[1 - r, :, :, :, pl.ds(at, count)]
            return [self.remote(source, land0, send.at[0], recv.at[0], self.partner)]
        copies = []
        for half in range(2):
            rows = pl.ds(at + count // 2 * half, count // 2)
            axes = ("x", "y") if half == 0 else ("y", "x")
            k = 1 + 5 * half
            if step == 1:
                place = (r, every, every, 1 - x, rows) if half == 0 else (r, every, 1 - y, every, rows)
                target, device = land1.at[half], self.across[axes[0]]
                copies.append(self.remote(ref.at[place], target, send.at[k], recv.at[k], device))
            elif step == 2:
                place = (r, every, 1 - y, x, rows) if half == 0 else (r, every, y, 1 - x, rows)
                target, device = land2.at[half], self.across[axes[1]]
                copies.append(self.remote(ref.at[place], target, send.at[k + 1], recv.at[k + 1], device))
            else:
                for d in range(3):
                    copies.append(self.remote(
                        ref.at[r, self.zs[d + 1], y, x, rows], land3.at[half, d],
                        send.at[k + 2 + d], recv.at[k + 2 + d], self.along[d],
                    ))
        return copies

    def summed(self, group):
        return ((self.wdn, 0, 128), (self.wup, 0, 128), (self.w8, 128, 96), None, (self.w8, 224, 32))[group]

    def landing(self, group):
        first, count = {2: (0, 96), 4: (96, 32)}.get(group, (0, 128))
        which = 2 if group == 4 else group
        rows, half = pl.ds(first, count), pl.ds(first // 2, count // 2)
        return (
            self.land0.at[which, :, :, :, rows], self.land1.at[which, :, :, :, half],
            self.land2.at[which, :, :, half], self.land3.at[which, :, :, half],
        )

    def reduce(self, group, step):
        r, z, y, x = self.r, self.z, self.y, self.x
        every = slice(None)
        if step > 0:
            for copy in self.sums(group, step - 1):
                copy.wait_recv()
        if group == 3:
            ref = self.gcol
            if step == 1:
                ref[r] = ref[r] + self.small[0][...]
            elif step == 2:
                ref[r, :, :, x] = ref[r, :, :, x] + self.small[1][...]
            elif step == 3:
                ref[r, :, y, x] = ref[r, :, y, x] + self.small[2][...]
            elif step == 4:
                total = ref[r, z, y, x]
                for d in range(3):
                    total = total + self.small[3][d]
                self.cout[...] = total
        elif step > 0:
            ref, at, count = self.summed(group)
            land0, land1, land2, land3 = self.landing(group)
            middle = count // 2

            def add(place, value):
                ref[place] = (ref[place].astype(F32) + value.astype(F32)).astype(BF16)

            if step == 1:
                for k in range(4):
                    add((r, k, every, every, slice(at, at + count)), land0[k])
            for half in range(2):
                rows = slice(at + middle * half, at + middle * half + middle)
                if step == 2 and half == 0:
                    add((r, every, every, x, rows), land1[half])
                elif step == 2:
                    add((r, every, y, every, rows), land1[half])
                elif step == 3:
                    add((r, every, y, x, rows), land2[half])
                elif step == 4:
                    total = ref[r, z, y, x, rows].astype(F32)
                    for d in range(3):
                        total = total + land3[half, d].astype(F32)
                    first = (96 if group == 4 else 0) + middle * half
                    self.gout[2 if group == 4 else group, first:first + middle] = total
        if step < 4:
            for copy in self.sums(group, step):
                copy.start()
        elif group == 0:
            for step in range(4):
                for copy in self.sums(group, step):
                    copy.wait_send()


    def pair_back(self, turn):
        return lax.rem(self.z + 1 + turn, 4)

    def plane_sums(self, turn, step):
        r, z, y, x = self.r, self.z, self.y, self.x
        ref, p = self.wdn, self.pair_back(turn)
        send, recv = self.psend.at[turn], self.precv.at[turn]
        if step == 0:
            return [self.remote(ref.at[1 - r, p], self.land0.at[3, turn], send.at[0], recv.at[0], self.partner)]
        if step == 1:
            return [
                self.remote(
                    ref.at[r, p, to_y, to_x], self.plane_land.at[turn, k],
                    send.at[1 + k], recv.at[1 + k], self.plane[k],
                )
                for k, (to_y, to_x) in enumerate(self.others)
            ]
        return [self.remote(
            ref.at[r, p, y, x], self.line_land.at[turn], send.at[4], recv.at[4], self.chip(p, y, x)
        )]

    def reduce_plane(self, turn, step):
        r, z, y, x = self.r, self.z, self.y, self.x
        ref, p = self.wdn, self.pair_back(turn)
        if step > 0:
            for copy in self.plane_sums(turn, step - 1):
                copy.wait_recv()
        if step == 1:
            for k in range(2):
                total = ref[r, p, k].astype(F32) + self.land0[3, turn, k].astype(F32)
                ref[r, p, k] = total.astype(BF16)
        if step == 2:
            total = ref[r, p, y, x].astype(F32)
            for k in range(3):
                total = total + self.plane_land[turn, k].astype(F32)
            ref[r, p, y, x] = total.astype(BF16)
        for copy in self.plane_sums(turn, step):
            copy.start()

    def end_planes(self):
        for copy in self.plane_sums(3, 1):
            copy.wait_recv()
        total = self.wdn[self.r, self.z, self.y, self.x].astype(F32)
        for k in range(3):
            total = total + self.plane_land[3, k].astype(F32)
        for turn in range(3):
            for copy in self.plane_sums(turn, 2):
                copy.wait_recv()
            total = total + self.line_land[turn].astype(F32)
        self.gout[3] = total
        for turn in range(4):
            for step in range(3 if turn < 3 else 2):
                for copy in self.plane_sums(turn, step):
                    copy.wait_send()


    def moment(self, name):
        if name == "turn_tokens":
            self.forward(0, 1)
            self.start_along(1)
            self.share(0, 0)
        elif name == "turn_memory":
            self.forward(0, 3)
            self.forward(0, 2)
            self.start_plane(1)
        elif name == "memory_projections":
            self.gather(3, 1)
        elif name == "first_norm":
            for d in (0, 1, 3, 2):
                self.share(2, d)
            self.gather(5, 1)
        elif name == "probes":
            self.gather(3, 2)
        elif name == "half_feed_up":
            self.gather(5, 3)
        elif name == "feed_down_back":
            self.reduce(0, 0)
        elif name == "feed_up_grad":
            self.reduce(0, 1)
            self.reduce(1, 0)
        elif name == "cross_output_back":
            self.reduce(1, 1)
            self.reduce(4, 0)
        elif name == "memory_grad":
            self.reduce(0, 3)
        elif name == "cross_grads":
            self.reduce(2, 0)
            self.reduce(4, 2)
        elif name == "inner_norm":
            self.reduce(3, 0)
            self.reduce(2, 1)
            self.reduce(1, 3)
        elif name == "tokens_grad":
            self.reduce_plane(2, 2)

    def at_turn(self, index, turns):
        for turn, actions in turns.items():

            @pl.when(index == turn)
            def _():
                for move, *where in actions:
                    move(*where)

    def pair_of(self, turn):
        back = turn + turn // 2 * (1 - 2 * lax.rem(turn, 2))
        return lax.rem(self.z - back + 4, 4)

    def before_self(self, turn):
        self.at_turn(turn, {n: [(self.wait, 0, 4 + d)] for n, d in enumerate((0, 1, 3, 2))})

    def amid_self(self, turn):
        self.at_turn(turn, {
            0: [(self.share, 0, 1)],
            1: [(self.share, 0, 3), (self.forward, 1, 1)],
            2: [(self.share, 0, 2), (self.forward, 1, 2), (self.start_plane, 2)],
            3: [(self.share, 1, 0), (self.share, 1, 1)],
        })

    def during_self(self, turn):
        self.at_turn(turn, {
            0: [(self.start_along, 2), (self.start, 4, 0)],
            1: [(self.forward, 1, 3), (self.start, 3, 0)],
            2: [(self.forward, 2, 1), (self.forward, 2, 3), (self.forward, 2, 2), (self.start, 5, 0)],
            3: [(self.share, 1, 3), (self.share, 1, 2), (self.gather, 4, 1)],
        })

    def during_cross(self, two):
        self.at_turn(two, {
            0: [(self.gather, 4, 2)],
            1: [(self.gather, 5, 2), (self.gather, 3, 3)],
            3: [(self.gather, 4, 3)],
        })

    def during_cross_back(self, two):
        self.at_turn(two, {
            0: [(self.reduce, 4, 1)],
            1: [(self.reduce, 0, 2)],
            3: [(self.reduce, 1, 2)],
        })

    def amid_self_back(self, turn):
        @pl.when(turn == 0)
        def _():
            self.reduce(0, 4)

        @pl.when(turn >= 1)
        def _():
            self.reduce_plane(turn - 1, 1)

        @pl.when(turn == 3)
        def _():
            self.reduce(2, 3)
            self.reduce_plane(0, 2)

    def during_self_back(self, turn):
        self.reduce_plane(turn, 0)
        self.at_turn(turn, {
            0: [(self.reduce, 3, 1), (self.reduce, 4, 3)],
            1: [(self.reduce, 2, 2)],
            2: [(self.reduce, 1, 4), (self.reduce, 3, 2), (self.reduce, 4, 4)],
            3: [],
        })

    def put_output(self, i):
        self.keep_out(i).start()
        self.swap_out(i).start()

    def free_output(self, i):
        self.reduce_plane(3, 1)
        self.reduce_plane(1, 2)
        self.reduce(3, 3)
        self.keep_out(i).wait()
        self.swap_out(i).wait_send()

    def finish(self):
        self.reduce(3, 4)
        self.reduce(2, 4)
        self.end_planes()
        for group in range(1, 5):
            for step in range(4):
                for copy in self.sums(group, step):
                    copy.wait_send()
        for i in range(3):
            self.swap_in(i).wait_send()
        self.swap_par().wait_send()
        for i in (0, 2):
            self.keep_out(i).wait()
            self.swap_out(i).wait_send()
        for i in range(3):
            self.swap_out(i).wait_recv()


CHIPS = 16


def to_sixteen(w):
    n = w.shape[1]
    if n == CHIPS:
        return w
    part = D // n

    def spread(block):
        block = block.reshape(2, n, -1, part, 256).swapaxes(1, 2).reshape(2, -1, CHIPS, 32, 256)
        return block.swapaxes(1, 2).reshape(2, CHIPS, -1, 256)

    return jnp.concatenate(
        [
            spread(w[:, :, :8 * part]),
            w[:, :, 8 * part:12 * part].reshape(2, CHIPS, 128, 256),
            spread(w[:, :, 12 * part:]),
        ],
        axis=2,
    )


def from_sixteen(g, n):
    if n == CHIPS:
        return g
    part = D // n

    def gather(block):
        block = block.reshape(2, CHIPS, -1, 32, 256).swapaxes(1, 2).reshape(2, -1, n, part, 256)
        return block.swapaxes(1, 2).reshape(2, n, -1, 256)

    return jnp.concatenate(
        [
            gather(g[:, :, :256]),
            g[:, :, 256:384].reshape(2, n, 4 * part, 256),
            gather(g[:, :, 384:]),
        ],
        axis=2,
    )


ANY = pl.BlockSpec(memory_space=pl.ANY)
VMEM = pl.BlockSpec(memory_space=pltpu.VMEM)
SHAPE = jax.ShapeDtypeStruct
STASH = [SHAPE((H, T, T), BF16), SHAPE((4, T, 1280), BF16)]


def layer_scratch():
    V = pltpu.VMEM
    return [
        V((2, 2, T, 256), BF16), V((2, T, 256), BF16),
        V((D, T), BF16), V((D, T), BF16),
        V((2, 4, 2, 2, 256, 256), BF16),
        V((2, 4, 2, 2, 128, 256), BF16), V((2, 4, 2, 2, 128, 256), BF16),
        V((3, H, HD, T), BF16), V((3, H, HD, T), BF16),
        V((H, HD, T), BF16), V((H, HD, T), BF16),
        V((2, H, 1, T), F32),
        V((D, T), F32), V((D, T), F32), V((2, 1, T), F32),
        V((D, T), BF16), V((D, T), BF16), V((D, T), BF16),
        V((4, T, 1280), BF16),
        V((D, T), F32), V((2, T, 256), BF16),
        V((D, 128), F32), V((9, D, 128), F32),
        V((2, 2, HD, T), F32),
        pltpu.SemaphoreType.DMA((4,)),
    ]


def run_alone(x, mem, cot, w, par, seg, pad):
    def kernel(x, mem, cot, w, par, seg, pad, lo, mg, tg, g, e, es, gcol, *rest):
        scratch, sem = rest[:-1], rest[-1]
        xs, cs, gs = scratch[0], scratch[1], scratch[20]
        link = Alone(
            (x, mem, cot), (lo, mg, tg), w, g, (xs, cs, gs, scratch[4], scratch[5], scratch[6]), sem
        )
        layer(link, e, es, par, seg, pad, *scratch[:-1], gcol, scratch[-1])

    wide = SHAPE((2, T, 256), BF16)
    return pl.pallas_call(
        kernel,
        in_specs=[ANY] * 4 + [VMEM] * 3,
        out_specs=[ANY] * 6 + [VMEM],
        out_shape=[wide] * 3
        + [SHAPE((2, 4, 2, 2, 512, 256), BF16), *STASH, SHAPE((2, 4, 2, 2, 16, 128), F32)],
        scratch_shapes=layer_scratch() + [pltpu.SemaphoreType.DMA((8,))],
        compiler_params=pltpu.CompilerParams(vmem_limit_bytes=63 * 2**20),
        name="layer",
    )(x, mem, cot, w, par, seg, pad)


def run_linked(inputs, shards, params, seg, pad):
    def kernel(*refs):
        inputs, shards, params, seg, pad = refs[0:3], refs[3:13], refs[13:16], refs[16], refs[17]
        outputs, e, es, gout, cout = refs[18:21], refs[21], refs[22], refs[23], refs[24]
        scratch = refs[25:25 + 25]
        par, gcol = refs[50], refs[51]
        landing, sems = refs[52:62], refs[62:]
        xs, cs, gs = scratch[0], scratch[1], scratch[20]
        link = Linked(
            inputs, shards, params, outputs, gout, cout,
            (xs, cs, gs, scratch[4], scratch[5], scratch[6], par, gcol), landing, sems,
        )
        layer(link, e, es, par, seg, pad, *scratch[:-1], gcol, scratch[-1])

    V = pltpu.VMEM
    DMA = pltpu.SemaphoreType.DMA
    wide = SHAPE((2, T, 256), BF16)
    return pl.pallas_call(
        kernel,
        in_specs=[ANY] * 3 + [VMEM] * 15,
        out_specs=[ANY] * 5 + [VMEM] * 2,
        out_shape=[wide] * 3 + STASH + [SHAPE((4, 128, 256), F32), SHAPE((16, 128), F32)],
        scratch_shapes=layer_scratch() + [
            V((2, 16, 256), F32), V((2, 4, 2, 2, 16, 128), F32),
            V((4, 4, 2, 2, 128, 256), BF16), V((3, 2, 4, 2, 64, 256), BF16),
            V((3, 2, 4, 64, 256), BF16), V((3, 2, 3, 64, 256), BF16),
            V((4, 3, 128, 256), BF16), V((3, 128, 256), BF16),
            V((4, 2, 2, 16, 128), F32), V((4, 2, 16, 128), F32),
            V((4, 16, 128), F32), V((3, 16, 128), F32),
            DMA((2, 4)), DMA((6,)), DMA((6, 2, 19)), DMA((6, 2, 19)), DMA((2, 3)),
            DMA((5, 11)), DMA((5, 11)), DMA((5, 5)), DMA((5, 5)),
        ],
        compiler_params=pltpu.CompilerParams(
            vmem_limit_bytes=63 * 2**20, collective_id=0, has_side_effects=True
        ),
        name="layer",
    )(*inputs, *shards, *params, seg, pad)


def ending(lo, mg, tg, gout, cout):
    def kernel(lo, mg, tg, gout, cout, lo_out, tg_out, mg_out, *rest):
        lo_out[...] = lo[...]
        mg_out[...] = mg[...].astype(F32)
        tg_out[...] = tg[...].astype(F32)

        @pl.when(pl.program_id(0) == 0)
        def _():
            for m in range(8):
                at = 32 * (SLOTS.index(m) % 4)
                rest[m][...] = gout[3 if m < 4 else 2, at:at + 32, :]
            rest[8][...] = gout[1].T
            for s in range(4):
                rest[9][:, 256 * s:256 * s + 256] = gout[0, 32 * s:32 * s + 32, :]
            small = cout[...].T
            for k in range(3):
                rest[10 + k][...] = small[3 * k:3 * k + 3, :]

    part = pl.BlockSpec((1, 512, 256), lambda i: (i // 2, i % 2, 0))

    def whole(*shape):
        return pl.BlockSpec(shape, lambda i: (0,) * len(shape))

    shapes = [(32, 256)] * 8 + [(256, 128), (32, 1024)] + [(3, 16)] * 3
    return pl.pallas_call(
        kernel,
        grid=(4,),
        in_specs=[part] * 3 + [whole(4, 128, 256), whole(16, 128)],
        out_specs=[part] * 3 + [whole(*one) for one in shapes],
        out_shape=[SHAPE((2, T, 256), BF16), SHAPE((2, T, 256), F32), SHAPE((2, T, 256), F32)]
        + [SHAPE(one, F32) for one in shapes],
        name="ending",
    )(lo, mg, tg, gout, cout)


def body(
    tokens, memory, cotangent, segments, padding,
    self_query, self_key, self_value, self_output,
    cross_query, cross_key, cross_value, cross_output,
    feed_up, feed_down, norm_gain, norm_bias, omegas,
):
    n = lax.axis_size("col")
    squares = (
        self_query, self_key, self_value, self_output,
        cross_query, cross_key, cross_value, cross_output,
    )
    if n == CHIPS:
        lo, mg, tg, _, _, gout, cout = run_linked(
            (tokens, memory, cotangent), (*[m.T for m in squares], feed_up, feed_down.T),
            (norm_gain, norm_bias, omegas), segments, padding,
        )
        out = ending(lo, mg, tg, gout, cout)
        turned = [one.T for one in out[3:11]]
        return (*out[0:3], *turned, out[11], out[12].T, *out[13:16])
    row = lax.axis_index("row")
    part = D // n
    blob = jnp.concatenate(
        [squares[m].T for m in SLOTS]
        + [feed_up.T]
        + [feed_down.T[:, 256 * s:256 * s + 256] for s in range(4)],
        axis=0,
    )
    w = lax.all_gather(blob, ("row", "col"), axis=0, tiled=False).reshape(2, n, 16 * part, 256)
    w = to_sixteen(w).reshape(2, 4, 2, 2, 512, 256)
    par = jnp.concatenate([norm_gain, norm_bias, omegas, jnp.zeros((7, 256), F32)], axis=0)
    par = lax.all_gather(par, "row", axis=0, tiled=False)

    def mine(array):
        return lax.all_to_all(array, "row", split_axis=0, concat_axis=0, tiled=True)

    seg = lax.dynamic_slice_in_dim(segments, row, 1, 0)
    pad = lax.dynamic_slice_in_dim(padding, row, 1, 0)
    lo, mg, tg, g, _, _, gcol = run_alone(
        mine(tokens), mine(memory), mine(cotangent), w, par, seg, pad
    )
    lo, tg, mg = mine(lo), mine(tg).astype(F32), mine(mg).astype(F32)
    g = from_sixteen(g.reshape(2, CHIPS, 512, 256), n).reshape(2 * n, 16 * part, 256)
    g = lax.psum_scatter(g.astype(F32), ("row", "col"), scatter_dimension=0, tiled=False)
    gcol = lax.psum_scatter(
        gcol.reshape(2 * n, part // 2, 128), ("row", "col"), scatter_dimension=0, tiled=False
    )
    small = gcol[:, 0:9].T
    last = 12 * part
    return (
        lo, tg, mg,
        *[g[part * i:part * i + part].T for i in (SLOTS.index(m) for m in range(8))],
        g[8 * part:last].T,
        jnp.concatenate([g[last + part * s:last + part * s + part].T for s in range(4)], axis=0),
        small[0:3], small[3:6], small[6:9],
    )


def solution(mesh):
    wide = P(None, "col", "row")
    square = P("row", "col")
    return jax.shard_map(
        body,
        mesh=mesh,
        in_specs=(wide,) * 3 + (P(None, "col"),) * 2 + (square,) * 10 + (P(None, "row"),) * 3,
        out_specs=(wide,) * 3 + (square,) * 10 + (P(None, ("row", "col")),) * 3,
        check_vma=False,
    )
```
